128 devices in a mesh: expert: 64 (over y, x, z), seq: 2 (over core).
Axes of the slice: x: 4, y: 4, z: 4, core: 2. Of those that a mesh axis runs over, the one named last changes fastest.
Arguments:
- out_grad: bfloat16 [16384, 7168], P(('expert', 'seq')), may hold values from -6 to 6
- route_ids: int32 [16384, 8], P('expert'), may hold values from 0 to 255, all different within a row
- route_weights: float32 [16384, 8], P('expert'), may hold values from 0.2 to 1
- gate_pre: bfloat16 [64, 768, 1024], P('expert', None, 'seq'), may hold values from -5 to 5
- up_pre: bfloat16 [64, 768, 1024], P('expert', None, 'seq'), may hold values from -5 to 5
- w_gate: bfloat16 [64, 7168, 1024], P('expert', None, 'seq'), may hold values from -0.75 to 0.75
- w_up: bfloat16 [64, 7168, 1024], P('expert', None, 'seq'), may hold values from -0.75 to 0.75
- w_down: bfloat16 [64, 1024, 7168], P('expert', 'seq'), may hold values from -0.0078125 to 0.0078125
Outputs:
- in_grad: bfloat16 [16384, 7168], P(('expert', 'seq'))
- weight_grad: bfloat16 [16384, 8], P(('expert', 'seq'))
The draws below stay inside these ranges and needn't reach their ends.
Inputs may be any that keep to these rules, and one draw needn't show every extreme that they name: `route_ids`: each row names 8 different experts; only experts below 64 are held in this window, the others are left to other windows.
All inputs are finite; a program needn't handle non-finite values.
Results may differ from the reference program's by a relative error of at most 0.0065.
Values may be sent and summed in bfloat16 or wider, within the bound.
No kernel may reach another device: no remote copies, remote signals or barrier semaphores. Data moves between devices by JAX's collectives and lax.ppermute only.
A program may use at most 192 MiB of HBM per device.

```python
import jax
import jax.numpy as jnp
from jax import lax

D = 7168
ROUTED = 256
TOPK = 8
FF = 1024
TOK_DEV = 128
EXPERTS = 64
TOKENS = 16384
CAP = 12
SLOTS = 768
N_EXPERT = 64
N_SEQ = 2


def block_scale(rng, shape, split, low, top_value):
    def one(dim, shards_of):
        steps = jax.random.uniform(jax.random.fold_in(jax.random.fold_in(rng, 6), dim), (shards_of,), jnp.float32, low / len(split), top_value / len(split))
        return jnp.repeat(jnp.exp(steps), shape[dim] // shards_of).reshape((-1,) + (1,) * (len(shape) - dim - 1))

    factor_of = one(*split[0])
    for cut in split[1:]:
        factor_of = factor_of * one(*cut)
    return factor_of


def choose_distinct(rng, rows, amount, top, lift):
    order = jax.random.permutation(jax.random.fold_in(rng, 1), amount)
    pull = order
    for power in range(3):
        pull = pull * pull // amount
    pull = pull * lift // amount
    lots = jax.random.randint(jax.random.fold_in(rng, 2), (rows, amount), 0, 4096) + pull
    sure = jax.random.permutation(jax.random.fold_in(rng, 3), rows)[jnp.arange(amount) % rows]
    lots = jnp.where(jnp.arange(rows)[:, None] == sure[None, :], 1 << 14, lots)
    priority = lots * amount + jnp.arange(amount)
    return lax.top_k(priority.astype(jnp.int32), top)[1].astype(jnp.int32)


def centred(key, dims, spread, reach, shards=(), kind=jnp.bfloat16):
    result = jax.random.normal(key, dims, jnp.float32) * spread
    if len(shards) > 0:
        result = block_scale(key, dims, shards, -0.22, 0.18) * result
    return jnp.clip(result, min=-reach, max=reach).astype(kind)


def setup_inputs(seed: int = 0) -> dict:
    splits = jax.random.split(jax.random.key(seed), 9)
    return {
        "out_grad": centred(splits[0], (TOKENS, D), 1.0, 6.0, ((0, 128),)),
        "route_ids": choose_distinct(splits[1], TOKENS, ROUTED, TOPK, 512),
        "route_weights": jnp.clip(0.2 + 0.8 * jax.random.uniform(splits[2], (TOKENS, TOPK), jnp.float32) ** block_scale(splits[2], (TOKENS, TOPK), ((0, 64),), -0.2, 0.2), 0.2, 1.0),
        "gate_pre": centred(splits[3], (EXPERTS, SLOTS, FF), 1.0, 5.0, ((0, 64), (2, 2))),
        "up_pre": centred(splits[4], (EXPERTS, SLOTS, FF), 1.0, 5.0, ((0, 64), (2, 2))),
        "w_gate": centred(splits[5], (EXPERTS, D, FF), (FF // 16) ** -0.5, 0.75, ((0, 64), (2, 2))),
        "w_up": centred(splits[6], (EXPERTS, D, FF), (FF // 16) ** -0.5, 0.75, ((0, 64), (2, 2))),
        "w_down": centred(splits[7], (EXPERTS, FF, D), (D * 64) ** -0.5, 0.0078125, ((0, 64), (1, 2))),
    }


def silu_parts(value):
    sigma = jax.nn.sigmoid(value)
    return value * sigma, sigma * (1.0 + value * (1.0 - sigma))


def pair_tables(group_ids):
    pair_count = group_ids.shape[0]
    fanout = group_ids.shape[1]
    assigned = group_ids.reshape(-1).astype(jnp.int32)
    one_hot = (assigned[:, None] == jnp.arange(EXPERTS, dtype=jnp.int32)[None, :]).astype(jnp.int32)
    earlier = jnp.cumsum(one_hot, axis=0) - one_hot
    position = jnp.sum(earlier * one_hot, axis=1).astype(jnp.int32)
    retained = (assigned < EXPERTS) & (position < CAP)
    slot_index = jnp.where(retained, assigned * CAP + position, EXPERTS * CAP).astype(jnp.int32)
    owner_row = (jnp.arange(assigned.shape[0], dtype=jnp.int32) // fanout).astype(jnp.int32)
    slot_rows = jnp.full((EXPERTS * CAP + 1,), pair_count, jnp.int32).at[slot_index].set(owner_row)
    return slot_index.reshape(pair_count, fanout), slot_rows[:EXPERTS * CAP].reshape(EXPERTS, CAP)


def reference(out_grad, route_ids, route_weights, gate_pre, up_pre, w_gate, w_up, w_down):
    pair_count = TOK_DEV * N_SEQ
    half_width = FF // N_SEQ
    grouped = route_ids.reshape(N_EXPERT, pair_count, TOPK)
    slot_index, slot_rows = jax.vmap(pair_tables)(grouped)
    offsets = (jnp.arange(N_EXPERT, dtype=jnp.int32) * pair_count)[:, None, None]
    global_rows = jnp.where(slot_rows == pair_count, TOKENS, slot_rows + offsets).astype(jnp.int32)
    expert_rows = jnp.transpose(global_rows, (1, 0, 2)).reshape(EXPERTS, SLOTS)
    padded_grad = jnp.concatenate([out_grad, jnp.zeros((1, D), jnp.bfloat16)], axis=0)

    def expert_work(inputs):
        rows, gate_val, up_val, gate_w, up_w, down_w = inputs
        slot_grad = padded_grad[rows]
        input_sum = jnp.zeros((SLOTS, D), jnp.float32)
        score_sum = jnp.zeros((SLOTS,), jnp.float32)
        for half_at in range(N_SEQ):
            lower = half_at * half_width
            upper = lower + half_width
            hidden_grad = jnp.dot(slot_grad, down_w[lower:upper].T, preferred_element_type=jnp.float32)
            active, slope_val = silu_parts(gate_val[:, lower:upper].astype(jnp.float32))
            up_part = up_val[:, lower:upper].astype(jnp.float32)
            score_part = jnp.sum(hidden_grad * active * up_part, axis=1)
            gate_diff = (hidden_grad * up_part * slope_val).astype(jnp.bfloat16)
            up_diff = (hidden_grad * active).astype(jnp.bfloat16)
            input_part = jnp.dot(gate_diff, gate_w[:, lower:upper].T, preferred_element_type=jnp.float32)
            input_part = input_part + jnp.dot(up_diff, up_w[:, lower:upper].T, preferred_element_type=jnp.float32)
            input_round = lax.optimization_barrier(input_part.astype(jnp.bfloat16))
            score_round = lax.optimization_barrier(score_part.astype(jnp.bfloat16))
            input_sum = input_sum + input_round.astype(jnp.float32)
            score_sum = score_sum + score_round.astype(jnp.float32)
        return input_sum.astype(jnp.bfloat16), score_sum.astype(jnp.bfloat16)

    slot_input, slot_score = lax.map(expert_work, (expert_rows, gate_pre, up_pre, w_gate, w_up, w_down))
    expert_of = slot_index // CAP
    place = slot_index % CAP
    group_of = jnp.arange(N_EXPERT, dtype=jnp.int32)[:, None, None]
    global_slot = jnp.where(slot_index == EXPERTS * CAP, EXPERTS * SLOTS, expert_of * SLOTS + group_of * CAP + place)
    global_slot = global_slot.astype(jnp.int32).reshape(TOKENS, TOPK)
    flat_input = jnp.concatenate([slot_input.reshape(EXPERTS * SLOTS, D), jnp.zeros((1, D), jnp.bfloat16)], axis=0)
    flat_score = jnp.concatenate([slot_score.reshape(EXPERTS * SLOTS), jnp.zeros((1,), jnp.bfloat16)], axis=0)
    in_grad = jnp.zeros((TOKENS, D), jnp.float32)
    for column in range(TOPK):
        in_grad = in_grad + route_weights[:, column:column + 1] * flat_input[global_slot[:, column]].astype(jnp.float32)
    return in_grad.astype(jnp.bfloat16), flat_score[global_slot]
```

```python
import jax
import jax.numpy as jnp
from jax import lax
from jax.experimental import pallas as pl
from jax.experimental.pallas import tpu as pltpu
from jax.sharding import PartitionSpec as P

F32 = jnp.float32
BF16 = jnp.bfloat16
NT = (((1,), (1,)), ((), ()))
MAIN = 8
REST = 4
LIMIT = 40 * 1024 * 1024


def iota(shape, dim):
    return lax.broadcasted_iota(jnp.int32, shape, dim)


def flag(cond):
    return jnp.where(cond, 1.0, 0.0).astype(F32)


def dot(a, b):
    return jnp.dot(a, b, preferred_element_type=F32)


def params():
    return pltpu.CompilerParams(vmem_limit_bytes=LIMIT)


def swap(value):
    return lax.ppermute(value, "seq", [(0, 1), (1, 0)])


def dispatch_kernel(at_ref, ids_ref, own_ref, other_ref, out_ref, g_ref, pa_ref, pb_ref):
    step = pl.program_id(0)
    experts = out_ref.shape[0] // MAIN
    tokens = g_ref.shape[0]
    half = tokens // 2
    rows = experts * MAIN
    tile = out_ref.shape[1]
    quarter = g_ref.shape[1] // 2

    @pl.when(step == 0)
    def _():
        at = at_ref[0]
        g_ref[pl.ds(pl.multiple_of(at * half, half), half), :] = own_ref[...]
        g_ref[pl.ds(pl.multiple_of((1 - at) * half, half), half), :] = other_ref[...]
        names = iota((experts, tokens), 0)
        member = jnp.zeros((experts, tokens), F32)
        for k in range(ids_ref.shape[0]):
            member = member + flag(names == ids_ref[k : k + 1, :])
        before = flag(iota((tokens, tokens), 0) < iota((tokens, tokens), 1)).astype(BF16)
        place = dot(member.astype(BF16), before)
        place = jnp.where(member > 0.5, place, -1.0).astype(BF16)
        spread = flag(iota((rows, experts), 0) // MAIN == iota((rows, experts), 1)).astype(BF16)
        wide = dot(spread, place).astype(jnp.int32)
        row = iota((rows, tokens), 0)
        pa_ref[...] = flag(wide == row % MAIN).astype(BF16)
        rest = flag(wide == MAIN + row % REST)
        upper = (row // REST) % 2
        pb_ref[:, :tokens] = jnp.where(upper == 0, rest, 0.0).astype(BF16)
        pb_ref[:, tokens:] = jnp.where(upper == 1, rest, 0.0).astype(BF16)

    steps_a = g_ref.shape[1] // tile

    @pl.when(step < steps_a)
    def _():
        cols = pl.ds(pl.multiple_of(step * tile, 128), tile)
        out_ref[...] = dot(pa_ref[...], g_ref[:, cols]).astype(BF16)

    @pl.when(step >= steps_a)
    def _():
        low = (step - steps_a) * tile
        first = g_ref[:, pl.ds(pl.multiple_of(low, 128), tile)]
        second = g_ref[:, pl.ds(pl.multiple_of(low + quarter, 128), tile)]
        out_ref[...] = (
            dot(pb_ref[:, :tokens], first) + dot(pb_ref[:, tokens:], second)
        ).astype(BF16)


def dispatch(at, ids_t, out_grad, other, experts):
    local, width = out_grad.shape
    part = width // 2
    tile = part // 4
    rows = experts * MAIN
    return pl.pallas_call(
        dispatch_kernel,
        grid_spec=pltpu.PrefetchScalarGridSpec(
            num_scalar_prefetch=1,
            grid=(6,),
            in_specs=[
                pl.BlockSpec(ids_t.shape, lambda j, at: (0, 0)),
                pl.BlockSpec((local, part), lambda j, at: (0, at[0])),
                pl.BlockSpec((local, part), lambda j, at: (0, 0)),
            ],
            out_specs=pl.BlockSpec((rows, tile), lambda j, at: (0, j)),
            scratch_shapes=[
                pltpu.VMEM((2 * local, part), BF16),
                pltpu.VMEM((rows, 2 * local), BF16),
                pltpu.VMEM((rows, 4 * local), BF16),
            ],
        ),
        out_shape=jax.ShapeDtypeStruct((rows, 6 * tile), BF16),
        compiler_params=params(),
        cost_estimate=pl.CostEstimate(flops=2 * 10**9, bytes_accessed=8 * 10**6, transcendentals=0),
        name="dispatch",
    )(at, ids_t, out_grad, other)


def hidden_kernel(at_ref, x_ref, w_ref, out_ref):
    step = pl.program_id(0)
    tile = x_ref.shape[0]
    part = w_ref.shape[1]
    quarter = part // 2
    units = w_ref.shape[0]
    main = lax.dot_general(x_ref[:, :part], w_ref[...], NT, preferred_element_type=F32)
    out_ref[pl.ds(pl.multiple_of(step * tile, tile), tile), :] = main
    rest = x_ref[:, part:]
    low = lax.dot_general(rest, w_ref[:, :quarter], NT, preferred_element_type=F32)
    high = lax.dot_general(rest, w_ref[:, quarter:], NT, preferred_element_type=F32)
    groups = tile // 16
    low = low.reshape(groups, 2, 8, units)
    high = high.reshape(groups, 2, 8, units)
    top = iota((groups, 8, units), 1) < REST
    even = low[:, 0] + pltpu.roll(high[:, 0], REST, 1)
    odd = high[:, 1] + pltpu.roll(low[:, 1], REST, 1)
    base = x_ref.shape[0] * pl.num_programs(0)
    out_ref[pl.ds(pl.multiple_of(base + step * (tile // 2), tile // 2), tile // 2), :] = jnp.where(
        top, even, odd
    ).reshape(tile // 2, units)


def hidden(at, x, w, own):
    rows, lanes = x.shape
    units = w.shape[0]
    part = lanes // 3 * 2
    tile = 128
    return pl.pallas_call(
        hidden_kernel,
        grid_spec=pltpu.PrefetchScalarGridSpec(
            num_scalar_prefetch=1,
            grid=(rows // tile,),
            in_specs=[
                pl.BlockSpec((tile, lanes), lambda i, at: (i, 0)),
                pl.BlockSpec((units, part), (lambda i, at: (0, at[0])) if own else (lambda i, at: (0, 0))),
            ],
            out_specs=pl.BlockSpec((rows // 2 * 3, units), lambda i, at: (0, 0)),
        ),
        out_shape=jax.ShapeDtypeStruct((rows // 2 * 3, units), F32),
        compiler_params=params(),
        cost_estimate=pl.CostEstimate(
            flops=4 * rows * part * units, bytes_accessed=12 * 10**6, transcendentals=0
        ),
        name="hidden_own" if own else "hidden_other",
    )(at, x, w)


def diff_kernel(mine_ref, other_ref, gate_ref, up_ref, out_ref):
    units = mine_ref.shape[1]
    grad = mine_ref[...] + other_ref[...]
    value = gate_ref[...].astype(F32)
    up = up_ref[...].astype(F32)
    sigma = jax.nn.sigmoid(value)
    active = value * sigma
    slope = sigma * (1.0 + value * (1.0 - sigma))
    through = grad * active
    score = jnp.sum(through * up, axis=1, keepdims=True)
    out_ref[:, :units] = (grad * up * slope).astype(BF16)
    out_ref[:, units : 2 * units] = through.astype(BF16)
    out_ref[:, 2 * units :] = jnp.broadcast_to(score, (score.shape[0], 128)).astype(BF16)


def diffs(mine, other, gate, up):
    rows, units = mine.shape
    tile = 256
    spec = pl.BlockSpec((tile, units), lambda i: (i, 0))
    return pl.pallas_call(
        diff_kernel,
        grid=(rows // tile,),
        in_specs=[spec] * 4,
        out_specs=pl.BlockSpec((tile, 2 * units + 128), lambda i: (i, 0)),
        out_shape=jax.ShapeDtypeStruct((rows, 2 * units + 128), BF16),
        compiler_params=params(),
        cost_estimate=pl.CostEstimate(flops=10**7, bytes_accessed=7 * 10**6, transcendentals=rows * units),
        name="diffs",
    )(mine, other, gate, up)


def spread_rows(low, high):
    rows, lanes = low.shape
    pairs = rows // 8
    low = low.reshape(pairs, 8, lanes)
    high = high.reshape(pairs, 8, lanes)
    top = iota((pairs, 8, lanes), 1) < REST
    even = jnp.where(top, low, pltpu.roll(high, REST, 1))
    odd = jnp.where(top, pltpu.roll(low, REST, 1), high)
    return jnp.stack([even, odd], axis=1).reshape(2 * rows, lanes)


def inputs_kernel(at_ref, mine_ref, other_ref, g0, g1, u0, u1, og0, og1, ou0, ou1, out_ref):
    step = pl.program_id(0)
    last = pl.num_programs(0) - 1
    units = g0.shape[1]
    tile = g0.shape[0]
    main = out_ref.shape[0]

    @pl.when(step < last)
    def _():
        def product(g, u, og, ou):
            def one(x, w):
                return lax.dot_general(x, w[...], NT, preferred_element_type=F32)

            total = one(mine_ref[:, :units], g) + one(mine_ref[:, units : 2 * units], u)
            return total + one(other_ref[:, :units], og) + one(other_ref[:, units : 2 * units], ou)

        low = product(g0, u0, og0, ou0)
        high = product(g1, u1, og1, ou1)
        out_ref[:, :tile] = low[:main].astype(BF16)
        out_ref[:, tile : 2 * tile] = high[:main].astype(BF16)
        out_ref[:, 2 * tile :] = spread_rows(low[main:], high[main:]).astype(BF16)

    @pl.when(step == last)
    def _():
        score = mine_ref[:, 2 * units :].astype(F32) + other_ref[:, 2 * units :].astype(F32)
        rest = spread_rows(score[main:], score[main:])
        lane = iota((main, 128), 1)
        out_ref[:, :128] = jnp.where(lane == 0, score[:main], rest).astype(BF16)


def inputs(at, mine, other, w_gate, w_up, gate_other, up_other):
    rows, lanes = mine.shape
    units = w_gate.shape[1]
    part = gate_other.shape[0]
    tile = 256
    steps = part // 2 // tile
    main = rows // 3 * 2

    def own(shift):
        return pl.BlockSpec(
            (tile, units),
            lambda j, at: (at[0] * 2 * steps + shift * steps + jnp.minimum(j, steps - 1), 0),
        )

    def far(shift):
        return pl.BlockSpec(
            (tile, units), lambda j, at: (shift * steps + jnp.minimum(j, steps - 1), 0)
        )

    whole = pl.BlockSpec((rows, lanes), lambda j, at: (0, 0))
    return pl.pallas_call(
        inputs_kernel,
        grid_spec=pltpu.PrefetchScalarGridSpec(
            num_scalar_prefetch=1,
            grid=(steps + 1,),
            in_specs=[whole, whole, own(0), own(1), own(0), own(1), far(0), far(1), far(0), far(1)],
            out_specs=pl.BlockSpec((main, 3 * tile), lambda j, at: (0, j)),
        ),
        out_shape=jax.ShapeDtypeStruct((main, 3 * tile * steps + 128), BF16),
        compiler_params=params(),
        cost_estimate=pl.CostEstimate(
            flops=8 * rows * part * units, bytes_accessed=24 * 10**6, transcendentals=0
        ),
        name="inputs",
    )(at, mine, other, w_gate, w_gate, w_up, w_up, gate_other, gate_other, up_other, up_other)


def combine_kernel(at_ref, ids_ref, weight_ref, back_ref, score_ref, out_ref, grad_ref, w_ref):
    step = pl.program_id(0)
    tokens, topk = ids_ref.shape
    rows = back_ref.shape[0]
    experts = rows // MAIN
    tile = back_ref.shape[1] // 3

    @pl.when(step == 0)
    def _():
        names = iota((tokens, experts), 1)
        ids = ids_ref[...]
        weights = weight_ref[...]
        member = jnp.zeros((tokens, experts), F32)
        gate = jnp.zeros((tokens, experts), F32)
        for k in range(topk):
            hit = names == ids[:, k : k + 1]
            member = member + flag(hit)
            gate = gate + jnp.where(hit, weights[:, k : k + 1], 0.0)
        before = flag(iota((tokens, tokens), 1) < iota((tokens, tokens), 0)).astype(BF16)
        place = dot(before, member.astype(BF16))
        place = jnp.where(member > 0.5, place, -1.0).astype(BF16)
        spread = flag(iota((experts, rows), 1) // MAIN == iota((experts, rows), 0)).astype(BF16)
        wide = dot(place, spread).astype(jnp.int32)
        gate_high = gate.astype(BF16)
        gate_low = (gate - gate_high.astype(F32)).astype(BF16)
        lane = iota((tokens, rows), 1)
        in_main = wide == lane % MAIN
        in_rest = wide == MAIN + lane % REST
        upper = (lane // REST) % 2
        masks = (in_main, in_rest & (upper == 0), in_rest & (upper == 1))
        for at_part, part in enumerate((dot(gate_high, spread), dot(gate_low, spread))):
            for at_mask, mask in enumerate(masks):
                low = (2 * at_mask + at_part) * tokens
                w_ref[low : low + tokens, :] = jnp.where(mask, part, 0.0).astype(BF16)
        block = iota((rows, experts), 0) // MAIN == iota((rows, experts), 1)
        score = score_ref[...].astype(F32)
        main_score = jnp.where(block, score[:, 0:1], 0.0).astype(BF16)
        rest_score = jnp.where(block, score[:, 1:2], 0.0).astype(BF16)
        table = dot(flag(masks[0]).astype(BF16), main_score)
        table = table + dot(flag(masks[1]).astype(BF16), rest_score)
        column = iota((tokens, topk), 1)
        result = jnp.zeros((tokens, topk), F32)
        for k in range(topk):
            hit = names == ids[:, k : k + 1]
            picked = jnp.sum(jnp.where(hit, table, 0.0), axis=1, keepdims=True)
            result = result + jnp.where(column == k, picked, 0.0)
        half = tokens // 2
        grad_ref[...] = jnp.where(at_ref[0] == 0, result[:half], result[half:]).astype(BF16)

    main = dot(w_ref[: 2 * tokens, :], back_ref[:, : 2 * tile])
    rest = dot(w_ref[2 * tokens :, :], back_ref[:, 2 * tile :])
    main = main[:tokens] + main[tokens:]
    out_ref[0] = (main[:, :tile] + (rest[:tokens] + rest[tokens : 2 * tokens])).astype(BF16)
    out_ref[1] = (
        main[:, tile:] + (rest[2 * tokens : 3 * tokens] + rest[3 * tokens :])
    ).astype(BF16)


def combine(at, ids, weights, back):
    tokens, topk = ids.shape
    rows, lanes = back.shape
    tile = 256
    steps = lanes // (3 * tile)
    return pl.pallas_call(
        combine_kernel,
        grid_spec=pltpu.PrefetchScalarGridSpec(
            num_scalar_prefetch=1,
            grid=(steps,),
            in_specs=[
                pl.BlockSpec((tokens, topk), lambda j, at: (0, 0)),
                pl.BlockSpec((tokens, topk), lambda j, at: (0, 0)),
                pl.BlockSpec((rows, 3 * tile), lambda j, at: (0, j)),
                pl.BlockSpec((rows, 128), lambda j, at: (0, 6 * steps)),
            ],
            out_specs=[
                pl.BlockSpec((2, tokens, tile), lambda j, at: (0, 0, j)),
                pl.BlockSpec((tokens // 2, topk), lambda j, at: (0, 0)),
            ],
            scratch_shapes=[pltpu.VMEM((6 * tokens, rows), BF16)],
        ),
        out_shape=[
            jax.ShapeDtypeStruct((2, tokens, steps * tile), BF16),
            jax.ShapeDtypeStruct((tokens // 2, topk), BF16),
        ],
        compiler_params=params(),
        cost_estimate=pl.CostEstimate(flops=4 * 10**9, bytes_accessed=8 * 10**6, transcendentals=0),
        name="combine",
    )(at, ids, weights, back, back)


def by_part(value, groups):
    units = value.shape[1]
    value = value.reshape(groups, MAIN + REST, units)
    first = value[:, :MAIN].reshape(groups * MAIN, units)
    return jnp.concatenate([first, value[:, MAIN:].reshape(groups * REST, units)], axis=0)


def on_device(out_grad, route_ids, route_weights, gate_pre, up_pre, w_gate, w_up, w_down):
    groups = lax.axis_size("expert")
    seq_at = lax.axis_index("seq")
    at = seq_at.astype(jnp.int32).reshape(1)
    local, width = out_grad.shape
    part = width // 2
    w_gate, w_up, w_down = w_gate[0], w_up[0], w_down[0]
    away = (1 - seq_at) * part
    other = swap(lax.dynamic_slice_in_dim(out_grad, away, part, 1))
    sent = dispatch(at, route_ids.T, out_grad, other, groups)
    w_gate, w_up, w_down, gate, up, sent = lax.optimization_barrier(
        (w_gate, w_up, w_down, gate_pre[0], up_pre[0], sent)
    )
    received = lax.all_to_all(
        sent.reshape(groups, MAIN, sent.shape[1]), "expert", split_axis=0, concat_axis=0, tiled=True
    )
    received = received.reshape(groups * MAIN, sent.shape[1])
    down_other = swap(lax.dynamic_slice_in_dim(w_down, away, part, 1))
    gate_other = swap(lax.dynamic_slice_in_dim(w_gate, away, part, 0))
    up_other = swap(lax.dynamic_slice_in_dim(w_up, away, part, 0))
    gate = by_part(gate, groups)
    up = by_part(up, groups)
    grad_other = swap(hidden(at, received, down_other, False))
    grad_mine = hidden(at, received, w_down, True)
    mine = diffs(grad_mine, grad_other, gate, up)
    theirs = swap(mine)
    slots = inputs(at, mine, theirs, w_gate, w_up, gate_other, up_other)
    back = lax.all_to_all(
        slots.reshape(groups, MAIN, slots.shape[1]), "expert", split_axis=0, concat_axis=0, tiled=True
    )
    total, weight_grad = combine(
        at, route_ids, route_weights, back.reshape(groups * MAIN, slots.shape[1])
    )
    keep = lax.dynamic_slice_in_dim(total, seq_at * local, local, 1)
    came = swap(lax.dynamic_slice_in_dim(total, (1 - seq_at) * local, local, 1))
    first = jnp.where(seq_at == 0, keep, came)
    second = jnp.where(seq_at == 0, came, keep)
    return jnp.concatenate([first[0], first[1], second[0], second[1]], axis=1), weight_grad


def solution(mesh):
    in_specs = (
        P(("expert", "seq"), None),
        P("expert", None),
        P("expert", None),
        P("expert", None, "seq"),
        P("expert", None, "seq"),
        P("expert", None, "seq"),
        P("expert", None, "seq"),
        P("expert", "seq", None),
    )
    out_specs = (P(("expert", "seq"), None), P(("expert", "seq"), None))
    return jax.shard_map(
        on_device, mesh=mesh, in_specs=in_specs, out_specs=out_specs, check_vma=False
    )
```

```python
import jax
import jax.numpy as jnp
from jax import lax
from jax.experimental import pallas as pl
from jax.experimental.pallas import tpu as pltpu
from jax.sharding import PartitionSpec as P

F32 = jnp.float32
BF16 = jnp.bfloat16
NT = (((1,), (1,)), ((), ()))
MAIN = 8
REST = 4
MIB = 1024 * 1024
LIMIT = 20 * MIB
TILE = 256


def iota(shape, dim):
    return lax.broadcasted_iota(jnp.int32, shape, dim)


def flag(cond):
    return jnp.where(cond, 1.0, 0.0).astype(F32)


def dot(a, b):
    return jnp.dot(a, b, preferred_element_type=F32)


def params(limit=LIMIT):
    return pltpu.CompilerParams(vmem_limit_bytes=limit)


def in_hbm(*values):
    return [pltpu.with_memory_space_constraint(v, pltpu.HBM) for v in values]


def swap(value):
    return lax.ppermute(value, "seq", [(0, 1), (1, 0)])


def actual(index, at, half):
    return (index + half * at) % (2 * half)


def routes_kernel(at_ref, own_ids, other_ids, own_weights, other_weights, pa_ref, pb_ref, w_ref):
    at = at_ref[0]
    ids = jnp.concatenate([own_ids[...], other_ids[...]], axis=1)
    weights = jnp.concatenate([own_weights[...], other_weights[...]], axis=1)
    topk, tokens = ids.shape
    rows = pa_ref.shape[0]
    experts = rows // MAIN
    names = iota((experts, tokens), 0)
    member = jnp.zeros((experts, tokens), F32)
    gate = jnp.zeros((experts, tokens), F32)
    for k in range(topk):
        hit = names == ids[k : k + 1, :]
        member = member + flag(hit)
        gate = gate + jnp.where(hit, weights[k : k + 1, :], 0.0)
    first = actual(iota((tokens, tokens), 0), at, tokens // 2)
    before = flag(first < actual(iota((tokens, tokens), 1), at, tokens // 2)).astype(BF16)
    place = dot(member.astype(BF16), before)
    place = jnp.where(member > 0.5, place, -1.0).astype(BF16)
    spread = flag(iota((rows, experts), 0) // MAIN == iota((rows, experts), 1)).astype(BF16)
    wide = dot(spread, place).astype(jnp.int32)
    row = iota((rows, tokens), 0)
    pa_ref[...] = flag(wide == row % MAIN).astype(BF16)
    rest = flag(wide == MAIN + row % REST)
    upper = (row // REST) % 2
    pb_ref[:, :tokens] = jnp.where(upper == 0, rest, 0.0).astype(BF16)
    pb_ref[:, tokens:] = jnp.where(upper == 1, rest, 0.0).astype(BF16)

    def by_token(value):
        return lax.dot_general(value, spread, (((0,), (1,)), ((), ())), preferred_element_type=F32)

    wide = by_token(place).astype(jnp.int32)
    gate_high = gate.astype(BF16)
    gate_low = (gate - gate_high.astype(F32)).astype(BF16)
    lane = iota((tokens, rows), 1)
    in_rest = wide == MAIN + lane % REST
    upper = (lane // REST) % 2
    masks = (wide == lane % MAIN, in_rest & (upper == 0), in_rest & (upper == 1))
    for at_part, part in enumerate((by_token(gate_high), by_token(gate_low))):
        for at_mask, mask in enumerate(masks):
            low = (2 * at_mask + at_part) * tokens
            w_ref[low : low + tokens, :] = jnp.where(mask, part, 0.0).astype(BF16)


def routes(at, ids_t, weights_t, experts):
    topk, tokens = ids_t.shape
    half = tokens // 2
    rows = experts * MAIN
    own = pl.BlockSpec((topk, half), lambda j, at: (0, at[0]))
    other = pl.BlockSpec((topk, half), lambda j, at: (0, 1 - at[0]))
    shapes = [(rows, tokens), (rows, 2 * tokens), (6 * tokens, rows)]
    return pl.pallas_call(
        routes_kernel,
        grid_spec=pltpu.PrefetchScalarGridSpec(
            num_scalar_prefetch=1,
            grid=(1,),
            in_specs=[own, other, own, other],
            out_specs=[pl.BlockSpec(shape, lambda j, at: (0, 0)) for shape in shapes],
        ),
        out_shape=[jax.ShapeDtypeStruct(shape, BF16) for shape in shapes],
        compiler_params=params(),
        cost_estimate=pl.CostEstimate(flops=10**9, bytes_accessed=10**6, transcendentals=0),
        name="routes",
    )(at, ids_t, ids_t, weights_t, weights_t)


def dispatch_kernel(at_ref, pa_ref, pb_ref, own0, own1, other0, other1, out_ref):
    step = pl.program_id(0)
    first = jnp.concatenate([own0[...], other0[...]], axis=0)

    @pl.when(step < 4)
    def _():
        out_ref[...] = dot(pa_ref[...], first).astype(BF16)

    @pl.when(step >= 4)
    def _():
        both = jnp.concatenate([first, own1[...], other1[...]], axis=0)
        out_ref[...] = dot(pb_ref[...], both).astype(BF16)


def dispatch(at, pa, pb, out_grad, other):
    local, width = out_grad.shape
    rows = pa.shape[0]
    tile = width // 8

    def low(j):
        return jnp.where(j < 4, j, j - 4)

    def high(j):
        return jnp.maximum(j - 2, 2)

    return pl.pallas_call(
        dispatch_kernel,
        grid_spec=pltpu.PrefetchScalarGridSpec(
            num_scalar_prefetch=1,
            grid=(6,),
            in_specs=[
                pl.BlockSpec(pa.shape, lambda j, at: (0, 0)),
                pl.BlockSpec(pb.shape, lambda j, at: (0, 0)),
                pl.BlockSpec((local, tile), lambda j, at: (0, 4 * at[0] + low(j))),
                pl.BlockSpec((local, tile), lambda j, at: (0, 4 * at[0] + high(j))),
                pl.BlockSpec((local, tile), lambda j, at: (0, low(j))),
                pl.BlockSpec((local, tile), lambda j, at: (0, high(j))),
            ],
            out_specs=pl.BlockSpec((rows, tile), lambda j, at: (0, j)),
        ),
        out_shape=jax.ShapeDtypeStruct((rows, 6 * tile), BF16),
        compiler_params=params(),
        cost_estimate=pl.CostEstimate(flops=2 * 10**9, bytes_accessed=8 * 10**6, transcendentals=0),
        name="dispatch",
    )(at, pa, pb, out_grad, out_grad, other, other)


def hidden_kernel(at_ref, x_ref, w_ref, out_ref):
    main = x_ref.shape[0]
    units, part = w_ref.shape
    quarter = part // 2

    def product(low, high, start):
        return lax.dot_general(
            x_ref[:, low:high],
            w_ref[:, start : start + high - low],
            NT,
            preferred_element_type=F32,
        )

    pairs = main // 16
    first = product(0, part, 0).reshape(pairs, 2, 8, units)
    low = product(part, part + quarter, 0).reshape(pairs, 2, 8, units)
    high = product(part, part + quarter, quarter).reshape(pairs, 2, 8, units)
    top = iota((pairs, 8, units), 1) < REST
    even = low[:, 0] + pltpu.roll(high[:, 0], REST, 1)
    odd = high[:, 1] + pltpu.roll(low[:, 1], REST, 1)
    turned = pltpu.roll(first[:, 1], REST, 1)
    out_ref[...] = jnp.stack(
        [first[:, 0], jnp.where(top, even, turned), jnp.where(top, turned, odd)], axis=1
    ).reshape(main // 2 * 3, units)


def hidden(at, x, w, name):
    rows, lanes = x.shape
    units = w.shape[0]
    part = w.shape[1] // 2
    tile = 256
    return pl.pallas_call(
        hidden_kernel,
        grid_spec=pltpu.PrefetchScalarGridSpec(
            num_scalar_prefetch=1,
            grid=(units // tile,),
            in_specs=[
                pl.BlockSpec(memory_space=pltpu.VMEM),
                pl.BlockSpec((tile, part), lambda j, at: (j, at[0])),
            ],
            out_specs=pl.BlockSpec((rows // 2 * 3, tile), lambda j, at: (0, j)),
        ),
        out_shape=jax.ShapeDtypeStruct((rows // 2 * 3, units), F32),
        compiler_params=params(),
        cost_estimate=pl.CostEstimate(flops=0, bytes_accessed=0, transcendentals=0),
        name=name,
    )(at, x, w)


def diff_kernel(mine_ref, other_ref, gate_ref, up_ref, out_ref):
    units = mine_ref.shape[1]
    grad = mine_ref[...] + other_ref[...]
    value = gate_ref[...].astype(F32)
    up = up_ref[...].astype(F32)
    sigma = jax.nn.sigmoid(value)
    active = value * sigma
    slope = sigma * (1.0 + value * (1.0 - sigma))
    through = grad * active
    score = jnp.sum(through * up, axis=1, keepdims=True)
    out_ref[:, :units] = (grad * up * slope).astype(BF16)
    out_ref[:, units : 2 * units] = through.astype(BF16)
    out_ref[:, 2 * units :] = jnp.broadcast_to(score, (score.shape[0], 128)).astype(BF16)


def diffs(mine, other, gate, up):
    rows, units = mine.shape
    tile = 256
    spec = pl.BlockSpec((tile, units), lambda i: (i, 0))
    return pl.pallas_call(
        diff_kernel,
        grid=(rows // tile,),
        in_specs=[spec] * 4,
        out_specs=pl.BlockSpec((tile, 2 * units + 128), lambda i: (i, 0)),
        out_shape=jax.ShapeDtypeStruct((rows, 2 * units + 128), BF16),
        compiler_params=params(),
        cost_estimate=pl.CostEstimate(flops=0, bytes_accessed=0, transcendentals=0),
        name="diffs",
    )(mine, other, gate, up)


def parts_of(value):
    rows, lanes = value.shape
    pairs = rows // 24
    value = value.reshape(pairs, 3, 8, lanes)
    top = iota((pairs, 8, lanes), 1) < REST
    odd = jnp.where(top, pltpu.roll(value[:, 1], REST, 1), pltpu.roll(value[:, 2], REST, 1))
    main = jnp.stack([value[:, 0], odd], axis=1).reshape(16 * pairs, lanes)
    return main, value[:, 1], value[:, 2]


def both_quarters(low, high):
    top = iota(low[1].shape, 1) < REST
    even = jnp.where(top, low[1], pltpu.roll(high[1], REST, 1))
    odd = jnp.where(top, pltpu.roll(low[2], REST, 1), high[2])
    return jnp.stack([even, odd], axis=1).reshape(low[0].shape)


def inputs_kernel(at_ref, mine_ref, other_ref, g0, g1, u0, u1, og_ref, ou_ref, out_ref):
    step = pl.program_id(0)
    last = pl.num_programs(0) - 1
    units = g0.shape[1]
    quarter = last * TILE

    @pl.when(step < last)
    def _():
        x = jnp.concatenate([mine_ref[:, : 2 * units], other_ref[:, : 2 * units]], axis=1)

        def product(g, u, start):
            far = pl.ds(pl.multiple_of(2 * quarter * at_ref[0] + start + step * TILE, TILE), TILE)
            w = jnp.concatenate([g[...], u[...], og_ref[far, :], ou_ref[far, :]], axis=1)
            return lax.dot_general(x, w, NT, preferred_element_type=F32)

        low = parts_of(product(g0, u0, 0))
        high = parts_of(product(g1, u1, quarter))
        out_ref[:, :TILE] = low[0].astype(BF16)
        out_ref[:, TILE : 2 * TILE] = high[0].astype(BF16)
        out_ref[:, 2 * TILE :] = both_quarters(low, high).astype(BF16)

    @pl.when(step == last)
    def _():
        score = mine_ref[:, 2 * units :].astype(F32) + other_ref[:, 2 * units :].astype(F32)
        score = parts_of(score)
        lane = iota(score[0].shape, 1)
        out_ref[:, :128] = jnp.where(lane == 0, score[0], both_quarters(score, score)).astype(BF16)


def inputs(at, mine, other, w_gate, w_up, gate_other, up_other):
    w_gate, w_up = in_hbm(w_gate, w_up)
    rows, lanes = mine.shape
    units = w_gate.shape[1]
    part = w_gate.shape[0] // 2
    steps = part // 2 // TILE
    main = rows // 3 * 2

    def block(shift):
        return pl.BlockSpec(
            (TILE, units),
            lambda j, at: (at[0] * 2 * steps + shift * steps + jnp.minimum(j, steps - 1), 0),
        )

    whole = pl.BlockSpec(memory_space=pltpu.VMEM)
    return pl.pallas_call(
        inputs_kernel,
        grid_spec=pltpu.PrefetchScalarGridSpec(
            num_scalar_prefetch=1,
            grid=(steps + 1,),
            in_specs=[whole, whole, block(0), block(1), block(0), block(1), whole, whole],
            out_specs=pl.BlockSpec((main, 3 * TILE), lambda j, at: (0, j)),
        ),
        out_shape=jax.ShapeDtypeStruct((main, 3 * TILE * steps + 128), BF16),
        compiler_params=params(),
        cost_estimate=pl.CostEstimate(
            flops=8 * rows * part * units, bytes_accessed=24 * 10**6, transcendentals=0
        ),
        name="inputs",
    )(at, mine, other, w_gate, w_gate, w_up, w_up, gate_other, up_other)


def combine_kernel(
    at_ref, ids_ref, pa_ref, pb_ref, w_ref, back_ref, score_ref, keep_ref, send_ref, grad_ref
):
    step = pl.program_id(0)
    topk, half = ids_ref.shape
    tokens = 2 * half
    rows = back_ref.shape[0]
    experts = rows // MAIN

    @pl.when(step == 0)
    def _():
        block = iota((rows, experts), 0) // MAIN == iota((rows, experts), 1)
        score = score_ref[...].astype(F32)

        def one(column, slots):
            value = jnp.where(block, column, 0.0).astype(BF16)
            return lax.dot_general(value, slots, (((0,), (0,)), ((), ())), preferred_element_type=F32)

        table = one(score[:, 0:1], pa_ref[...]) + one(score[:, 1:2], pb_ref[...])
        names = iota((experts, half), 0)
        row = iota((topk, half), 0)
        ids = ids_ref[...]
        result = jnp.zeros((topk, half), F32)
        for k in range(topk):
            hit = names == ids[k : k + 1, :]
            picked = jnp.sum(jnp.where(hit, table, 0.0), axis=0, keepdims=True)
            result = result + jnp.where(row == k, picked, 0.0)
        grad_ref[...] = result.astype(BF16)

    main = dot(w_ref[: 2 * tokens, :], back_ref[:, : 2 * TILE])
    rest = dot(w_ref[2 * tokens :, :], back_ref[:, 2 * TILE :])
    main = main[:tokens] + main[tokens:]
    low = (main[:, :TILE] + (rest[:tokens] + rest[tokens : 2 * tokens])).astype(BF16)
    high = (main[:, TILE:] + (rest[2 * tokens : 3 * tokens] + rest[3 * tokens :])).astype(BF16)
    keep_ref[0] = low[:half]
    keep_ref[1] = high[:half]
    send_ref[0] = low[half:]
    send_ref[1] = high[half:]


def combine(at, ids_t, pa, pb, w, back):
    topk, tokens = ids_t.shape
    half = tokens // 2
    rows, lanes = back.shape
    steps = lanes // (3 * TILE)
    half_spec = pl.BlockSpec((2, half, TILE), lambda j, at: (0, 0, j))
    half_shape = jax.ShapeDtypeStruct((2, half, steps * TILE), BF16)
    return pl.pallas_call(
        combine_kernel,
        grid_spec=pltpu.PrefetchScalarGridSpec(
            num_scalar_prefetch=1,
            grid=(steps,),
            in_specs=[
                pl.BlockSpec((topk, half), lambda j, at: (0, at[0])),
                pl.BlockSpec((rows, half), lambda j, at: (0, 0)),
                pl.BlockSpec((rows, half), lambda j, at: (0, 0)),
                pl.BlockSpec(memory_space=pltpu.VMEM),
                pl.BlockSpec((rows, 3 * TILE), lambda j, at: (0, j)),
                pl.BlockSpec((rows, 128), lambda j, at: (0, steps * 3 * TILE // 128)),
            ],
            out_specs=[half_spec, half_spec, pl.BlockSpec((topk, half), lambda j, at: (0, 0))],
        ),
        out_shape=[half_shape, half_shape, jax.ShapeDtypeStruct((topk, half), BF16)],
        compiler_params=params(),
        cost_estimate=pl.CostEstimate(flops=4 * 10**9, bytes_accessed=8 * 10**6, transcendentals=0),
        name="combine",
    )(at, ids_t, pa, pb, w, back, back)


def join_kernel(at_ref, keep_ref, came_ref, out_ref):
    own = pl.program_id(0) // 2 == at_ref[0]

    @pl.when(own)
    def _():
        out_ref[...] = keep_ref[0]

    @pl.when(jnp.logical_not(own))
    def _():
        out_ref[...] = came_ref[0]


def join(at, keep, came):
    _, half, quarter = keep.shape
    spec = pl.BlockSpec((1, half, quarter), lambda j, at: (j % 2, 0, 0))
    return pl.pallas_call(
        join_kernel,
        grid_spec=pltpu.PrefetchScalarGridSpec(
            num_scalar_prefetch=1,
            grid=(4,),
            in_specs=[spec, spec],
            out_specs=pl.BlockSpec((half, quarter), lambda j, at: (0, j)),
        ),
        out_shape=jax.ShapeDtypeStruct((half, 4 * quarter), BF16),
        compiler_params=params(),
        cost_estimate=pl.CostEstimate(flops=0, bytes_accessed=4 * 10**6, transcendentals=0),
        name="join",
    )(at, keep, came)


def exchange(value, groups):
    rows, lanes = value.shape
    value = lax.all_to_all(
        value.reshape(groups, MAIN, lanes), "expert", split_axis=0, concat_axis=0, tiled=True
    )
    return value.reshape(rows, lanes)


def on_device(out_grad, route_ids, route_weights, gate_pre, up_pre, w_gate, w_up, w_down):
    groups = lax.axis_size("expert")
    seq_at = lax.axis_index("seq")
    at = seq_at.astype(jnp.int32).reshape(1)
    part = out_grad.shape[1] // 2
    w_gate, w_up, w_down = w_gate[0], w_up[0], w_down[0]
    other = swap(lax.dynamic_slice_in_dim(out_grad, (1 - seq_at) * part, part, 1))
    ids_t = route_ids.T
    pa, pb, w = routes(at, ids_t, route_weights.T, groups)
    sent = dispatch(at, pa, pb, out_grad, other)
    w_gate, w_up, w_down, sent = lax.optimization_barrier((w_gate, w_up, w_down, sent))
    down_other, gate_other, up_other = swap(w_down), swap(w_gate), swap(w_up)
    received = exchange(sent, groups)
    received, down_other, gate_other, up_other = lax.optimization_barrier(
        (received, down_other, gate_other, up_other)
    )
    grad_other = swap(hidden(at, received, down_other, "hidden_other"))
    grad_mine = hidden(at, received, in_hbm(w_down)[0], "hidden_own")
    mine = diffs(grad_mine, grad_other, gate_pre[0], up_pre[0])
    theirs = swap(mine)
    slots = inputs(at, mine, theirs, w_gate, w_up, gate_other, up_other)
    keep, send, weight_grad = combine(at, ids_t, pa, pb, w, exchange(slots, groups))
    return join(at, keep, swap(send)), weight_grad.T


def solution(mesh):
    in_specs = (
        P(("expert", "seq"), None),
        P("expert", None),
        P("expert", None),
        P("expert", None, "seq"),
        P("expert", None, "seq"),
        P("expert", None, "seq"),
        P("expert", None, "seq"),
        P("expert", "seq", None),
    )
    out_specs = (P(("expert", "seq"), None), P(("expert", "seq"), None))
    return jax.shard_map(
        on_device, mesh=mesh, in_specs=in_specs, out_specs=out_specs, check_vma=False
    )
```

```python
import jax
import jax.numpy as jnp
from jax import lax
from jax.experimental import pallas as pl
from jax.experimental.pallas import tpu as pltpu
from jax.sharding import PartitionSpec as P

F32 = jnp.float32
BF16 = jnp.bfloat16
NT = (((1,), (1,)), ((), ()))
MAIN = 8
REST = 4
MIB = 1024 * 1024
LIMIT = 20 * MIB
TILE = 256


def iota(shape, dim):
    return lax.broadcasted_iota(jnp.int32, shape, dim)


def flag(cond):
    return jnp.where(cond, 1.0, 0.0).astype(F32)


def dot(a, b):
    return jnp.dot(a, b, preferred_element_type=F32)


def params(limit=LIMIT):
    return pltpu.CompilerParams(vmem_limit_bytes=limit)


def in_hbm(*values):
    return [pltpu.with_memory_space_constraint(v, pltpu.HBM) for v in values]


def swap(value):
    return lax.ppermute(value, "seq", [(0, 1), (1, 0)])


def actual(index, at, half):
    return (index + half * at) % (2 * half)


def routes_kernel(at_ref, own_ids, other_ids, own_weights, other_weights, pa_ref, pb_ref, w_ref):
    at = at_ref[0]
    ids = jnp.concatenate([own_ids[...], other_ids[...]], axis=1)
    weights = jnp.concatenate([own_weights[...], other_weights[...]], axis=1)
    topk, tokens = ids.shape
    rows = pa_ref.shape[0]
    experts = rows // MAIN
    names = iota((experts, tokens), 0)
    member = jnp.zeros((experts, tokens), F32)
    gate = jnp.zeros((experts, tokens), F32)
    for k in range(topk):
        hit = names == ids[k : k + 1, :]
        member = member + flag(hit)
        gate = gate + jnp.where(hit, weights[k : k + 1, :], 0.0)
    first = actual(iota((tokens, tokens), 0), at, tokens // 2)
    before = flag(first < actual(iota((tokens, tokens), 1), at, tokens // 2)).astype(BF16)
    place = dot(member.astype(BF16), before)
    place = jnp.where(member > 0.5, place, -1.0).astype(BF16)
    spread = flag(iota((rows, experts), 0) // MAIN == iota((rows, experts), 1)).astype(BF16)
    wide = dot(spread, place).astype(jnp.int32)
    row = iota((rows, tokens), 0)
    pa_ref[...] = flag(wide == row % MAIN).astype(BF16)
    rest = flag(wide == MAIN + row % REST)
    upper = (row // REST) % 2
    pb_ref[:, :tokens] = jnp.where(upper == 0, rest, 0.0).astype(BF16)
    pb_ref[:, tokens:] = jnp.where(upper == 1, rest, 0.0).astype(BF16)

    def by_token(value):
        return lax.dot_general(value, spread, (((0,), (1,)), ((), ())), preferred_element_type=F32)

    wide = by_token(place).astype(jnp.int32)
    lane = iota((tokens, rows), 1)
    in_rest = wide == MAIN + lane % REST
    upper = (lane // REST) % 2
    gate = by_token(gate.astype(BF16))
    masks = (wide == lane % MAIN, in_rest & (upper == 0), in_rest & (upper == 1))
    for at_mask, mask in enumerate(masks):
        low = at_mask * tokens
        w_ref[low : low + tokens, :] = jnp.where(mask, gate, 0.0).astype(BF16)


def routes(at, ids_t, weights_t, experts):
    topk, tokens = ids_t.shape
    half = tokens // 2
    rows = experts * MAIN
    own = pl.BlockSpec((topk, half), lambda j, at: (0, at[0]))
    other = pl.BlockSpec((topk, half), lambda j, at: (0, 1 - at[0]))
    shapes = [(rows, tokens), (rows, 2 * tokens), (3 * tokens, rows)]
    return pl.pallas_call(
        routes_kernel,
        grid_spec=pltpu.PrefetchScalarGridSpec(
            num_scalar_prefetch=1,
            grid=(1,),
            in_specs=[own, other, own, other],
            out_specs=[pl.BlockSpec(shape, lambda j, at: (0, 0)) for shape in shapes],
        ),
        out_shape=[jax.ShapeDtypeStruct(shape, BF16) for shape in shapes],
        compiler_params=params(),
        cost_estimate=pl.CostEstimate(flops=10**9, bytes_accessed=10**6, transcendentals=0),
        name="routes",
    )(at, ids_t, ids_t, weights_t, weights_t)


def dispatch_kernel(at_ref, pa_ref, pb_ref, own0, own1, other0, other1, out_ref):
    step = pl.program_id(0)
    tile = own0.shape[1]
    cols = pl.ds(pl.multiple_of(step * tile, 128), tile)
    first = jnp.concatenate([own0[...], other0[...]], axis=0)

    @pl.when(step < 4)
    def _():
        out_ref[:, cols] = dot(pa_ref[...], first).astype(BF16)

    @pl.when(step >= 4)
    def _():
        both = jnp.concatenate([first, own1[...], other1[...]], axis=0)
        out_ref[:, cols] = dot(pb_ref[...], both).astype(BF16)


def dispatch(at, pa, pb, out_grad, other):
    local, width = out_grad.shape
    rows = pa.shape[0]
    tile = width // 8

    def low(j):
        return jnp.where(j < 4, j, j - 4)

    def high(j):
        return jnp.maximum(j - 2, 2)

    return pl.pallas_call(
        dispatch_kernel,
        grid_spec=pltpu.PrefetchScalarGridSpec(
            num_scalar_prefetch=1,
            grid=(6,),
            in_specs=[
                pl.BlockSpec(pa.shape, lambda j, at: (0, 0)),
                pl.BlockSpec(pb.shape, lambda j, at: (0, 0)),
                pl.BlockSpec((local, tile), lambda j, at: (0, 4 * at[0] + low(j))),
                pl.BlockSpec((local, tile), lambda j, at: (0, 4 * at[0] + high(j))),
                pl.BlockSpec((local, tile), lambda j, at: (0, low(j))),
                pl.BlockSpec((local, tile), lambda j, at: (0, high(j))),
            ],
            out_specs=pl.BlockSpec(memory_space=pltpu.VMEM),
        ),
        out_shape=jax.ShapeDtypeStruct((rows, 6 * tile), BF16),
        compiler_params=params(),
        cost_estimate=pl.CostEstimate(flops=2 * 10**9, bytes_accessed=8 * 10**6, transcendentals=0),
        name="dispatch",
    )(at, pa, pb, out_grad, out_grad, other, other)


def hidden_kernel(at_ref, x_ref, w_ref, out_ref):
    main = x_ref.shape[0]
    units, part = w_ref.shape
    quarter = part // 2

    def product(low, high, start):
        return lax.dot_general(
            x_ref[:, low:high],
            w_ref[:, start : start + high - low],
            NT,
            preferred_element_type=F32,
        )

    pairs = main // 16
    first = product(0, part, 0).reshape(pairs, 2, 8, units)
    low = product(part, part + quarter, 0).reshape(pairs, 2, 8, units)
    high = product(part, part + quarter, quarter).reshape(pairs, 2, 8, units)
    top = iota((pairs, 8, units), 1) < REST
    even = low[:, 0] + pltpu.roll(high[:, 0], REST, 1)
    odd = high[:, 1] + pltpu.roll(low[:, 1], REST, 1)
    turned = pltpu.roll(first[:, 1], REST, 1)
    out_ref[...] = jnp.stack(
        [first[:, 0], jnp.where(top, even, turned), jnp.where(top, turned, odd)], axis=1
    ).reshape(main // 2 * 3, units)


def hidden(at, x, w, name):
    rows, lanes = x.shape
    units = w.shape[0]
    part = w.shape[1] // 2
    tile = 256
    return pl.pallas_call(
        hidden_kernel,
        grid_spec=pltpu.PrefetchScalarGridSpec(
            num_scalar_prefetch=1,
            grid=(units // tile,),
            in_specs=[
                pl.BlockSpec(memory_space=pltpu.VMEM),
                pl.BlockSpec((tile, part), lambda j, at: (j, at[0])),
            ],
            out_specs=pl.BlockSpec((rows // 2 * 3, tile), lambda j, at: (0, j)),
        ),
        out_shape=jax.ShapeDtypeStruct((rows // 2 * 3, units), F32),
        compiler_params=params(),
        cost_estimate=pl.CostEstimate(flops=0, bytes_accessed=0, transcendentals=0),
        name=name,
    )(at, x, w)


def diff_kernel(mine_ref, other_ref, gate_ref, up_ref, out_ref):
    units = mine_ref.shape[1]
    grad = mine_ref[...] + other_ref[...]
    value = gate_ref[...].astype(F32)
    up = up_ref[...].astype(F32)
    sigma = jax.nn.sigmoid(value)
    active = value * sigma
    slope = sigma * (1.0 + value * (1.0 - sigma))
    through = grad * active
    score = jnp.sum(through * up, axis=1, keepdims=True)
    out_ref[:, :units] = (grad * up * slope).astype(BF16)
    out_ref[:, units : 2 * units] = through.astype(BF16)
    out_ref[:, 2 * units :] = jnp.broadcast_to(score, (score.shape[0], 128)).astype(BF16)


def diffs(mine, other, gate, up):
    rows, units = mine.shape
    tile = 256
    spec = pl.BlockSpec((tile, units), lambda i: (i, 0))
    return pl.pallas_call(
        diff_kernel,
        grid=(rows // tile,),
        in_specs=[spec] * 4,
        out_specs=pl.BlockSpec((tile, 2 * units + 128), lambda i: (i, 0)),
        out_shape=jax.ShapeDtypeStruct((rows, 2 * units + 128), BF16),
        compiler_params=params(),
        cost_estimate=pl.CostEstimate(flops=0, bytes_accessed=0, transcendentals=0),
        name="diffs",
    )(mine, other, gate, up)


def parts_of(value):
    rows, lanes = value.shape
    pairs = rows // 24
    value = value.reshape(pairs, 3, 8, lanes)
    top = iota((pairs, 8, lanes), 1) < REST
    odd = jnp.where(top, pltpu.roll(value[:, 1], REST, 1), pltpu.roll(value[:, 2], REST, 1))
    main = jnp.stack([value[:, 0], odd], axis=1).reshape(16 * pairs, lanes)
    return main, value[:, 1], value[:, 2]


def both_quarters(low, high):
    top = iota(low[1].shape, 1) < REST
    even = jnp.where(top, low[1], pltpu.roll(high[1], REST, 1))
    odd = jnp.where(top, pltpu.roll(low[2], REST, 1), high[2])
    return jnp.stack([even, odd], axis=1).reshape(low[0].shape)


def inputs_kernel(at_ref, mine_ref, other_ref, g0, g1, u0, u1, og_ref, ou_ref, out_ref):
    step = pl.program_id(0)
    units = g0.shape[1]
    quarter = pl.num_programs(0) * TILE
    x = jnp.concatenate([mine_ref[:, : 2 * units], other_ref[:, : 2 * units]], axis=1)

    def at_cols(start):
        return pl.ds(pl.multiple_of(start + step * TILE, TILE), TILE)

    def block(g, u, start):
        far = at_cols(2 * quarter * at_ref[0] + start)
        return jnp.concatenate([g[...], u[...], og_ref[far, :], ou_ref[far, :]], axis=1)

    w = jnp.concatenate([block(g0, u0, 0), block(g1, u1, quarter)], axis=0)
    result = lax.dot_general(x, w, NT, preferred_element_type=F32)
    low = parts_of(result[:, :TILE])
    high = parts_of(result[:, TILE:])
    out_ref[:, at_cols(0)] = low[0].astype(BF16)
    out_ref[:, at_cols(quarter)] = high[0].astype(BF16)
    out_ref[:, at_cols(2 * quarter)] = both_quarters(low, high).astype(BF16)

    @pl.when(step == 0)
    def _():
        score = mine_ref[:, 2 * units :].astype(F32) + other_ref[:, 2 * units :].astype(F32)
        score = parts_of(score)
        lane = iota(score[0].shape, 1)
        end = out_ref.shape[1] - 128
        out_ref[:, end:] = jnp.where(lane == 0, score[0], both_quarters(score, score)).astype(BF16)


def inputs(at, mine, other, w_gate, w_up, gate_other, up_other):
    w_gate, w_up = in_hbm(w_gate, w_up)
    rows, lanes = mine.shape
    units = w_gate.shape[1]
    part = w_gate.shape[0] // 2
    steps = part // 2 // TILE
    main = rows // 3 * 2

    def block(shift):
        return pl.BlockSpec(
            (TILE, units),
            lambda j, at: (at[0] * 2 * steps + shift * steps + j, 0),
        )

    whole = pl.BlockSpec(memory_space=pltpu.VMEM)
    return pl.pallas_call(
        inputs_kernel,
        grid_spec=pltpu.PrefetchScalarGridSpec(
            num_scalar_prefetch=1,
            grid=(steps,),
            in_specs=[whole, whole, block(0), block(1), block(0), block(1), whole, whole],
            out_specs=whole,
        ),
        out_shape=jax.ShapeDtypeStruct((main, 3 * TILE * steps + 128), BF16),
        compiler_params=params(),
        cost_estimate=pl.CostEstimate(
            flops=8 * rows * part * units, bytes_accessed=24 * 10**6, transcendentals=0
        ),
        name="inputs",
    )(at, mine, other, w_gate, w_gate, w_up, w_up, gate_other, up_other)


def combine_kernel(
    at_ref, ids_ref, pa_ref, pb_ref, w_ref, back_ref, keep_ref, send_ref, grad_ref
):
    step = pl.program_id(0)
    topk, half = ids_ref.shape
    tokens = 2 * half
    rows = back_ref.shape[0]
    experts = rows // MAIN

    @pl.when(step == 0)
    def _():
        block = iota((rows, experts), 0) // MAIN == iota((rows, experts), 1)
        score = back_ref[:, back_ref.shape[1] - 128 :].astype(F32)

        def one(column, slots):
            value = jnp.where(block, column, 0.0).astype(BF16)
            return lax.dot_general(value, slots, (((0,), (0,)), ((), ())), preferred_element_type=F32)

        table = one(score[:, 0:1], pa_ref[...]) + one(score[:, 1:2], pb_ref[...])
        names = iota((experts, half), 0)
        row = iota((topk, half), 0)
        ids = ids_ref[...]
        result = jnp.zeros((topk, half), F32)
        for k in range(topk):
            hit = names == ids[k : k + 1, :]
            picked = jnp.sum(jnp.where(hit, table, 0.0), axis=0, keepdims=True)
            result = result + jnp.where(row == k, picked, 0.0)
        grad_ref[...] = result.astype(BF16)

    tile = keep_ref.shape[1]
    low = pl.ds(pl.multiple_of(step * tile, 128), tile)
    rest = pl.ds(pl.multiple_of((4 + step % 2) * tile, 128), tile)
    part = pl.ds(pl.multiple_of((1 + step // 2) * tokens, tokens), tokens)
    slots = jnp.concatenate([back_ref[:, low], back_ref[:, rest]], axis=0)
    total = dot(jnp.concatenate([w_ref[:tokens, :], w_ref[part, :]], axis=1), slots).astype(BF16)
    keep_ref[...] = total[:half]
    send_ref[...] = total[half:]


def combine(at, ids_t, pa, pb, w, back):
    topk, tokens = ids_t.shape
    half = tokens // 2
    rows, lanes = back.shape
    tile = (lanes - 128) // 6
    whole = pl.BlockSpec(memory_space=pltpu.VMEM)
    return pl.pallas_call(
        combine_kernel,
        grid_spec=pltpu.PrefetchScalarGridSpec(
            num_scalar_prefetch=1,
            grid=(4,),
            in_specs=[
                pl.BlockSpec((topk, half), lambda j, at: (0, at[0])),
                pl.BlockSpec((rows, half), lambda j, at: (0, 0)),
                pl.BlockSpec((rows, half), lambda j, at: (0, 0)),
                whole,
                whole,
            ],
            out_specs=[
                pl.BlockSpec((half, tile), lambda j, at: (0, 4 * at[0] + j)),
                pl.BlockSpec((half, tile), lambda j, at: (0, j)),
                pl.BlockSpec((topk, half), lambda j, at: (0, 0)),
            ],
        ),
        out_shape=[
            jax.ShapeDtypeStruct((half, 8 * tile), BF16),
            jax.ShapeDtypeStruct((half, 4 * tile), BF16),
            jax.ShapeDtypeStruct((topk, half), BF16),
        ],
        compiler_params=params(),
        cost_estimate=pl.CostEstimate(flops=2 * 10**9, bytes_accessed=8 * 10**6, transcendentals=0),
        name="combine",
    )(at, ids_t, pa, pb, w, back)


def join_kernel(at_ref, base_ref, came_ref, out_ref):
    out_ref[...] = came_ref[...]


def join(at, base, came):
    half, part = came.shape
    return pl.pallas_call(
        join_kernel,
        grid_spec=pltpu.PrefetchScalarGridSpec(
            num_scalar_prefetch=1,
            grid=(2,),
            in_specs=[
                pl.BlockSpec(memory_space=pl.ANY),
                pl.BlockSpec((half, part // 2), lambda j, at: (0, j)),
            ],
            out_specs=pl.BlockSpec((half, part // 2), lambda j, at: (0, 2 * (1 - at[0]) + j)),
        ),
        out_shape=jax.ShapeDtypeStruct(base.shape, BF16),
        input_output_aliases={1: 0},
        compiler_params=params(),
        cost_estimate=pl.CostEstimate(flops=0, bytes_accessed=2 * 10**6, transcendentals=0),
        name="join",
    )(at, base, came)


def exchange(value, groups):
    rows, lanes = value.shape
    value = lax.all_to_all(
        value.reshape(groups, MAIN, lanes), "expert", split_axis=0, concat_axis=0, tiled=True
    )
    return value.reshape(rows, lanes)


def on_device(out_grad, route_ids, route_weights, gate_pre, up_pre, w_gate, w_up, w_down):
    groups = lax.axis_size("expert")
    seq_at = lax.axis_index("seq")
    at = seq_at.astype(jnp.int32).reshape(1)
    part = out_grad.shape[1] // 2
    w_gate, w_up, w_down = w_gate[0], w_up[0], w_down[0]
    other = swap(lax.dynamic_slice_in_dim(out_grad, (1 - seq_at) * part, part, 1))
    ids_t = route_ids.T
    pa, pb, w = routes(at, ids_t, route_weights.T, groups)
    sent = dispatch(at, pa, pb, out_grad, other)
    w_gate, w_up, w_down, sent = lax.optimization_barrier((w_gate, w_up, w_down, sent))
    down_other, gate_other, up_other = swap(w_down), swap(w_gate), swap(w_up)
    received = exchange(sent, groups)
    received, down_other, gate_other, up_other = lax.optimization_barrier(
        (received, down_other, gate_other, up_other)
    )
    grad_other = swap(hidden(at, received, down_other, "hidden_other"))
    grad_mine = hidden(at, received, in_hbm(w_down)[0], "hidden_own")
    mine = diffs(grad_mine, grad_other, gate_pre[0], up_pre[0])
    theirs = swap(mine)
    slots = inputs(at, mine, theirs, w_gate, w_up, gate_other, up_other)
    keep, send, weight_grad = combine(at, ids_t, pa, pb, w, exchange(slots, groups))
    return join(at, keep, swap(send)), weight_grad.T


def solution(mesh):
    in_specs = (
        P(("expert", "seq"), None),
        P("expert", None),
        P("expert", None),
        P("expert", None, "seq"),
        P("expert", None, "seq"),
        P("expert", None, "seq"),
        P("expert", None, "seq"),
        P("expert", "seq", None),
    )
    out_specs = (P(("expert", "seq"), None), P(("expert", "seq"), None))
    return jax.shard_map(
        on_device, mesh=mesh, in_specs=in_specs, out_specs=out_specs, check_vma=False
    )
```

```python
import jax
import jax.numpy as jnp
from jax import lax
from jax.experimental import pallas as pl
from jax.experimental.pallas import tpu as pltpu
from jax.sharding import PartitionSpec as P

F32 = jnp.float32
BF16 = jnp.bfloat16
NT = (((1,), (1,)), ((), ()))
MAIN = 8
REST = 4
MIB = 1024 * 1024
LIMIT = 14 * MIB
TILE = 256
EARLY = 3


def iota(shape, dim):
    return lax.broadcasted_iota(jnp.int32, shape, dim)


def flag(cond):
    return jnp.where(cond, 1.0, 0.0).astype(F32)


def dot(a, b):
    return jnp.dot(a, b, preferred_element_type=F32)


def params(limit=LIMIT):
    return pltpu.CompilerParams(vmem_limit_bytes=limit)


def in_hbm(*values):
    return [pltpu.with_memory_space_constraint(v, pltpu.HBM) for v in values]


def swap(value):
    return lax.ppermute(value, "seq", [(0, 1), (1, 0)])


def actual(index, at, half):
    return (index + half * at) % (2 * half)


def routes_kernel(at_ref, own_ids, other_ids, own_weights, other_weights, pa_ref, pb_ref, w_ref):
    at = at_ref[0]
    ids = jnp.concatenate([own_ids[...], other_ids[...]], axis=1)
    weights = jnp.concatenate([own_weights[...], other_weights[...]], axis=1)
    topk, tokens = ids.shape
    rows = pa_ref.shape[0]
    experts = rows // MAIN
    names = iota((experts, tokens), 0)
    member = jnp.zeros((experts, tokens), F32)
    gate = jnp.zeros((experts, tokens), F32)
    for k in range(topk):
        hit = names == ids[k : k + 1, :]
        member = member + flag(hit)
        gate = gate + jnp.where(hit, weights[k : k + 1, :], 0.0)
    first = actual(iota((tokens, tokens), 0), at, tokens // 2)
    before = flag(first < actual(iota((tokens, tokens), 1), at, tokens // 2)).astype(BF16)
    place = dot(member.astype(BF16), before)
    place = jnp.where(member > 0.5, place, -1.0).astype(BF16)
    spread = flag(iota((rows, experts), 0) // MAIN == iota((rows, experts), 1)).astype(BF16)
    wide = dot(spread, place).astype(jnp.int32)
    row = iota((rows, tokens), 0)
    pa_ref[...] = flag(wide == row % MAIN).astype(BF16)
    rest = flag(wide == MAIN + row % REST)
    upper = (row // REST) % 2
    pb_ref[:, :tokens] = jnp.where(upper == 0, rest, 0.0).astype(BF16)
    pb_ref[:, tokens:] = jnp.where(upper == 1, rest, 0.0).astype(BF16)

    def by_token(value):
        return lax.dot_general(value, spread, (((0,), (1,)), ((), ())), preferred_element_type=F32)

    wide = by_token(place).astype(jnp.int32)
    lane = iota((tokens, rows), 1)
    in_rest = wide == MAIN + lane % REST
    upper = (lane // REST) % 2
    gate = by_token(gate.astype(BF16))
    masks = (wide == lane % MAIN, in_rest & (upper == 0), in_rest & (upper == 1))
    for at_mask, mask in enumerate(masks):
        low = at_mask * tokens
        w_ref[low : low + tokens, :] = jnp.where(mask, gate, 0.0).astype(BF16)


def routes(at, ids_t, weights_t, experts):
    topk, tokens = ids_t.shape
    half = tokens // 2
    rows = experts * MAIN
    own = pl.BlockSpec((topk, half), lambda j, at: (0, at[0]))
    other = pl.BlockSpec((topk, half), lambda j, at: (0, 1 - at[0]))
    shapes = [(rows, tokens), (rows, 2 * tokens), (3 * tokens, rows)]
    return pl.pallas_call(
        routes_kernel,
        grid_spec=pltpu.PrefetchScalarGridSpec(
            num_scalar_prefetch=1,
            grid=(1,),
            in_specs=[own, other, own, other],
            out_specs=[pl.BlockSpec(shape, lambda j, at: (0, 0)) for shape in shapes],
        ),
        out_shape=[jax.ShapeDtypeStruct(shape, BF16) for shape in shapes],
        compiler_params=params(),
        cost_estimate=pl.CostEstimate(flops=10**9, bytes_accessed=10**6, transcendentals=0),
        name="routes",
    )(at, ids_t, ids_t, weights_t, weights_t)


def dispatch_kernel(at_ref, pa_ref, pb_ref, own0, own1, other0, other1, out_ref):
    step = pl.program_id(0)
    tile = own0.shape[1]
    cols = pl.ds(pl.multiple_of(step * tile, 128), tile)
    first = jnp.concatenate([own0[...], other0[...]], axis=0)

    @pl.when(step < 4)
    def _():
        out_ref[:, cols] = dot(pa_ref[...], first).astype(BF16)

    @pl.when(step >= 4)
    def _():
        both = jnp.concatenate([first, own1[...], other1[...]], axis=0)
        out_ref[:, cols] = dot(pb_ref[...], both).astype(BF16)


def dispatch(at, pa, pb, out_grad, other):
    local, width = out_grad.shape
    rows = pa.shape[0]
    tile = width // 8

    def low(j):
        return jnp.where(j < 4, j, j - 4)

    def high(j):
        return jnp.maximum(j - 2, 2)

    return pl.pallas_call(
        dispatch_kernel,
        grid_spec=pltpu.PrefetchScalarGridSpec(
            num_scalar_prefetch=1,
            grid=(6,),
            in_specs=[
                pl.BlockSpec(pa.shape, lambda j, at: (0, 0)),
                pl.BlockSpec(pb.shape, lambda j, at: (0, 0)),
                pl.BlockSpec((local, tile), lambda j, at: (0, 4 * at[0] + low(j))),
                pl.BlockSpec((local, tile), lambda j, at: (0, 4 * at[0] + high(j))),
                pl.BlockSpec((local, tile), lambda j, at: (0, low(j))),
                pl.BlockSpec((local, tile), lambda j, at: (0, high(j))),
            ],
            out_specs=pl.BlockSpec(memory_space=pltpu.VMEM),
        ),
        out_shape=jax.ShapeDtypeStruct((rows, 6 * tile), BF16),
        compiler_params=params(),
        cost_estimate=pl.CostEstimate(flops=2 * 10**9, bytes_accessed=8 * 10**6, transcendentals=0),
        name="dispatch",
    )(at, pa, pb, out_grad, out_grad, other, other)


def hidden_kernel(at_ref, x_ref, w_ref, out_ref):
    step = pl.program_id(0)
    main = x_ref.shape[0]
    units = out_ref.shape[1]
    part = w_ref.shape[1] // 2
    quarter = part // 2

    def product(low, high, start):
        rows = pl.ds(pl.multiple_of(step * units, units), units)
        cols = pl.ds(pl.multiple_of(at_ref[0] * part + start, 128), high - low)
        return lax.dot_general(x_ref[:, low:high], w_ref[rows, cols], NT, preferred_element_type=F32)

    pairs = main // 16
    first = product(0, part, 0).reshape(pairs, 2, 8, units)
    low = product(part, part + quarter, 0).reshape(pairs, 2, 8, units)
    high = product(part, part + quarter, quarter).reshape(pairs, 2, 8, units)
    top = iota((pairs, 8, units), 1) < REST
    even = low[:, 0] + pltpu.roll(high[:, 0], REST, 1)
    odd = high[:, 1] + pltpu.roll(low[:, 1], REST, 1)
    turned = pltpu.roll(first[:, 1], REST, 1)
    out_ref[...] = jnp.stack(
        [first[:, 0], jnp.where(top, even, turned), jnp.where(top, turned, odd)], axis=1
    ).reshape(main // 2 * 3, units)


def hidden(at, x, w, name):
    rows, lanes = x.shape
    units = w.shape[0]
    tile = 256
    whole = pl.BlockSpec(memory_space=pltpu.VMEM)
    return pl.pallas_call(
        hidden_kernel,
        grid_spec=pltpu.PrefetchScalarGridSpec(
            num_scalar_prefetch=1,
            grid=(units // tile,),
            in_specs=[whole, whole],
            out_specs=pl.BlockSpec((rows // 2 * 3, tile), lambda j, at: (0, j)),
        ),
        out_shape=jax.ShapeDtypeStruct((rows // 2 * 3, units), F32),
        compiler_params=params(),
        cost_estimate=pl.CostEstimate(flops=0, bytes_accessed=0, transcendentals=0),
        name=name,
    )(at, x, w)


def diff_kernel(mine_ref, other_ref, gate_ref, up_ref, out_ref):
    units = mine_ref.shape[1]
    grad = mine_ref[...] + other_ref[...]
    value = gate_ref[...].astype(F32)
    up = up_ref[...].astype(F32)
    sigma = jax.nn.sigmoid(value)
    active = value * sigma
    slope = sigma * (1.0 + value * (1.0 - sigma))
    through = grad * active
    score = jnp.sum(through * up, axis=1, keepdims=True)
    out_ref[:, :units] = (grad * up * slope).astype(BF16)
    out_ref[:, units : 2 * units] = through.astype(BF16)
    out_ref[:, 2 * units :] = jnp.broadcast_to(score, (score.shape[0], 128)).astype(BF16)


def diffs(mine, other, gate, up):
    rows, units = mine.shape
    tile = 256
    spec = pl.BlockSpec((tile, units), lambda i: (i, 0))
    return pl.pallas_call(
        diff_kernel,
        grid=(rows // tile,),
        in_specs=[spec] * 4,
        out_specs=pl.BlockSpec((tile, 2 * units + 128), lambda i: (i, 0)),
        out_shape=jax.ShapeDtypeStruct((rows, 2 * units + 128), BF16),
        compiler_params=params(),
        cost_estimate=pl.CostEstimate(flops=0, bytes_accessed=0, transcendentals=0),
        name="diffs",
    )(mine, other, gate, up)


def parts_of(value):
    rows, lanes = value.shape
    pairs = rows // 24
    value = value.reshape(pairs, 3, 8, lanes)
    top = iota((pairs, 8, lanes), 1) < REST
    odd = jnp.where(top, pltpu.roll(value[:, 1], REST, 1), pltpu.roll(value[:, 2], REST, 1))
    main = jnp.stack([value[:, 0], odd], axis=1).reshape(16 * pairs, lanes)
    return main, value[:, 1], value[:, 2]


def both_quarters(low, high):
    top = iota(low[1].shape, 1) < REST
    even = jnp.where(top, low[1], pltpu.roll(high[1], REST, 1))
    odd = jnp.where(top, pltpu.roll(low[2], REST, 1), high[2])
    return jnp.stack([even, odd], axis=1).reshape(low[0].shape)


def own_block(units, steps, shift):
    return pl.BlockSpec((TILE, units), lambda j, at: (at[0] * 2 * steps + shift * steps + j, 0))


def early_kernel(at_ref, mine_ref, g0, g1, u0, u1, out_ref):
    units = g0.shape[1]
    w = jnp.concatenate(
        [
            jnp.concatenate([g0[...], u0[...]], axis=1),
            jnp.concatenate([g1[...], u1[...]], axis=1),
        ],
        axis=0,
    )
    cols = pl.ds(pl.multiple_of(pl.program_id(0) * 2 * TILE, TILE), 2 * TILE)
    out_ref[:, cols] = lax.dot_general(mine_ref[:, : 2 * units], w, NT, preferred_element_type=F32)


def early_inputs(at, mine, w_gate, w_up):
    w_gate, w_up = in_hbm(w_gate, w_up)
    rows = mine.shape[0]
    units = w_gate.shape[1]
    steps = w_gate.shape[0] // 4 // TILE
    whole = pl.BlockSpec(memory_space=pltpu.VMEM)
    blocks = [own_block(units, steps, 0), own_block(units, steps, 1)]
    return pl.pallas_call(
        early_kernel,
        grid_spec=pltpu.PrefetchScalarGridSpec(
            num_scalar_prefetch=1,
            grid=(EARLY,),
            in_specs=[whole] + blocks + blocks,
            out_specs=whole,
        ),
        out_shape=jax.ShapeDtypeStruct((rows, EARLY * 2 * TILE), F32),
        compiler_params=params(),
        cost_estimate=pl.CostEstimate(
            flops=8 * EARLY * rows * TILE * units, bytes_accessed=10**7, transcendentals=0
        ),
        name="early_inputs",
    )(at, mine, w_gate, w_gate, w_up, w_up)


def inputs_kernel(
    at_ref, mine_ref, other_ref, early_ref, g0, g1, u0, u1, og_ref, ou_ref, out_ref
):
    step = pl.program_id(0)
    units = g0.shape[1]
    quarter = pl.num_programs(0) * TILE

    def at_cols(start):
        return pl.ds(pl.multiple_of(start + step * TILE, TILE), TILE)

    def far(start):
        rows = at_cols(2 * quarter * at_ref[0] + start)
        return [og_ref[rows, :], ou_ref[rows, :]]

    def product(x, low, high):
        w = jnp.concatenate(
            [jnp.concatenate(low, axis=1), jnp.concatenate(high, axis=1)], axis=0
        )
        return lax.dot_general(x, w, NT, preferred_element_type=F32)

    def finish(result):
        low = parts_of(result[:, :TILE])
        high = parts_of(result[:, TILE:])
        out_ref[:, at_cols(0)] = low[0].astype(BF16)
        out_ref[:, at_cols(quarter)] = high[0].astype(BF16)
        out_ref[:, at_cols(2 * quarter)] = both_quarters(low, high).astype(BF16)

    @pl.when(step < EARLY)
    def _():
        cols = pl.ds(pl.multiple_of(step * 2 * TILE, TILE), 2 * TILE)
        finish(product(other_ref[:, : 2 * units], far(0), far(quarter)) + early_ref[:, cols])

    @pl.when(step >= EARLY)
    def _():
        x = jnp.concatenate([mine_ref[:, : 2 * units], other_ref[:, : 2 * units]], axis=1)
        low = [g0[...], u0[...]] + far(0)
        high = [g1[...], u1[...]] + far(quarter)
        finish(product(x, low, high))

    @pl.when(step == 0)
    def _():
        score = mine_ref[:, 2 * units :].astype(F32) + other_ref[:, 2 * units :].astype(F32)
        score = parts_of(score)
        lane = iota(score[0].shape, 1)
        end = out_ref.shape[1] - 128
        out_ref[:, end:] = jnp.where(lane == 0, score[0], both_quarters(score, score)).astype(BF16)


def inputs(at, mine, other, early, w_gate, w_up, gate_other, up_other):
    w_gate, w_up = in_hbm(w_gate, w_up)
    rows, lanes = mine.shape
    units = w_gate.shape[1]
    part = w_gate.shape[0] // 2
    steps = part // 2 // TILE
    main = rows // 3 * 2

    def block(shift):
        return pl.BlockSpec(
            (TILE, units),
            lambda j, at: (at[0] * 2 * steps + shift * steps + jnp.maximum(j, EARLY), 0),
        )

    whole = pl.BlockSpec(memory_space=pltpu.VMEM)
    return pl.pallas_call(
        inputs_kernel,
        grid_spec=pltpu.PrefetchScalarGridSpec(
            num_scalar_prefetch=1,
            grid=(steps,),
            in_specs=[whole] * 3 + [block(0), block(1), block(0), block(1), whole, whole],
            out_specs=whole,
        ),
        out_shape=jax.ShapeDtypeStruct((main, 3 * TILE * steps + 128), BF16),
        compiler_params=params(),
        cost_estimate=pl.CostEstimate(
            flops=8 * rows * part * units, bytes_accessed=24 * 10**6, transcendentals=0
        ),
        name="inputs",
    )(at, mine, other, early, w_gate, w_gate, w_up, w_up, gate_other, up_other)


def tokens_of(w_ref, back_ref, out_ref, first):
    step = pl.program_id(0)
    half, tile = out_ref.shape
    tokens = 2 * half
    low = pl.ds(pl.multiple_of(step * tile, 128), tile)
    rest = pl.ds(pl.multiple_of((4 + step % 2) * tile, 128), tile)
    part = pl.ds(pl.multiple_of((1 + step // 2) * tokens + first, half), half)
    slots = jnp.concatenate([back_ref[:, low], back_ref[:, rest]], axis=0)
    w = jnp.concatenate([w_ref[first : first + half, :], w_ref[part, :]], axis=1)
    out_ref[...] = dot(w, slots).astype(BF16)


def send_kernel(w_ref, back_ref, send_ref):
    tokens_of(w_ref, back_ref, send_ref, send_ref.shape[0])


def combine_send(w, back):
    half = w.shape[0] // 6
    tile = (back.shape[1] - 128) // 6
    whole = pl.BlockSpec(memory_space=pltpu.VMEM)
    return pl.pallas_call(
        send_kernel,
        grid=(4,),
        in_specs=[whole, whole],
        out_specs=pl.BlockSpec((half, tile), lambda j: (0, j)),
        out_shape=jax.ShapeDtypeStruct((half, 4 * tile), BF16),
        compiler_params=params(),
        cost_estimate=pl.CostEstimate(flops=10**9, bytes_accessed=7 * 10**6, transcendentals=0),
        name="combine_send",
    )(w, back)


def keep_kernel(at_ref, ids_ref, pa_ref, pb_ref, w_ref, back_ref, keep_ref, grad_ref):
    topk, half = ids_ref.shape
    rows = back_ref.shape[0]
    experts = rows // MAIN

    @pl.when(pl.program_id(0) == 0)
    def _():
        block = iota((rows, experts), 0) // MAIN == iota((rows, experts), 1)
        score = back_ref[:, back_ref.shape[1] - 128 :].astype(F32)

        def one(column, slots):
            value = jnp.where(block, column, 0.0).astype(BF16)
            return lax.dot_general(value, slots, (((0,), (0,)), ((), ())), preferred_element_type=F32)

        table = one(score[:, 0:1], pa_ref[...]) + one(score[:, 1:2], pb_ref[...])
        names = iota((experts, half), 0)
        row = iota((topk, half), 0)
        ids = ids_ref[...]
        result = jnp.zeros((topk, half), F32)
        for k in range(topk):
            hit = names == ids[k : k + 1, :]
            picked = jnp.sum(jnp.where(hit, table, 0.0), axis=0, keepdims=True)
            result = result + jnp.where(row == k, picked, 0.0)
        grad_ref[...] = result.astype(BF16)

    tokens_of(w_ref, back_ref, keep_ref, 0)


def combine_keep(at, ids_t, pa, pb, w, back):
    topk, tokens = ids_t.shape
    half = tokens // 2
    rows, lanes = back.shape
    tile = (lanes - 128) // 6
    whole = pl.BlockSpec(memory_space=pltpu.VMEM)
    return pl.pallas_call(
        keep_kernel,
        grid_spec=pltpu.PrefetchScalarGridSpec(
            num_scalar_prefetch=1,
            grid=(4,),
            in_specs=[
                pl.BlockSpec((topk, half), lambda j, at: (0, at[0])),
                pl.BlockSpec((rows, half), lambda j, at: (0, 0)),
                pl.BlockSpec((rows, half), lambda j, at: (0, 0)),
                whole,
                whole,
            ],
            out_specs=[
                pl.BlockSpec((half, tile), lambda j, at: (0, 4 * at[0] + j)),
                pl.BlockSpec((topk, half), lambda j, at: (0, 0)),
            ],
        ),
        out_shape=[
            jax.ShapeDtypeStruct((half, 8 * tile), BF16),
            jax.ShapeDtypeStruct((topk, half), BF16),
        ],
        compiler_params=params(),
        cost_estimate=pl.CostEstimate(flops=10**9, bytes_accessed=7 * 10**6, transcendentals=0),
        name="combine_keep",
    )(at, ids_t, pa, pb, w, back)


def join_kernel(at_ref, base_ref, came_ref, out_ref):
    out_ref[...] = came_ref[...]


def join(at, base, came):
    half, part = came.shape
    return pl.pallas_call(
        join_kernel,
        grid_spec=pltpu.PrefetchScalarGridSpec(
            num_scalar_prefetch=1,
            grid=(2,),
            in_specs=[
                pl.BlockSpec(memory_space=pl.ANY),
                pl.BlockSpec((half, part // 2), lambda j, at: (0, j)),
            ],
            out_specs=pl.BlockSpec((half, part // 2), lambda j, at: (0, 2 * (1 - at[0]) + j)),
        ),
        out_shape=jax.ShapeDtypeStruct(base.shape, BF16),
        input_output_aliases={1: 0},
        compiler_params=params(),
        cost_estimate=pl.CostEstimate(flops=0, bytes_accessed=2 * 10**6, transcendentals=0),
        name="join",
    )(at, base, came)


def exchange(value, groups):
    rows, lanes = value.shape
    value = lax.all_to_all(
        value.reshape(groups, MAIN, lanes), "expert", split_axis=0, concat_axis=0, tiled=True
    )
    return value.reshape(rows, lanes)


def on_device(out_grad, route_ids, route_weights, gate_pre, up_pre, w_gate, w_up, w_down):
    groups = lax.axis_size("expert")
    seq_at = lax.axis_index("seq")
    at = seq_at.astype(jnp.int32).reshape(1)
    part = out_grad.shape[1] // 2
    w_gate, w_up, w_down = w_gate[0], w_up[0], w_down[0]
    other = swap(lax.dynamic_slice_in_dim(out_grad, (1 - seq_at) * part, part, 1))
    ids_t = route_ids.T
    pa, pb, w = routes(at, ids_t, route_weights.T, groups)
    sent = dispatch(at, pa, pb, out_grad, other)
    w_gate, w_up, w_down, sent = lax.optimization_barrier((w_gate, w_up, w_down, sent))
    down_other, gate_other, up_other = swap(w_down), swap(w_gate), swap(w_up)
    received = exchange(sent, groups)
    received, down_other, gate_other, up_other = lax.optimization_barrier(
        (received, down_other, gate_other, up_other)
    )
    grad_other = swap(hidden(at, received, down_other, "hidden_other"))
    grad_mine = hidden(at, received, w_down, "hidden_own")
    mine = diffs(grad_mine, grad_other, gate_pre[0], up_pre[0])
    theirs = swap(mine)
    early = early_inputs(at, mine, w_gate, w_up)
    slots = inputs(at, mine, theirs, early, w_gate, w_up, gate_other, up_other)
    back = exchange(slots, groups)
    came = swap(combine_send(w, back))
    keep, weight_grad = combine_keep(at, ids_t, pa, pb, w, back)
    return join(at, keep, came), weight_grad.T


def solution(mesh):
    in_specs = (
        P(("expert", "seq"), None),
        P("expert", None),
        P("expert", None),
        P("expert", None, "seq"),
        P("expert", None, "seq"),
        P("expert", None, "seq"),
        P("expert", None, "seq"),
        P("expert", "seq", None),
    )
    out_specs = (P(("expert", "seq"), None), P(("expert", "seq"), None))
    return jax.shard_map(
        on_device, mesh=mesh, in_specs=in_specs, out_specs=out_specs, check_vma=False
    )
```

```python
import jax
import jax.numpy as jnp
from jax import lax
from jax.experimental import pallas as pl
from jax.experimental.pallas import tpu as pltpu
from jax.sharding import PartitionSpec as P

F32 = jnp.float32
BF16 = jnp.bfloat16
NT = (((1,), (1,)), ((), ()))
MAIN = 8
REST = 4
MIB = 1024 * 1024
LIMIT = 14 * MIB
TILE = 256
EARLY = 2


def iota(shape, dim):
    return lax.broadcasted_iota(jnp.int32, shape, dim)


def flag(cond):
    return jnp.where(cond, 1.0, 0.0).astype(F32)


def dot(a, b):
    return jnp.dot(a, b, preferred_element_type=F32)


def params(limit=LIMIT):
    return pltpu.CompilerParams(vmem_limit_bytes=limit)


def in_hbm(*values):
    return [pltpu.with_memory_space_constraint(v, pltpu.HBM) for v in values]


def swap(value):
    return lax.ppermute(value, "seq", [(0, 1), (1, 0)])


def actual(index, at, half):
    return (index + half * at) % (2 * half)


def routes_kernel(at_ref, own_ids, other_ids, own_weights, other_weights, pa_ref, pb_ref, w_ref):
    at = at_ref[0]
    ids = jnp.concatenate([own_ids[...], other_ids[...]], axis=1)
    weights = jnp.concatenate([own_weights[...], other_weights[...]], axis=1)
    topk, tokens = ids.shape
    rows = pa_ref.shape[0]
    experts = rows // MAIN
    names = iota((experts, tokens), 0)
    member = jnp.zeros((experts, tokens), F32)
    gate = jnp.zeros((experts, tokens), F32)
    for k in range(topk):
        hit = names == ids[k : k + 1, :]
        member = member + flag(hit)
        gate = gate + jnp.where(hit, weights[k : k + 1, :], 0.0)
    first = actual(iota((tokens, tokens), 0), at, tokens // 2)
    before = flag(first < actual(iota((tokens, tokens), 1), at, tokens // 2)).astype(BF16)
    place = dot(member.astype(BF16), before)
    place = jnp.where(member > 0.5, place, -1.0).astype(BF16)
    spread = flag(iota((rows, experts), 0) // MAIN == iota((rows, experts), 1)).astype(BF16)
    wide = dot(spread, place).astype(jnp.int32)
    row = iota((rows, tokens), 0)
    pa_ref[...] = flag(wide == row % MAIN).astype(BF16)
    rest = flag(wide == MAIN + row % REST)
    upper = (row // REST) % 2
    pb_ref[:, :tokens] = jnp.where(upper == 0, rest, 0.0).astype(BF16)
    pb_ref[:, tokens:] = jnp.where(upper == 1, rest, 0.0).astype(BF16)

    def by_token(value):
        return lax.dot_general(value, spread, (((0,), (1,)), ((), ())), preferred_element_type=F32)

    wide = by_token(place).astype(jnp.int32)
    lane = iota((tokens, rows), 1)
    in_rest = wide == MAIN + lane % REST
    upper = (lane // REST) % 2
    gate = by_token(gate.astype(BF16))
    masks = (wide == lane % MAIN, in_rest & (upper == 0), in_rest & (upper == 1))
    for at_mask, mask in enumerate(masks):
        low = at_mask * tokens
        w_ref[low : low + tokens, :] = jnp.where(mask, gate, 0.0).astype(BF16)


def routes(at, ids_t, weights_t, experts):
    topk, tokens = ids_t.shape
    half = tokens // 2
    rows = experts * MAIN
    own = pl.BlockSpec((topk, half), lambda j, at: (0, at[0]))
    other = pl.BlockSpec((topk, half), lambda j, at: (0, 1 - at[0]))
    shapes = [(rows, tokens), (rows, 2 * tokens), (3 * tokens, rows)]
    return pl.pallas_call(
        routes_kernel,
        grid_spec=pltpu.PrefetchScalarGridSpec(
            num_scalar_prefetch=1,
            grid=(1,),
            in_specs=[own, other, own, other],
            out_specs=[pl.BlockSpec(shape, lambda j, at: (0, 0)) for shape in shapes],
        ),
        out_shape=[jax.ShapeDtypeStruct(shape, BF16) for shape in shapes],
        compiler_params=params(),
        cost_estimate=pl.CostEstimate(flops=10**9, bytes_accessed=10**6, transcendentals=0),
        name="routes",
    )(at, ids_t, ids_t, weights_t, weights_t)


def dispatch_kernel(at_ref, pa_ref, pb_ref, own_ref, other_ref, out_ref):
    step = pl.program_id(0)
    part = other_ref.shape[1]
    tile = part // 4
    cols = pl.ds(pl.multiple_of(step * tile, 128), tile)

    def tokens(index):
        own = pl.ds(pl.multiple_of(at_ref[0] * part + index * tile, 128), tile)
        other = pl.ds(pl.multiple_of(index * tile, 128), tile)
        return [own_ref[:, own], other_ref[:, other]]

    @pl.when(step < 4)
    def _():
        out_ref[:, cols] = dot(pa_ref[...], jnp.concatenate(tokens(step), axis=0)).astype(BF16)

    @pl.when(step >= 4)
    def _():
        both = jnp.concatenate(tokens(step - 4) + tokens(step - 2), axis=0)
        out_ref[:, cols] = dot(pb_ref[...], both).astype(BF16)


def dispatch(at, pa, pb, out_grad, other):
    rows = pa.shape[0]
    whole = pl.BlockSpec(memory_space=pltpu.VMEM)
    return pl.pallas_call(
        dispatch_kernel,
        grid_spec=pltpu.PrefetchScalarGridSpec(
            num_scalar_prefetch=1,
            grid=(6,),
            in_specs=[whole] * 4,
            out_specs=whole,
        ),
        out_shape=jax.ShapeDtypeStruct((rows, other.shape[1] // 2 * 3), BF16),
        compiler_params=params(),
        cost_estimate=pl.CostEstimate(flops=2 * 10**9, bytes_accessed=8 * 10**6, transcendentals=0),
        name="dispatch",
    )(at, pa, pb, out_grad, other)


def hidden_kernel(at_ref, x_ref, w_ref, out_ref):
    step = pl.program_id(0)
    main = x_ref.shape[0]
    units = out_ref.shape[1]
    part = w_ref.shape[1] // 2
    quarter = part // 2

    def product(low, high, start):
        rows = pl.ds(pl.multiple_of(step * units, units), units)
        cols = pl.ds(pl.multiple_of(at_ref[0] * part + start, 128), high - low)
        return lax.dot_general(x_ref[:, low:high], w_ref[rows, cols], NT, preferred_element_type=F32)

    pairs = main // 16
    first = product(0, part, 0).reshape(pairs, 2, 8, units)
    low = product(part, part + quarter, 0).reshape(pairs, 2, 8, units)
    high = product(part, part + quarter, quarter).reshape(pairs, 2, 8, units)
    top = iota((pairs, 8, units), 1) < REST
    even = low[:, 0] + pltpu.roll(high[:, 0], REST, 1)
    odd = high[:, 1] + pltpu.roll(low[:, 1], REST, 1)
    turned = pltpu.roll(first[:, 1], REST, 1)
    out_ref[...] = jnp.stack(
        [first[:, 0], jnp.where(top, even, turned), jnp.where(top, turned, odd)], axis=1
    ).reshape(main // 2 * 3, units)


def hidden(at, x, w, name):
    rows, lanes = x.shape
    units = w.shape[0]
    tile = 256
    whole = pl.BlockSpec(memory_space=pltpu.VMEM)
    return pl.pallas_call(
        hidden_kernel,
        grid_spec=pltpu.PrefetchScalarGridSpec(
            num_scalar_prefetch=1,
            grid=(units // tile,),
            in_specs=[whole, whole],
            out_specs=pl.BlockSpec((rows // 2 * 3, tile), lambda j, at: (0, j)),
        ),
        out_shape=jax.ShapeDtypeStruct((rows // 2 * 3, units), F32),
        compiler_params=params(),
        cost_estimate=pl.CostEstimate(flops=0, bytes_accessed=0, transcendentals=0),
        name=name,
    )(at, x, w)


def diff_kernel(mine_ref, other_ref, gate_ref, up_ref, out_ref):
    units = mine_ref.shape[1]
    rows = pl.ds(pl.multiple_of(pl.program_id(0) * TILE, TILE), TILE)
    grad = mine_ref[rows, :] + other_ref[rows, :]
    value = gate_ref[rows, :].astype(F32)
    up = up_ref[rows, :].astype(F32)
    sigma = jax.nn.sigmoid(value)
    active = value * sigma
    slope = sigma * (1.0 + value * (1.0 - sigma))
    through = grad * active
    score = jnp.sum(through * up, axis=1, keepdims=True)
    out_ref[rows, :units] = (grad * up * slope).astype(BF16)
    out_ref[rows, units : 2 * units] = through.astype(BF16)
    out_ref[rows, 2 * units :] = jnp.broadcast_to(score, (TILE, 128)).astype(BF16)


def diffs(mine, other, gate, up):
    rows, units = mine.shape
    whole = pl.BlockSpec(memory_space=pltpu.VMEM)
    return pl.pallas_call(
        diff_kernel,
        grid=(rows // TILE,),
        in_specs=[whole] * 4,
        out_specs=whole,
        out_shape=jax.ShapeDtypeStruct((rows, 2 * units + 128), BF16),
        compiler_params=params(),
        cost_estimate=pl.CostEstimate(flops=0, bytes_accessed=0, transcendentals=0),
        name="diffs",
    )(mine, other, gate, up)


def parts_of(value):
    rows, lanes = value.shape
    pairs = rows // 24
    value = value.reshape(pairs, 3, 8, lanes)
    top = iota((pairs, 8, lanes), 1) < REST
    odd = jnp.where(top, pltpu.roll(value[:, 1], REST, 1), pltpu.roll(value[:, 2], REST, 1))
    main = jnp.stack([value[:, 0], odd], axis=1).reshape(16 * pairs, lanes)
    return main, value[:, 1], value[:, 2]


def both_quarters(low, high):
    top = iota(low[1].shape, 1) < REST
    even = jnp.where(top, low[1], pltpu.roll(high[1], REST, 1))
    odd = jnp.where(top, pltpu.roll(low[2], REST, 1), high[2])
    return jnp.stack([even, odd], axis=1).reshape(low[0].shape)


def own_block(units, steps, shift):
    return pl.BlockSpec((TILE, units), lambda j, at: (at[0] * 2 * steps + shift * steps + j, 0))


def early_kernel(at_ref, mine_ref, g0, g1, u0, u1, out_ref):
    units = g0.shape[1]
    w = jnp.concatenate(
        [
            jnp.concatenate([g0[...], u0[...]], axis=1),
            jnp.concatenate([g1[...], u1[...]], axis=1),
        ],
        axis=0,
    )
    cols = pl.ds(pl.multiple_of(pl.program_id(0) * 2 * TILE, TILE), 2 * TILE)
    out_ref[:, cols] = lax.dot_general(mine_ref[:, : 2 * units], w, NT, preferred_element_type=F32)


def early_inputs(at, mine, w_gate, w_up):
    w_gate, w_up = in_hbm(w_gate, w_up)
    rows = mine.shape[0]
    units = w_gate.shape[1]
    steps = w_gate.shape[0] // 4 // TILE
    whole = pl.BlockSpec(memory_space=pltpu.VMEM)
    blocks = [own_block(units, steps, 0), own_block(units, steps, 1)]
    return pl.pallas_call(
        early_kernel,
        grid_spec=pltpu.PrefetchScalarGridSpec(
            num_scalar_prefetch=1,
            grid=(EARLY,),
            in_specs=[whole] + blocks + blocks,
            out_specs=whole,
        ),
        out_shape=jax.ShapeDtypeStruct((rows, EARLY * 2 * TILE), F32),
        compiler_params=params(),
        cost_estimate=pl.CostEstimate(
            flops=8 * EARLY * rows * TILE * units, bytes_accessed=10**7, transcendentals=0
        ),
        name="early_inputs",
    )(at, mine, w_gate, w_gate, w_up, w_up)


def inputs_kernel(
    at_ref, mine_ref, other_ref, early_ref, g0, g1, u0, u1, og_ref, ou_ref, out_ref, sum_ref
):
    step = pl.program_id(0)
    last = pl.num_programs(0) - 1
    units = g0.shape[1]
    quarter = last * TILE

    def at_cols(tile, start):
        return pl.ds(pl.multiple_of(start + tile * TILE, TILE), TILE)

    def far(start):
        rows = at_cols(step, 2 * quarter * at_ref[0] + start)
        return [og_ref[rows, :], ou_ref[rows, :]]

    def product(x, low, high):
        w = jnp.concatenate(
            [jnp.concatenate(low, axis=1), jnp.concatenate(high, axis=1)], axis=0
        )
        return lax.dot_general(x, w, NT, preferred_element_type=F32)

    def early():
        cols = pl.ds(pl.multiple_of(step * 2 * TILE, TILE), 2 * TILE)
        far_terms = product(other_ref[:, : 2 * units], far(0), far(quarter))
        sum_ref[step % 2] = far_terms + early_ref[:, cols]

    def full():
        x = jnp.concatenate([mine_ref[:, : 2 * units], other_ref[:, : 2 * units]], axis=1)
        low = [g0[...], u0[...]] + far(0)
        high = [g1[...], u1[...]] + far(quarter)
        sum_ref[step % 2] = product(x, low, high)

    def finish():
        tile = step - 1
        result = sum_ref[tile % 2]
        low = parts_of(result[:, :TILE])
        high = parts_of(result[:, TILE:])
        out_ref[:, at_cols(tile, 0)] = low[0].astype(BF16)
        out_ref[:, at_cols(tile, quarter)] = high[0].astype(BF16)
        out_ref[:, at_cols(tile, 2 * quarter)] = both_quarters(low, high).astype(BF16)

    @pl.when(step == 0)
    def _():
        early()
        score = mine_ref[:, 2 * units :].astype(F32) + other_ref[:, 2 * units :].astype(F32)
        score = parts_of(score)
        lane = iota(score[0].shape, 1)
        end = out_ref.shape[1] - 128
        out_ref[:, end:] = jnp.where(lane == 0, score[0], both_quarters(score, score)).astype(BF16)

    @pl.when((step > 0) & (step < EARLY))
    def _():
        finish()
        early()

    @pl.when((step >= EARLY) & (step < last))
    def _():
        finish()
        full()

    @pl.when(step == last)
    def _():
        finish()


def inputs(at, mine, other, early, w_gate, w_up, gate_other, up_other):
    w_gate, w_up = in_hbm(w_gate, w_up)
    rows, lanes = mine.shape
    units = w_gate.shape[1]
    part = w_gate.shape[0] // 2
    steps = part // 2 // TILE
    main = rows // 3 * 2

    def block(shift):
        return pl.BlockSpec(
            (TILE, units),
            lambda j, at: (at[0] * 2 * steps + shift * steps + jnp.clip(j, EARLY, steps - 1), 0),
        )

    whole = pl.BlockSpec(memory_space=pltpu.VMEM)
    return pl.pallas_call(
        inputs_kernel,
        grid_spec=pltpu.PrefetchScalarGridSpec(
            num_scalar_prefetch=1,
            grid=(steps + 1,),
            in_specs=[whole] * 3 + [block(0), block(1), block(0), block(1), whole, whole],
            out_specs=whole,
            scratch_shapes=[pltpu.VMEM((2, rows, 2 * TILE), F32)],
        ),
        out_shape=jax.ShapeDtypeStruct((main, 3 * TILE * steps + 128), BF16),
        compiler_params=params(),
        cost_estimate=pl.CostEstimate(
            flops=8 * rows * part * units, bytes_accessed=24 * 10**6, transcendentals=0
        ),
        name="inputs",
    )(at, mine, other, early, w_gate, w_gate, w_up, w_up, gate_other, up_other)


def tokens_of(w_ref, back_ref, out_ref, first):
    step = pl.program_id(0)
    half, tile = out_ref.shape
    tokens = 2 * half
    low = pl.ds(pl.multiple_of(step * tile, 128), tile)
    rest = pl.ds(pl.multiple_of((4 + step % 2) * tile, 128), tile)
    part = pl.ds(pl.multiple_of((1 + step // 2) * tokens + first, half), half)
    slots = jnp.concatenate([back_ref[:, low], back_ref[:, rest]], axis=0)
    w = jnp.concatenate([w_ref[first : first + half, :], w_ref[part, :]], axis=1)
    out_ref[...] = dot(w, slots).astype(BF16)


def send_kernel(w_ref, back_ref, send_ref):
    tokens_of(w_ref, back_ref, send_ref, send_ref.shape[0])


def combine_send(w, back):
    half = w.shape[0] // 6
    tile = (back.shape[1] - 128) // 6
    whole = pl.BlockSpec(memory_space=pltpu.VMEM)
    return pl.pallas_call(
        send_kernel,
        grid=(4,),
        in_specs=[whole, whole],
        out_specs=pl.BlockSpec((half, tile), lambda j: (0, j)),
        out_shape=jax.ShapeDtypeStruct((half, 4 * tile), BF16),
        compiler_params=params(),
        cost_estimate=pl.CostEstimate(flops=10**9, bytes_accessed=7 * 10**6, transcendentals=0),
        name="combine_send",
    )(w, back)


def keep_kernel(at_ref, ids_ref, pa_ref, pb_ref, w_ref, back_ref, keep_ref, grad_ref):
    topk, half = ids_ref.shape
    rows = back_ref.shape[0]
    experts = rows // MAIN

    @pl.when(pl.program_id(0) == 0)
    def _():
        block = iota((rows, experts), 0) // MAIN == iota((rows, experts), 1)
        score = back_ref[:, back_ref.shape[1] - 128 :].astype(F32)

        def one(column, slots):
            value = jnp.where(block, column, 0.0).astype(BF16)
            return lax.dot_general(value, slots, (((0,), (0,)), ((), ())), preferred_element_type=F32)

        table = one(score[:, 0:1], pa_ref[...]) + one(score[:, 1:2], pb_ref[...])
        names = iota((experts, half), 0)
        row = iota((topk, half), 0)
        ids = ids_ref[...]
        result = jnp.zeros((topk, half), F32)
        for k in range(topk):
            hit = names == ids[k : k + 1, :]
            picked = jnp.sum(jnp.where(hit, table, 0.0), axis=0, keepdims=True)
            result = result + jnp.where(row == k, picked, 0.0)
        grad_ref[...] = result.astype(BF16)

    tokens_of(w_ref, back_ref, keep_ref, 0)


def combine_keep(at, ids_t, pa, pb, w, back):
    topk, tokens = ids_t.shape
    half = tokens // 2
    rows, lanes = back.shape
    tile = (lanes - 128) // 6
    whole = pl.BlockSpec(memory_space=pltpu.VMEM)
    return pl.pallas_call(
        keep_kernel,
        grid_spec=pltpu.PrefetchScalarGridSpec(
            num_scalar_prefetch=1,
            grid=(4,),
            in_specs=[
                pl.BlockSpec((topk, half), lambda j, at: (0, at[0])),
                pl.BlockSpec((rows, half), lambda j, at: (0, 0)),
                pl.BlockSpec((rows, half), lambda j, at: (0, 0)),
                whole,
                whole,
            ],
            out_specs=[
                pl.BlockSpec((half, tile), lambda j, at: (0, 4 * at[0] + j)),
                pl.BlockSpec((topk, half), lambda j, at: (0, 0)),
            ],
        ),
        out_shape=[
            jax.ShapeDtypeStruct((half, 8 * tile), BF16),
            jax.ShapeDtypeStruct((topk, half), BF16),
        ],
        compiler_params=params(),
        cost_estimate=pl.CostEstimate(flops=10**9, bytes_accessed=7 * 10**6, transcendentals=0),
        name="combine_keep",
    )(at, ids_t, pa, pb, w, back)


def join_kernel(at_ref, base_ref, came_ref, out_ref):
    out_ref[...] = came_ref[...]


def join(at, base, came):
    half, part = came.shape
    return pl.pallas_call(
        join_kernel,
        grid_spec=pltpu.PrefetchScalarGridSpec(
            num_scalar_prefetch=1,
            grid=(2,),
            in_specs=[
                pl.BlockSpec(memory_space=pl.ANY),
                pl.BlockSpec((half, part // 2), lambda j, at: (0, j)),
            ],
            out_specs=pl.BlockSpec((half, part // 2), lambda j, at: (0, 2 * (1 - at[0]) + j)),
        ),
        out_shape=jax.ShapeDtypeStruct(base.shape, BF16),
        input_output_aliases={1: 0},
        compiler_params=params(),
        cost_estimate=pl.CostEstimate(flops=0, bytes_accessed=2 * 10**6, transcendentals=0),
        name="join",
    )(at, base, came)


def exchange(value, groups):
    rows, lanes = value.shape
    value = lax.all_to_all(
        value.reshape(groups, MAIN, lanes), "expert", split_axis=0, concat_axis=0, tiled=True
    )
    return value.reshape(rows, lanes)


def on_device(out_grad, route_ids, route_weights, gate_pre, up_pre, w_gate, w_up, w_down):
    groups = lax.axis_size("expert")
    seq_at = lax.axis_index("seq")
    at = seq_at.astype(jnp.int32).reshape(1)
    part = out_grad.shape[1] // 2
    w_gate, w_up, w_down = w_gate[0], w_up[0], w_down[0]
    other = swap(lax.dynamic_slice_in_dim(out_grad, (1 - seq_at) * part, part, 1))
    ids_t = route_ids.T
    pa, pb, w = routes(at, ids_t, route_weights.T, groups)
    sent = dispatch(at, pa, pb, out_grad, other)
    w_gate, w_up, w_down, sent = lax.optimization_barrier((w_gate, w_up, w_down, sent))
    down_other, gate_other, up_other = swap(w_down), swap(w_gate), swap(w_up)
    received = exchange(sent, groups)
    received, down_other, gate_other, up_other = lax.optimization_barrier(
        (received, down_other, gate_other, up_other)
    )
    grad_other = swap(hidden(at, received, down_other, "hidden_other"))
    grad_mine = hidden(at, received, w_down, "hidden_own")
    mine = diffs(grad_mine, grad_other, gate_pre[0], up_pre[0])
    theirs = swap(mine)
    early = early_inputs(at, mine, w_gate, w_up)
    slots = inputs(at, mine, theirs, early, w_gate, w_up, gate_other, up_other)
    back = exchange(slots, groups)
    came = swap(combine_send(w, back))
    keep, weight_grad = combine_keep(at, ids_t, pa, pb, w, back)
    return join(at, keep, came), weight_grad.T


def solution(mesh):
    in_specs = (
        P(("expert", "seq"), None),
        P("expert", None),
        P("expert", None),
        P("expert", None, "seq"),
        P("expert", None, "seq"),
        P("expert", None, "seq"),
        P("expert", None, "seq"),
        P("expert", "seq", None),
    )
    out_specs = (P(("expert", "seq"), None), P(("expert", "seq"), None))
    return jax.shard_map(
        on_device, mesh=mesh, in_specs=in_specs, out_specs=out_specs, check_vma=False
    )
```

```python
import jax
import jax.numpy as jnp
from jax import lax
from jax.experimental import pallas as pl
from jax.experimental.pallas import tpu as pltpu
from jax.sharding import PartitionSpec as P

F32 = jnp.float32
BF16 = jnp.bfloat16
NT = (((1,), (1,)), ((), ()))
MAIN = 8
REST = 4
MIB = 1024 * 1024
LIMIT = 14 * MIB
TILE = 256
EARLY = 2


def iota(shape, dim):
    return lax.broadcasted_iota(jnp.int32, shape, dim)


def flag(cond):
    return jnp.where(cond, 1.0, 0.0).astype(F32)


def dot(a, b):
    return jnp.dot(a, b, preferred_element_type=F32)


def params(limit=LIMIT):
    return pltpu.CompilerParams(vmem_limit_bytes=limit)


def in_hbm(*values):
    return [pltpu.with_memory_space_constraint(v, pltpu.HBM) for v in values]


def swap(value):
    return lax.ppermute(value, "seq", [(0, 1), (1, 0)])


def actual(index, at, half):
    return (index + half * at) % (2 * half)


def routes_kernel(at_ref, own_ids, other_ids, own_weights, other_weights, pa_ref, pb_ref, w_ref):
    at = at_ref[0]
    ids = jnp.concatenate([own_ids[...], other_ids[...]], axis=1)
    weights = jnp.concatenate([own_weights[...], other_weights[...]], axis=1)
    topk, tokens = ids.shape
    rows = pa_ref.shape[0]
    experts = rows // MAIN
    names = iota((experts, tokens), 0)
    member = jnp.zeros((experts, tokens), F32)
    gate = jnp.zeros((experts, tokens), F32)
    for k in range(topk):
        hit = names == ids[k : k + 1, :]
        member = member + flag(hit)
        gate = gate + jnp.where(hit, weights[k : k + 1, :], 0.0)
    first = actual(iota((tokens, tokens), 0), at, tokens // 2)
    before = flag(first < actual(iota((tokens, tokens), 1), at, tokens // 2)).astype(BF16)
    place = dot(member.astype(BF16), before)
    place = jnp.where(member > 0.5, place, -1.0).astype(BF16)
    spread = flag(iota((rows, experts), 0) // MAIN == iota((rows, experts), 1)).astype(BF16)
    wide = dot(spread, place).astype(jnp.int32)
    row = iota((rows, tokens), 0)
    pa_ref[...] = flag(wide == row % MAIN).astype(BF16)
    rest = flag(wide == MAIN + row % REST)
    upper = (row // REST) % 2
    pb_ref[:, :tokens] = jnp.where(upper == 0, rest, 0.0).astype(BF16)
    pb_ref[:, tokens:] = jnp.where(upper == 1, rest, 0.0).astype(BF16)

    def by_token(value):
        return lax.dot_general(value, spread, (((0,), (1,)), ((), ())), preferred_element_type=F32)

    wide = by_token(place).astype(jnp.int32)
    lane = iota((tokens, rows), 1)
    in_rest = wide == MAIN + lane % REST
    upper = (lane // REST) % 2
    gate = by_token(gate.astype(BF16))
    masks = (wide == lane % MAIN, in_rest & (upper == 0), in_rest & (upper == 1))
    for at_mask, mask in enumerate(masks):
        low = at_mask * tokens
        w_ref[low : low + tokens, :] = jnp.where(mask, gate, 0.0).astype(BF16)


def routes(at, ids_t, weights_t, experts):
    topk, tokens = ids_t.shape
    half = tokens // 2
    rows = experts * MAIN
    own = pl.BlockSpec((topk, half), lambda j, at: (0, at[0]))
    other = pl.BlockSpec((topk, half), lambda j, at: (0, 1 - at[0]))
    shapes = [(rows, tokens), (rows, 2 * tokens), (3 * tokens, rows)]
    return pl.pallas_call(
        routes_kernel,
        grid_spec=pltpu.PrefetchScalarGridSpec(
            num_scalar_prefetch=1,
            grid=(1,),
            in_specs=[own, other, own, other],
            out_specs=[pl.BlockSpec(shape, lambda j, at: (0, 0)) for shape in shapes],
        ),
        out_shape=[jax.ShapeDtypeStruct(shape, BF16) for shape in shapes],
        compiler_params=params(),
        cost_estimate=pl.CostEstimate(flops=10**9, bytes_accessed=10**6, transcendentals=0),
        name="routes",
    )(at, ids_t, ids_t, weights_t, weights_t)


def dispatch_kernel(at_ref, pa_ref, pb_ref, own_ref, other_ref, out_ref):
    step = pl.program_id(0)
    part = other_ref.shape[1]
    tile = part // 4
    cols = pl.ds(pl.multiple_of(step * tile, 128), tile)

    def tokens(index):
        own = pl.ds(pl.multiple_of(at_ref[0] * part + index * tile, 128), tile)
        other = pl.ds(pl.multiple_of(index * tile, 128), tile)
        return [own_ref[:, own], other_ref[:, other]]

    @pl.when(step < 4)
    def _():
        out_ref[:, cols] = dot(pa_ref[...], jnp.concatenate(tokens(step), axis=0)).astype(BF16)

    @pl.when(step >= 4)
    def _():
        both = jnp.concatenate(tokens(step - 4) + tokens(step - 2), axis=0)
        out_ref[:, cols] = dot(pb_ref[...], both).astype(BF16)


def dispatch(at, pa, pb, out_grad, other):
    rows = pa.shape[0]
    whole = pl.BlockSpec(memory_space=pltpu.VMEM)
    return pl.pallas_call(
        dispatch_kernel,
        grid_spec=pltpu.PrefetchScalarGridSpec(
            num_scalar_prefetch=1,
            grid=(6,),
            in_specs=[whole] * 4,
            out_specs=whole,
        ),
        out_shape=jax.ShapeDtypeStruct((rows, other.shape[1] // 2 * 3), BF16),
        compiler_params=params(),
        cost_estimate=pl.CostEstimate(flops=2 * 10**9, bytes_accessed=8 * 10**6, transcendentals=0),
        name="dispatch",
    )(at, pa, pb, out_grad, other)


def hidden_kernel(at_ref, x_ref, w_ref, out_ref):
    step = pl.program_id(0)
    main = x_ref.shape[0]
    units = out_ref.shape[1]
    part = w_ref.shape[1] // 2
    quarter = part // 2

    def product(low, high, start):
        rows = pl.ds(pl.multiple_of(step * units, units), units)
        cols = pl.ds(pl.multiple_of(at_ref[0] * part + start, 128), high - low)
        return lax.dot_general(x_ref[:, low:high], w_ref[rows, cols], NT, preferred_element_type=F32)

    pairs = main // 16
    first = product(0, part, 0).reshape(pairs, 2, 8, units)
    low = product(part, part + quarter, 0).reshape(pairs, 2, 8, units)
    high = product(part, part + quarter, quarter).reshape(pairs, 2, 8, units)
    top = iota((pairs, 8, units), 1) < REST
    even = low[:, 0] + pltpu.roll(high[:, 0], REST, 1)
    odd = high[:, 1] + pltpu.roll(low[:, 1], REST, 1)
    turned = pltpu.roll(first[:, 1], REST, 1)
    out_ref[...] = jnp.stack(
        [first[:, 0], jnp.where(top, even, turned), jnp.where(top, turned, odd)], axis=1
    ).reshape(main // 2 * 3, units)


def hidden(at, x, w, name):
    rows, lanes = x.shape
    units = w.shape[0]
    tile = 256
    whole = pl.BlockSpec(memory_space=pltpu.VMEM)
    return pl.pallas_call(
        hidden_kernel,
        grid_spec=pltpu.PrefetchScalarGridSpec(
            num_scalar_prefetch=1,
            grid=(units // tile,),
            in_specs=[whole, whole],
            out_specs=pl.BlockSpec((rows // 2 * 3, tile), lambda j, at: (0, j)),
        ),
        out_shape=jax.ShapeDtypeStruct((rows // 2 * 3, units), F32),
        compiler_params=params(),
        cost_estimate=pl.CostEstimate(flops=0, bytes_accessed=0, transcendentals=0),
        name=name,
    )(at, x, w)


def diff_kernel(mine_ref, other_ref, gate_ref, up_ref, out_ref):
    step = pl.program_id(0)
    total, units = mine_ref.shape
    count = total // pl.num_programs(0)
    pairs = count // 24
    rows = pl.ds(pl.multiple_of(step * count, count), count)
    main_rows = pl.ds(pl.multiple_of(step * 16 * pairs, 16 * pairs), 16 * pairs)
    rest_rows = pl.ds(pl.multiple_of(total // 3 * 2 + step * 8 * pairs, 8 * pairs), 8 * pairs)

    def put(value, low):
        lanes = value.shape[1]
        value = value.reshape(pairs, 3, 8, lanes)
        top = iota((pairs, 8, lanes), 1) < REST
        odd = jnp.where(top, pltpu.roll(value[:, 1], REST, 1), pltpu.roll(value[:, 2], REST, 1))
        main = jnp.stack([value[:, 0], odd], axis=1).reshape(16 * pairs, lanes)
        rest = jnp.where(top, value[:, 1], value[:, 2]).reshape(8 * pairs, lanes)
        out_ref[main_rows, low : low + lanes] = main.astype(BF16)
        out_ref[rest_rows, low : low + lanes] = rest.astype(BF16)

    grad = mine_ref[rows, :] + other_ref[rows, :]
    value = gate_ref[rows, :].astype(F32)
    up = up_ref[rows, :].astype(F32)
    sigma = jax.nn.sigmoid(value)
    active = value * sigma
    slope = sigma * (1.0 + value * (1.0 - sigma))
    through = grad * active
    score = jnp.sum(through * up, axis=1, keepdims=True)
    put(grad * up * slope, 0)
    put(through, units)
    put(jnp.broadcast_to(score, (count, 128)), 2 * units)


def diffs(mine, other, gate, up):
    rows, units = mine.shape
    whole = pl.BlockSpec(memory_space=pltpu.VMEM)
    return pl.pallas_call(
        diff_kernel,
        grid=(2,),
        in_specs=[whole] * 4,
        out_specs=whole,
        out_shape=jax.ShapeDtypeStruct((rows, 2 * units + 128), BF16),
        compiler_params=params(),
        cost_estimate=pl.CostEstimate(flops=0, bytes_accessed=0, transcendentals=0),
        name="diffs",
    )(mine, other, gate, up)


def spread_rows(low, high):
    rows, lanes = low.shape
    pairs = rows // 8
    low = low.reshape(pairs, 8, lanes)
    high = high.reshape(pairs, 8, lanes)
    top = iota((pairs, 8, lanes), 1) < REST
    even = jnp.where(top, low, pltpu.roll(high, REST, 1))
    odd = jnp.where(top, pltpu.roll(low, REST, 1), high)
    return jnp.stack([even, odd], axis=1).reshape(2 * rows, lanes)


def own_block(units, steps, shift):
    return pl.BlockSpec((TILE, units), lambda j, at: (at[0] * 2 * steps + shift * steps + j, 0))


def early_kernel(at_ref, mine_ref, g0, g1, u0, u1, out_ref):
    units = g0.shape[1]
    w = jnp.concatenate(
        [
            jnp.concatenate([g0[...], u0[...]], axis=1),
            jnp.concatenate([g1[...], u1[...]], axis=1),
        ],
        axis=0,
    )
    cols = pl.ds(pl.multiple_of(pl.program_id(0) * 2 * TILE, TILE), 2 * TILE)
    out_ref[:, cols] = lax.dot_general(mine_ref[:, : 2 * units], w, NT, preferred_element_type=F32)


def early_inputs(at, mine, w_gate, w_up):
    w_gate, w_up = in_hbm(w_gate, w_up)
    rows = mine.shape[0]
    units = w_gate.shape[1]
    steps = w_gate.shape[0] // 4 // TILE
    whole = pl.BlockSpec(memory_space=pltpu.VMEM)
    blocks = [own_block(units, steps, 0), own_block(units, steps, 1)]
    return pl.pallas_call(
        early_kernel,
        grid_spec=pltpu.PrefetchScalarGridSpec(
            num_scalar_prefetch=1,
            grid=(EARLY,),
            in_specs=[whole] + blocks + blocks,
            out_specs=whole,
        ),
        out_shape=jax.ShapeDtypeStruct((rows, EARLY * 2 * TILE), F32),
        compiler_params=params(),
        cost_estimate=pl.CostEstimate(
            flops=8 * EARLY * rows * TILE * units, bytes_accessed=10**7, transcendentals=0
        ),
        name="early_inputs",
    )(at, mine, w_gate, w_gate, w_up, w_up)


def inputs_kernel(
    at_ref, mine_ref, other_ref, early_ref, g0, g1, u0, u1, og_ref, ou_ref, out_ref
):
    step = pl.program_id(0)
    units = g0.shape[1]
    main = out_ref.shape[0]
    quarter = pl.num_programs(0) * TILE

    def at_cols(start):
        return pl.ds(pl.multiple_of(start + step * TILE, TILE), TILE)

    def far(start):
        rows = at_cols(2 * quarter * at_ref[0] + start)
        return [og_ref[rows, :], ou_ref[rows, :]]

    def product(x, low, high):
        w = jnp.concatenate(
            [jnp.concatenate(low, axis=1), jnp.concatenate(high, axis=1)], axis=0
        )
        return lax.dot_general(x, w, NT, preferred_element_type=F32)

    def finish(result):
        out_ref[:, at_cols(0)] = result[:main, :TILE].astype(BF16)
        out_ref[:, at_cols(quarter)] = result[:main, TILE:].astype(BF16)
        rest = spread_rows(result[main:, :TILE], result[main:, TILE:])
        out_ref[:, at_cols(2 * quarter)] = rest.astype(BF16)

    @pl.when(step < EARLY)
    def _():
        cols = pl.ds(pl.multiple_of(step * 2 * TILE, TILE), 2 * TILE)
        finish(product(other_ref[:, : 2 * units], far(0), far(quarter)) + early_ref[:, cols])

    @pl.when(step >= EARLY)
    def _():
        x = jnp.concatenate([mine_ref[:, : 2 * units], other_ref[:, : 2 * units]], axis=1)
        low = [g0[...], u0[...]] + far(0)
        high = [g1[...], u1[...]] + far(quarter)
        finish(product(x, low, high))

    @pl.when(step == 0)
    def _():
        score = mine_ref[:, 2 * units :].astype(F32) + other_ref[:, 2 * units :].astype(F32)
        rest = spread_rows(score[main:], score[main:])
        lane = iota(rest.shape, 1)
        end = out_ref.shape[1] - 128
        out_ref[:, end:] = jnp.where(lane == 0, score[:main], rest).astype(BF16)


def inputs(at, mine, other, early, w_gate, w_up, gate_other, up_other):
    w_gate, w_up = in_hbm(w_gate, w_up)
    rows, lanes = mine.shape
    units = w_gate.shape[1]
    part = w_gate.shape[0] // 2
    steps = part // 2 // TILE
    main = rows // 3 * 2

    def block(shift):
        return pl.BlockSpec(
            (TILE, units),
            lambda j, at: (at[0] * 2 * steps + shift * steps + jnp.maximum(j, EARLY), 0),
        )

    whole = pl.BlockSpec(memory_space=pltpu.VMEM)
    return pl.pallas_call(
        inputs_kernel,
        grid_spec=pltpu.PrefetchScalarGridSpec(
            num_scalar_prefetch=1,
            grid=(steps,),
            in_specs=[whole] * 3 + [block(0), block(1), block(0), block(1), whole, whole],
            out_specs=whole,
        ),
        out_shape=jax.ShapeDtypeStruct((main, 3 * TILE * steps + 128), BF16),
        compiler_params=params(),
        cost_estimate=pl.CostEstimate(
            flops=8 * rows * part * units, bytes_accessed=24 * 10**6, transcendentals=0
        ),
        name="inputs",
    )(at, mine, other, early, w_gate, w_gate, w_up, w_up, gate_other, up_other)


def tokens_of(w_ref, back_ref, out_ref, first):
    step = pl.program_id(0)
    half, tile = out_ref.shape
    tokens = 2 * half
    low = pl.ds(pl.multiple_of(step * tile, 128), tile)
    rest = pl.ds(pl.multiple_of((4 + step % 2) * tile, 128), tile)
    part = pl.ds(pl.multiple_of((1 + step // 2) * tokens + first, half), half)
    slots = jnp.concatenate([back_ref[:, low], back_ref[:, rest]], axis=0)
    w = jnp.concatenate([w_ref[first : first + half, :], w_ref[part, :]], axis=1)
    out_ref[...] = dot(w, slots).astype(BF16)


def send_kernel(w_ref, back_ref, send_ref):
    tokens_of(w_ref, back_ref, send_ref, send_ref.shape[0])


def combine_send(w, back):
    half = w.shape[0] // 6
    tile = (back.shape[1] - 128) // 6
    whole = pl.BlockSpec(memory_space=pltpu.VMEM)
    return pl.pallas_call(
        send_kernel,
        grid=(4,),
        in_specs=[whole, whole],
        out_specs=pl.BlockSpec((half, tile), lambda j: (0, j)),
        out_shape=jax.ShapeDtypeStruct((half, 4 * tile), BF16),
        compiler_params=params(),
        cost_estimate=pl.CostEstimate(flops=10**9, bytes_accessed=7 * 10**6, transcendentals=0),
        name="combine_send",
    )(w, back)


def keep_kernel(at_ref, ids_ref, pa_ref, pb_ref, w_ref, back_ref, keep_ref, grad_ref):
    topk, half = ids_ref.shape
    rows = back_ref.shape[0]
    experts = rows // MAIN

    @pl.when(pl.program_id(0) == 0)
    def _():
        block = iota((rows, experts), 0) // MAIN == iota((rows, experts), 1)
        score = back_ref[:, back_ref.shape[1] - 128 :].astype(F32)

        def one(column, slots):
            value = jnp.where(block, column, 0.0).astype(BF16)
            return lax.dot_general(value, slots, (((0,), (0,)), ((), ())), preferred_element_type=F32)

        table = one(score[:, 0:1], pa_ref[...]) + one(score[:, 1:2], pb_ref[...])
        names = iota((experts, half), 0)
        row = iota((topk, half), 0)
        ids = ids_ref[...]
        result = jnp.zeros((topk, half), F32)
        for k in range(topk):
            hit = names == ids[k : k + 1, :]
            picked = jnp.sum(jnp.where(hit, table, 0.0), axis=0, keepdims=True)
            result = result + jnp.where(row == k, picked, 0.0)
        grad_ref[...] = result.astype(BF16)

    tokens_of(w_ref, back_ref, keep_ref, 0)


def combine_keep(at, ids_t, pa, pb, w, back):
    topk, tokens = ids_t.shape
    half = tokens // 2
    rows, lanes = back.shape
    tile = (lanes - 128) // 6
    whole = pl.BlockSpec(memory_space=pltpu.VMEM)
    return pl.pallas_call(
        keep_kernel,
        grid_spec=pltpu.PrefetchScalarGridSpec(
            num_scalar_prefetch=1,
            grid=(4,),
            in_specs=[
                pl.BlockSpec((topk, half), lambda j, at: (0, at[0])),
                pl.BlockSpec((rows, half), lambda j, at: (0, 0)),
                pl.BlockSpec((rows, half), lambda j, at: (0, 0)),
                whole,
                whole,
            ],
            out_specs=[
                pl.BlockSpec((half, tile), lambda j, at: (0, 4 * at[0] + j)),
                pl.BlockSpec((topk, half), lambda j, at: (0, 0)),
            ],
        ),
        out_shape=[
            jax.ShapeDtypeStruct((half, 8 * tile), BF16),
            jax.ShapeDtypeStruct((topk, half), BF16),
        ],
        compiler_params=params(),
        cost_estimate=pl.CostEstimate(flops=10**9, bytes_accessed=7 * 10**6, transcendentals=0),
        name="combine_keep",
    )(at, ids_t, pa, pb, w, back)


def join_kernel(at_ref, base_ref, came_ref, out_ref):
    out_ref[...] = came_ref[...]


def join(at, base, came):
    half, part = came.shape
    return pl.pallas_call(
        join_kernel,
        grid_spec=pltpu.PrefetchScalarGridSpec(
            num_scalar_prefetch=1,
            grid=(2,),
            in_specs=[
                pl.BlockSpec(memory_space=pl.ANY),
                pl.BlockSpec((half, part // 2), lambda j, at: (0, j)),
            ],
            out_specs=pl.BlockSpec((half, part // 2), lambda j, at: (0, 2 * (1 - at[0]) + j)),
        ),
        out_shape=jax.ShapeDtypeStruct(base.shape, BF16),
        input_output_aliases={1: 0},
        compiler_params=params(),
        cost_estimate=pl.CostEstimate(flops=0, bytes_accessed=2 * 10**6, transcendentals=0),
        name="join",
    )(at, base, came)


def exchange(value, groups):
    rows, lanes = value.shape
    value = lax.all_to_all(
        value.reshape(groups, MAIN, lanes), "expert", split_axis=0, concat_axis=0, tiled=True
    )
    return value.reshape(rows, lanes)


def on_device(out_grad, route_ids, route_weights, gate_pre, up_pre, w_gate, w_up, w_down):
    groups = lax.axis_size("expert")
    seq_at = lax.axis_index("seq")
    at = seq_at.astype(jnp.int32).reshape(1)
    part = out_grad.shape[1] // 2
    w_gate, w_up, w_down = w_gate[0], w_up[0], w_down[0]
    other = swap(lax.dynamic_slice_in_dim(out_grad, (1 - seq_at) * part, part, 1))
    ids_t = route_ids.T
    pa, pb, w = routes(at, ids_t, route_weights.T, groups)
    sent = dispatch(at, pa, pb, out_grad, other)
    w_gate, w_up, w_down, sent = lax.optimization_barrier((w_gate, w_up, w_down, sent))
    down_other, gate_other, up_other = swap(w_down), swap(w_gate), swap(w_up)
    received = exchange(sent, groups)
    received, down_other, gate_other, up_other = lax.optimization_barrier(
        (received, down_other, gate_other, up_other)
    )
    grad_other = swap(hidden(at, received, down_other, "hidden_other"))
    grad_mine = hidden(at, received, w_down, "hidden_own")
    mine = diffs(grad_mine, grad_other, gate_pre[0], up_pre[0])
    theirs = swap(mine)
    early = early_inputs(at, mine, w_gate, w_up)
    slots = inputs(at, mine, theirs, early, w_gate, w_up, gate_other, up_other)
    back = exchange(slots, groups)
    came = swap(combine_send(w, back))
    keep, weight_grad = combine_keep(at, ids_t, pa, pb, w, back)
    return join(at, keep, came), weight_grad.T


def solution(mesh):
    in_specs = (
        P(("expert", "seq"), None),
        P("expert", None),
        P("expert", None),
        P("expert", None, "seq"),
        P("expert", None, "seq"),
        P("expert", None, "seq"),
        P("expert", None, "seq"),
        P("expert", "seq", None),
    )
    out_specs = (P(("expert", "seq"), None), P(("expert", "seq"), None))
    return jax.shard_map(
        on_device, mesh=mesh, in_specs=in_specs, out_specs=out_specs, check_vma=False
    )
```

```python
import jax
import jax.numpy as jnp
from jax import lax
from jax.experimental import pallas as pl
from jax.experimental.pallas import tpu as pltpu
from jax.sharding import PartitionSpec as P

F32 = jnp.float32
BF16 = jnp.bfloat16
NT = (((1,), (1,)), ((), ()))
MAIN = 8
REST = 4
MIB = 1024 * 1024
LIMIT = 14 * MIB
TILE = 256
EARLY = 2


def iota(shape, dim):
    return lax.broadcasted_iota(jnp.int32, shape, dim)


def flag(cond):
    return jnp.where(cond, 1.0, 0.0).astype(F32)


def dot(a, b):
    return jnp.dot(a, b, preferred_element_type=F32)


def params(limit=LIMIT):
    return pltpu.CompilerParams(vmem_limit_bytes=limit)


def in_hbm(*values):
    return [pltpu.with_memory_space_constraint(v, pltpu.HBM) for v in values]


def swap(value):
    return lax.ppermute(value, "seq", [(0, 1), (1, 0)])


def actual(index, at, half):
    return (index + half * at) % (2 * half)


def routes_kernel(at_ref, own_ids, other_ids, own_weights, other_weights, pa_ref, pb_ref, w_ref):
    at = at_ref[0]
    ids = jnp.concatenate([own_ids[...], other_ids[...]], axis=1)
    weights = jnp.concatenate([own_weights[...], other_weights[...]], axis=1)
    topk, tokens = ids.shape
    rows = pa_ref.shape[0]
    experts = rows // MAIN
    names = iota((experts, tokens), 0)
    member = jnp.zeros((experts, tokens), F32)
    gate = jnp.zeros((experts, tokens), F32)
    for k in range(topk):
        hit = names == ids[k : k + 1, :]
        member = member + flag(hit)
        gate = gate + jnp.where(hit, weights[k : k + 1, :], 0.0)
    first = actual(iota((tokens, tokens), 0), at, tokens // 2)
    before = flag(first < actual(iota((tokens, tokens), 1), at, tokens // 2)).astype(BF16)
    place = dot(member.astype(BF16), before)
    place = jnp.where(member > 0.5, place, -1.0).astype(BF16)
    spread = flag(iota((rows, experts), 0) // MAIN == iota((rows, experts), 1)).astype(BF16)
    wide = dot(spread, place).astype(jnp.int32)
    row = iota((rows, tokens), 0)
    pa_ref[...] = flag(wide == row % MAIN).astype(BF16)
    rest = flag(wide == MAIN + row % REST)
    upper = (row // REST) % 2
    pb_ref[:, :tokens] = jnp.where(upper == 0, rest, 0.0).astype(BF16)
    pb_ref[:, tokens:] = jnp.where(upper == 1, rest, 0.0).astype(BF16)

    def by_token(value):
        return lax.dot_general(value, spread, (((0,), (1,)), ((), ())), preferred_element_type=F32)

    wide = by_token(place).astype(jnp.int32)
    lane = iota((tokens, rows), 1)
    in_rest = wide == MAIN + lane % REST
    upper = (lane // REST) % 2
    gate = by_token(gate.astype(BF16))
    masks = (wide == lane % MAIN, in_rest & (upper == 0), in_rest & (upper == 1))
    for at_mask, mask in enumerate(masks):
        low = at_mask * tokens
        w_ref[low : low + tokens, :] = jnp.where(mask, gate, 0.0).astype(BF16)


def routes(at, ids_t, weights_t, experts):
    topk, tokens = ids_t.shape
    half = tokens // 2
    rows = experts * MAIN
    own = pl.BlockSpec((topk, half), lambda j, at: (0, at[0]))
    other = pl.BlockSpec((topk, half), lambda j, at: (0, 1 - at[0]))
    shapes = [(rows, tokens), (rows, 2 * tokens), (3 * tokens, rows)]
    return pl.pallas_call(
        routes_kernel,
        grid_spec=pltpu.PrefetchScalarGridSpec(
            num_scalar_prefetch=1,
            grid=(1,),
            in_specs=[own, other, own, other],
            out_specs=[pl.BlockSpec(shape, lambda j, at: (0, 0)) for shape in shapes],
        ),
        out_shape=[jax.ShapeDtypeStruct(shape, BF16) for shape in shapes],
        compiler_params=params(),
        cost_estimate=pl.CostEstimate(flops=10**9, bytes_accessed=10**6, transcendentals=0),
        name="routes",
    )(at, ids_t, ids_t, weights_t, weights_t)


def dispatch_kernel(at_ref, pa_ref, pb_ref, own_ref, other_ref, out_ref):
    step = pl.program_id(0)
    part = other_ref.shape[1]
    tile = part // 4
    cols = pl.ds(pl.multiple_of(step * tile, 128), tile)

    def tokens(index):
        own = pl.ds(pl.multiple_of(at_ref[0] * part + index * tile, 128), tile)
        other = pl.ds(pl.multiple_of(index * tile, 128), tile)
        return [own_ref[:, own], other_ref[:, other]]

    @pl.when(step < 4)
    def _():
        out_ref[:, cols] = dot(pa_ref[...], jnp.concatenate(tokens(step), axis=0)).astype(BF16)

    @pl.when(step >= 4)
    def _():
        both = jnp.concatenate(tokens(step - 4) + tokens(step - 2), axis=0)
        out_ref[:, cols] = dot(pb_ref[...], both).astype(BF16)


def dispatch(at, pa, pb, out_grad, other):
    rows = pa.shape[0]
    whole = pl.BlockSpec(memory_space=pltpu.VMEM)
    return pl.pallas_call(
        dispatch_kernel,
        grid_spec=pltpu.PrefetchScalarGridSpec(
            num_scalar_prefetch=1,
            grid=(6,),
            in_specs=[whole] * 4,
            out_specs=whole,
        ),
        out_shape=jax.ShapeDtypeStruct((rows, other.shape[1] // 2 * 3), BF16),
        compiler_params=params(),
        cost_estimate=pl.CostEstimate(flops=2 * 10**9, bytes_accessed=8 * 10**6, transcendentals=0),
        name="dispatch",
    )(at, pa, pb, out_grad, other)


def hidden_slots(at_ref, x_ref, rest_ref, w_ref, out_ref):
    step = pl.program_id(0)
    main = x_ref.shape[0]
    units = out_ref.shape[1]
    part = rest_ref.shape[1]
    rows = pl.ds(pl.multiple_of(step * units, units), units)
    cols = pl.ds(pl.multiple_of(at_ref[0] * part, 128), part)
    w = w_ref[rows, cols]
    pairs = main // 16
    first = lax.dot_general(x_ref[:, :part], w, NT, preferred_element_type=F32)
    first = first.reshape(pairs, 2, 8, units)
    rest = lax.dot_general(rest_ref[...], w, NT, preferred_element_type=F32)
    rest = rest.reshape(pairs, 8, units)
    top = iota((pairs, 8, units), 1) < REST
    turned = pltpu.roll(first[:, 1], REST, 1)
    out_ref[...] = jnp.stack(
        [first[:, 0], jnp.where(top, rest, turned), jnp.where(top, turned, rest)], axis=1
    ).reshape(main // 2 * 3, units)


def first_kernel(at_ref, x_ref, w_ref, out_ref, rest_ref):
    rows, part = rest_ref.shape
    pairs = rows // 8
    quarter = part // 2

    @pl.when(pl.program_id(0) == 0)
    def _():
        value = x_ref[:, part:].astype(F32).reshape(pairs, 2, 8, quarter)
        top = iota((pairs, 8, quarter), 1) < REST
        low = jnp.where(top, value[:, 0], pltpu.roll(value[:, 1], REST, 1))
        high = jnp.where(top, pltpu.roll(value[:, 0], REST, 1), value[:, 1])
        rest_ref[:, :quarter] = low.reshape(rows, quarter).astype(BF16)
        rest_ref[:, quarter:] = high.reshape(rows, quarter).astype(BF16)

    hidden_slots(at_ref, x_ref, rest_ref, w_ref, out_ref)


def hidden(at, x, w, rest=None):
    rows, lanes = x.shape
    units = w.shape[0]
    tile = 256
    whole = pl.BlockSpec(memory_space=pltpu.VMEM)
    out_spec = pl.BlockSpec((rows // 2 * 3, tile), lambda j, at: (0, j))
    out_shape = jax.ShapeDtypeStruct((rows // 2 * 3, units), F32)
    rest_shape = jax.ShapeDtypeStruct((rows // 2, lanes // 3 * 2), BF16)
    first = rest is None
    return pl.pallas_call(
        first_kernel if first else hidden_slots,
        grid_spec=pltpu.PrefetchScalarGridSpec(
            num_scalar_prefetch=1,
            grid=(units // tile,),
            in_specs=[whole] * (2 if first else 3),
            out_specs=[out_spec, whole] if first else out_spec,
        ),
        out_shape=[out_shape, rest_shape] if first else out_shape,
        compiler_params=params(),
        cost_estimate=pl.CostEstimate(flops=0, bytes_accessed=0, transcendentals=0),
        name="hidden_other" if first else "hidden_own",
    )(*((at, x, w) if first else (at, x, rest, w)))


def diff_kernel(mine_ref, other_ref, gate_ref, up_ref, out_ref):
    step = pl.program_id(0)
    total, units = mine_ref.shape
    count = total // pl.num_programs(0)
    pairs = count // 24
    rows = pl.ds(pl.multiple_of(step * count, count), count)
    main_rows = pl.ds(pl.multiple_of(step * 16 * pairs, 16 * pairs), 16 * pairs)
    rest_rows = pl.ds(pl.multiple_of(total // 3 * 2 + step * 8 * pairs, 8 * pairs), 8 * pairs)

    def put(value, low):
        lanes = value.shape[1]
        value = value.reshape(pairs, 3, 8, lanes)
        top = iota((pairs, 8, lanes), 1) < REST
        odd = jnp.where(top, pltpu.roll(value[:, 1], REST, 1), pltpu.roll(value[:, 2], REST, 1))
        main = jnp.stack([value[:, 0], odd], axis=1).reshape(16 * pairs, lanes)
        rest = jnp.where(top, value[:, 1], value[:, 2]).reshape(8 * pairs, lanes)
        out_ref[main_rows, low : low + lanes] = main.astype(BF16)
        out_ref[rest_rows, low : low + lanes] = rest.astype(BF16)

    grad = mine_ref[rows, :] + other_ref[rows, :]
    value = gate_ref[rows, :].astype(F32)
    up = up_ref[rows, :].astype(F32)
    sigma = jax.nn.sigmoid(value)
    active = value * sigma
    slope = sigma * (1.0 + value * (1.0 - sigma))
    through = grad * active
    score = jnp.sum(through * up, axis=1, keepdims=True)
    put(grad * up * slope, 0)
    put(through, units)
    put(jnp.broadcast_to(score, (count, 128)), 2 * units)


def diffs(mine, other, gate, up):
    rows, units = mine.shape
    whole = pl.BlockSpec(memory_space=pltpu.VMEM)
    return pl.pallas_call(
        diff_kernel,
        grid=(2,),
        in_specs=[whole] * 4,
        out_specs=whole,
        out_shape=jax.ShapeDtypeStruct((rows, 2 * units + 128), BF16),
        compiler_params=params(),
        cost_estimate=pl.CostEstimate(flops=0, bytes_accessed=0, transcendentals=0),
        name="diffs",
    )(mine, other, gate, up)


def spread_rows(low, high):
    rows, lanes = low.shape
    pairs = rows // 8
    low = low.reshape(pairs, 8, lanes)
    high = high.reshape(pairs, 8, lanes)
    top = iota((pairs, 8, lanes), 1) < REST
    even = jnp.where(top, low, pltpu.roll(high, REST, 1))
    odd = jnp.where(top, pltpu.roll(low, REST, 1), high)
    return jnp.stack([even, odd], axis=1).reshape(2 * rows, lanes)


def own_block(units, steps, shift):
    return pl.BlockSpec((TILE, units), lambda j, at: (at[0] * 2 * steps + shift * steps + j, 0))


def early_kernel(at_ref, mine_ref, g0, g1, u0, u1, out_ref):
    units = g0.shape[1]
    w = jnp.concatenate(
        [
            jnp.concatenate([g0[...], u0[...]], axis=1),
            jnp.concatenate([g1[...], u1[...]], axis=1),
        ],
        axis=0,
    )
    cols = pl.ds(pl.multiple_of(pl.program_id(0) * 2 * TILE, TILE), 2 * TILE)
    out_ref[:, cols] = lax.dot_general(mine_ref[:, : 2 * units], w, NT, preferred_element_type=F32)


def early_inputs(at, mine, w_gate, w_up):
    w_gate, w_up = in_hbm(w_gate, w_up)
    rows = mine.shape[0]
    units = w_gate.shape[1]
    steps = w_gate.shape[0] // 4 // TILE
    whole = pl.BlockSpec(memory_space=pltpu.VMEM)
    blocks = [own_block(units, steps, 0), own_block(units, steps, 1)]
    return pl.pallas_call(
        early_kernel,
        grid_spec=pltpu.PrefetchScalarGridSpec(
            num_scalar_prefetch=1,
            grid=(EARLY,),
            in_specs=[whole] + blocks + blocks,
            out_specs=whole,
        ),
        out_shape=jax.ShapeDtypeStruct((rows, EARLY * 2 * TILE), F32),
        compiler_params=params(),
        cost_estimate=pl.CostEstimate(
            flops=8 * EARLY * rows * TILE * units, bytes_accessed=10**7, transcendentals=0
        ),
        name="early_inputs",
    )(at, mine, w_gate, w_gate, w_up, w_up)


def inputs_kernel(
    at_ref, mine_ref, other_ref, early_ref, g0, g1, u0, u1, og_ref, ou_ref, out_ref
):
    step = pl.program_id(0)
    units = g0.shape[1]
    main = out_ref.shape[0]
    quarter = pl.num_programs(0) * TILE

    def at_cols(start):
        return pl.ds(pl.multiple_of(start + step * TILE, TILE), TILE)

    def far(start):
        rows = at_cols(2 * quarter * at_ref[0] + start)
        return [og_ref[rows, :], ou_ref[rows, :]]

    def product(x, low, high):
        w = jnp.concatenate(
            [jnp.concatenate(low, axis=1), jnp.concatenate(high, axis=1)], axis=0
        )
        return lax.dot_general(x, w, NT, preferred_element_type=F32)

    def finish(result):
        out_ref[:, at_cols(0)] = result[:main, :TILE].astype(BF16)
        out_ref[:, at_cols(quarter)] = result[:main, TILE:].astype(BF16)
        rest = spread_rows(result[main:, :TILE], result[main:, TILE:])
        out_ref[:, at_cols(2 * quarter)] = rest.astype(BF16)

    @pl.when(step < EARLY)
    def _():
        cols = pl.ds(pl.multiple_of(step * 2 * TILE, TILE), 2 * TILE)
        finish(product(other_ref[:, : 2 * units], far(0), far(quarter)) + early_ref[:, cols])

    @pl.when(step >= EARLY)
    def _():
        x = jnp.concatenate([mine_ref[:, : 2 * units], other_ref[:, : 2 * units]], axis=1)
        low = [g0[...], u0[...]] + far(0)
        high = [g1[...], u1[...]] + far(quarter)
        finish(product(x, low, high))

    @pl.when(step == 0)
    def _():
        score = mine_ref[:, 2 * units :].astype(F32) + other_ref[:, 2 * units :].astype(F32)
        rest = spread_rows(score[main:], score[main:])
        lane = iota(rest.shape, 1)
        end = out_ref.shape[1] - 128
        out_ref[:, end:] = jnp.where(lane == 0, score[:main], rest).astype(BF16)


def inputs(at, mine, other, early, w_gate, w_up, gate_other, up_other):
    w_gate, w_up = in_hbm(w_gate, w_up)
    rows, lanes = mine.shape
    units = w_gate.shape[1]
    part = w_gate.shape[0] // 2
    steps = part // 2 // TILE
    main = rows // 3 * 2

    def block(shift):
        return pl.BlockSpec(
            (TILE, units),
            lambda j, at: (at[0] * 2 * steps + shift * steps + jnp.maximum(j, EARLY), 0),
        )

    whole = pl.BlockSpec(memory_space=pltpu.VMEM)
    return pl.pallas_call(
        inputs_kernel,
        grid_spec=pltpu.PrefetchScalarGridSpec(
            num_scalar_prefetch=1,
            grid=(steps,),
            in_specs=[whole] * 3 + [block(0), block(1), block(0), block(1), whole, whole],
            out_specs=whole,
        ),
        out_shape=jax.ShapeDtypeStruct((main, 3 * TILE * steps + 128), BF16),
        compiler_params=params(),
        cost_estimate=pl.CostEstimate(
            flops=8 * rows * part * units, bytes_accessed=24 * 10**6, transcendentals=0
        ),
        name="inputs",
    )(at, mine, other, early, w_gate, w_gate, w_up, w_up, gate_other, up_other)


def tokens_of(w_ref, back_ref, out_ref, first):
    step = pl.program_id(0)
    half, tile = out_ref.shape
    tokens = 2 * half
    low = pl.ds(pl.multiple_of(step * tile, 128), tile)
    rest = pl.ds(pl.multiple_of((4 + step % 2) * tile, 128), tile)
    part = pl.ds(pl.multiple_of((1 + step // 2) * tokens + first, half), half)
    slots = jnp.concatenate([back_ref[:, low], back_ref[:, rest]], axis=0)
    w = jnp.concatenate([w_ref[first : first + half, :], w_ref[part, :]], axis=1)
    out_ref[...] = dot(w, slots).astype(BF16)


def send_kernel(w_ref, back_ref, send_ref):
    tokens_of(w_ref, back_ref, send_ref, send_ref.shape[0])


def combine_send(w, back):
    half = w.shape[0] // 6
    tile = (back.shape[1] - 128) // 6
    whole = pl.BlockSpec(memory_space=pltpu.VMEM)
    return pl.pallas_call(
        send_kernel,
        grid=(4,),
        in_specs=[whole, whole],
        out_specs=pl.BlockSpec((half, tile), lambda j: (0, j)),
        out_shape=jax.ShapeDtypeStruct((half, 4 * tile), BF16),
        compiler_params=params(),
        cost_estimate=pl.CostEstimate(flops=10**9, bytes_accessed=7 * 10**6, transcendentals=0),
        name="combine_send",
    )(w, back)


def keep_kernel(at_ref, ids_ref, pa_ref, pb_ref, w_ref, back_ref, keep_ref, grad_ref):
    topk, half = ids_ref.shape
    rows = back_ref.shape[0]
    experts = rows // MAIN

    @pl.when(pl.program_id(0) == 0)
    def _():
        block = iota((rows, experts), 0) // MAIN == iota((rows, experts), 1)
        score = back_ref[:, back_ref.shape[1] - 128 :].astype(F32)

        def one(column, slots):
            value = jnp.where(block, column, 0.0).astype(BF16)
            return lax.dot_general(value, slots, (((0,), (0,)), ((), ())), preferred_element_type=F32)

        table = one(score[:, 0:1], pa_ref[...]) + one(score[:, 1:2], pb_ref[...])
        names = iota((experts, half), 0)
        row = iota((topk, half), 0)
        ids = ids_ref[...]
        result = jnp.zeros((topk, half), F32)
        for k in range(topk):
            hit = names == ids[k : k + 1, :]
            picked = jnp.sum(jnp.where(hit, table, 0.0), axis=0, keepdims=True)
            result = result + jnp.where(row == k, picked, 0.0)
        grad_ref[...] = result.astype(BF16)

    tokens_of(w_ref, back_ref, keep_ref, 0)


def combine_keep(at, ids_t, pa, pb, w, back):
    topk, tokens = ids_t.shape
    half = tokens // 2
    rows, lanes = back.shape
    tile = (lanes - 128) // 6
    whole = pl.BlockSpec(memory_space=pltpu.VMEM)
    return pl.pallas_call(
        keep_kernel,
        grid_spec=pltpu.PrefetchScalarGridSpec(
            num_scalar_prefetch=1,
            grid=(4,),
            in_specs=[
                pl.BlockSpec((topk, half), lambda j, at: (0, at[0])),
                pl.BlockSpec((rows, half), lambda j, at: (0, 0)),
                pl.BlockSpec((rows, half), lambda j, at: (0, 0)),
                whole,
                whole,
            ],
            out_specs=[
                pl.BlockSpec((half, tile), lambda j, at: (0, 4 * at[0] + j)),
                pl.BlockSpec((topk, half), lambda j, at: (0, 0)),
            ],
        ),
        out_shape=[
            jax.ShapeDtypeStruct((half, 8 * tile), BF16),
            jax.ShapeDtypeStruct((topk, half), BF16),
        ],
        compiler_params=params(),
        cost_estimate=pl.CostEstimate(flops=10**9, bytes_accessed=7 * 10**6, transcendentals=0),
        name="combine_keep",
    )(at, ids_t, pa, pb, w, back)


def join_kernel(at_ref, base_ref, came_ref, out_ref):
    out_ref[...] = came_ref[...]


def join(at, base, came):
    half, part = came.shape
    return pl.pallas_call(
        join_kernel,
        grid_spec=pltpu.PrefetchScalarGridSpec(
            num_scalar_prefetch=1,
            grid=(2,),
            in_specs=[
                pl.BlockSpec(memory_space=pl.ANY),
                pl.BlockSpec((half, part // 2), lambda j, at: (0, j)),
            ],
            out_specs=pl.BlockSpec((half, part // 2), lambda j, at: (0, 2 * (1 - at[0]) + j)),
        ),
        out_shape=jax.ShapeDtypeStruct(base.shape, BF16),
        input_output_aliases={1: 0},
        compiler_params=params(),
        cost_estimate=pl.CostEstimate(flops=0, bytes_accessed=2 * 10**6, transcendentals=0),
        name="join",
    )(at, base, came)


def exchange(value, groups):
    rows, lanes = value.shape
    value = lax.all_to_all(
        value.reshape(groups, MAIN, lanes), "expert", split_axis=0, concat_axis=0, tiled=True
    )
    return value.reshape(rows, lanes)


def on_device(out_grad, route_ids, route_weights, gate_pre, up_pre, w_gate, w_up, w_down):
    groups = lax.axis_size("expert")
    seq_at = lax.axis_index("seq")
    at = seq_at.astype(jnp.int32).reshape(1)
    part = out_grad.shape[1] // 2
    w_gate, w_up, w_down = w_gate[0], w_up[0], w_down[0]
    other = swap(lax.dynamic_slice_in_dim(out_grad, (1 - seq_at) * part, part, 1))
    ids_t = route_ids.T
    pa, pb, w = routes(at, ids_t, route_weights.T, groups)
    sent = dispatch(at, pa, pb, out_grad, other)
    w_gate, w_up, w_down, sent = lax.optimization_barrier((w_gate, w_up, w_down, sent))
    down_other, gate_other, up_other = swap(w_down), swap(w_gate), swap(w_up)
    received = exchange(sent, groups)
    received, down_other, gate_other, up_other = lax.optimization_barrier(
        (received, down_other, gate_other, up_other)
    )
    grad_other, rest = hidden(at, received, down_other)
    grad_other = swap(grad_other)
    grad_mine = hidden(at, received, w_down, rest)
    mine = diffs(grad_mine, grad_other, gate_pre[0], up_pre[0])
    theirs = swap(mine)
    early = early_inputs(at, mine, w_gate, w_up)
    slots = inputs(at, mine, theirs, early, w_gate, w_up, gate_other, up_other)
    back = exchange(slots, groups)
    came = swap(combine_send(w, back))
    keep, weight_grad = combine_keep(at, ids_t, pa, pb, w, back)
    return join(at, keep, came), weight_grad.T


def solution(mesh):
    in_specs = (
        P(("expert", "seq"), None),
        P("expert", None),
        P("expert", None),
        P("expert", None, "seq"),
        P("expert", None, "seq"),
        P("expert", None, "seq"),
        P("expert", None, "seq"),
        P("expert", "seq", None),
    )
    out_specs = (P(("expert", "seq"), None), P(("expert", "seq"), None))
    return jax.shard_map(
        on_device, mesh=mesh, in_specs=in_specs, out_specs=out_specs, check_vma=False
    )
```

```python
import jax
import jax.numpy as jnp
from jax import lax
from jax.experimental import pallas as pl
from jax.experimental.pallas import tpu as pltpu
from jax.sharding import PartitionSpec as P

F32 = jnp.float32
BF16 = jnp.bfloat16
NT = (((1,), (1,)), ((), ()))
MAIN = 8
REST = 4
MIB = 1024 * 1024
LIMIT = 14 * MIB
TILE = 256
EARLY = 2


def iota(shape, dim):
    return lax.broadcasted_iota(jnp.int32, shape, dim)


def flag(cond):
    return jnp.where(cond, 1.0, 0.0).astype(F32)


def dot(a, b):
    return jnp.dot(a, b, preferred_element_type=F32)


def params(limit=LIMIT):
    return pltpu.CompilerParams(vmem_limit_bytes=limit)


def in_hbm(*values):
    return [pltpu.with_memory_space_constraint(v, pltpu.HBM) for v in values]


def swap(value):
    return lax.ppermute(value, "seq", [(0, 1), (1, 0)])


def actual(index, at, half):
    return (index + half * at) % (2 * half)


def routes_kernel(at_ref, own_ids, other_ids, own_weights, other_weights, pa_ref, pb_ref, w_ref):
    at = at_ref[0]
    ids = jnp.concatenate([own_ids[...], other_ids[...]], axis=1)
    weights = jnp.concatenate([own_weights[...], other_weights[...]], axis=1)
    topk, tokens = ids.shape
    rows = pa_ref.shape[0]
    experts = rows // MAIN
    names = iota((experts, tokens), 0)
    member = jnp.zeros((experts, tokens), F32)
    gate = jnp.zeros((experts, tokens), F32)
    for k in range(topk):
        hit = names == ids[k : k + 1, :]
        member = member + flag(hit)
        gate = gate + jnp.where(hit, weights[k : k + 1, :], 0.0)
    first = actual(iota((tokens, tokens), 0), at, tokens // 2)
    before = flag(first < actual(iota((tokens, tokens), 1), at, tokens // 2)).astype(BF16)
    place = dot(member.astype(BF16), before)
    place = jnp.where(member > 0.5, place, -1.0).astype(BF16)
    spread = flag(iota((rows, experts), 0) // MAIN == iota((rows, experts), 1)).astype(BF16)
    wide = dot(spread, place).astype(jnp.int32)
    row = iota((rows, tokens), 0)
    pa_ref[...] = flag(wide == row % MAIN).astype(BF16)
    rest = flag(wide == MAIN + row % REST)
    upper = (row // REST) % 2
    pb_ref[:, :tokens] = jnp.where(upper == 0, rest, 0.0).astype(BF16)
    pb_ref[:, tokens:] = jnp.where(upper == 1, rest, 0.0).astype(BF16)

    def by_token(value):
        return lax.dot_general(value, spread, (((0,), (1,)), ((), ())), preferred_element_type=F32)

    wide = by_token(place).astype(jnp.int32)
    lane = iota((tokens, rows), 1)
    in_rest = wide == MAIN + lane % REST
    upper = (lane // REST) % 2
    gate = by_token(gate.astype(BF16))
    masks = (wide == lane % MAIN, in_rest & (upper == 0), in_rest & (upper == 1))
    for at_mask, mask in enumerate(masks):
        low = at_mask * tokens
        w_ref[low : low + tokens, :] = jnp.where(mask, gate, 0.0).astype(BF16)


def routes(at, ids_t, weights_t, experts):
    topk, tokens = ids_t.shape
    half = tokens // 2
    rows = experts * MAIN
    own = pl.BlockSpec((topk, half), lambda j, at: (0, at[0]))
    other = pl.BlockSpec((topk, half), lambda j, at: (0, 1 - at[0]))
    shapes = [(rows, tokens), (rows, 2 * tokens), (3 * tokens, rows)]
    return pl.pallas_call(
        routes_kernel,
        grid_spec=pltpu.PrefetchScalarGridSpec(
            num_scalar_prefetch=1,
            grid=(1,),
            in_specs=[own, other, own, other],
            out_specs=[pl.BlockSpec(shape, lambda j, at: (0, 0)) for shape in shapes],
        ),
        out_shape=[jax.ShapeDtypeStruct(shape, BF16) for shape in shapes],
        compiler_params=params(),
        cost_estimate=pl.CostEstimate(flops=10**9, bytes_accessed=10**6, transcendentals=0),
        name="routes",
    )(at, ids_t, ids_t, weights_t, weights_t)


def dispatch_kernel(at_ref, pa_ref, pb_ref, own_ref, other_ref, out_ref):
    step = pl.program_id(0)
    part = other_ref.shape[1]
    tile = part // 4
    cols = pl.ds(pl.multiple_of(step * tile, 128), tile)

    def tokens(index):
        own = pl.ds(pl.multiple_of(at_ref[0] * part + index * tile, 128), tile)
        other = pl.ds(pl.multiple_of(index * tile, 128), tile)
        return [own_ref[:, own], other_ref[:, other]]

    @pl.when(step < 4)
    def _():
        out_ref[:, cols] = dot(pa_ref[...], jnp.concatenate(tokens(step), axis=0)).astype(BF16)

    @pl.when(step >= 4)
    def _():
        both = jnp.concatenate(tokens(step - 4) + tokens(step - 2), axis=0)
        out_ref[:, cols] = dot(pb_ref[...], both).astype(BF16)


def dispatch(at, pa, pb, out_grad, other):
    rows = pa.shape[0]
    whole = pl.BlockSpec(memory_space=pltpu.VMEM)
    return pl.pallas_call(
        dispatch_kernel,
        grid_spec=pltpu.PrefetchScalarGridSpec(
            num_scalar_prefetch=1,
            grid=(6,),
            in_specs=[whole] * 4,
            out_specs=whole,
        ),
        out_shape=jax.ShapeDtypeStruct((rows, other.shape[1] // 2 * 3), BF16),
        compiler_params=params(),
        cost_estimate=pl.CostEstimate(flops=2 * 10**9, bytes_accessed=8 * 10**6, transcendentals=0),
        name="dispatch",
    )(at, pa, pb, out_grad, other)


def hidden_slots(at_ref, x_ref, rest_ref, w_ref, out_ref):
    step = pl.program_id(0)
    main = x_ref.shape[0]
    units = out_ref.shape[1]
    part = rest_ref.shape[1]
    rows = pl.ds(pl.multiple_of(step * units, units), units)
    cols = pl.ds(pl.multiple_of(at_ref[0] * part, 128), part)
    w = w_ref[rows, cols]
    pairs = main // 16
    first = lax.dot_general(x_ref[:, :part], w, NT, preferred_element_type=F32)
    first = first.reshape(pairs, 2, 8, units)
    rest = lax.dot_general(rest_ref[...], w, NT, preferred_element_type=F32)
    rest = rest.reshape(pairs, 8, units)
    top = iota((pairs, 8, units), 1) < REST
    turned = pltpu.roll(first[:, 1], REST, 1)
    out_ref[...] = jnp.stack(
        [first[:, 0], jnp.where(top, rest, turned), jnp.where(top, turned, rest)], axis=1
    ).reshape(main // 2 * 3, units)


def first_kernel(at_ref, x_ref, w_ref, out_ref, rest_ref):
    rows, part = rest_ref.shape
    pairs = rows // 8
    quarter = part // 2

    @pl.when(pl.program_id(0) == 0)
    def _():
        value = x_ref[:, part:].astype(F32).reshape(pairs, 2, 8, quarter)
        top = iota((pairs, 8, quarter), 1) < REST
        low = jnp.where(top, value[:, 0], pltpu.roll(value[:, 1], REST, 1))
        high = jnp.where(top, pltpu.roll(value[:, 0], REST, 1), value[:, 1])
        rest_ref[:, :quarter] = low.reshape(rows, quarter).astype(BF16)
        rest_ref[:, quarter:] = high.reshape(rows, quarter).astype(BF16)

    hidden_slots(at_ref, x_ref, rest_ref, w_ref, out_ref)


def hidden(at, x, w, rest=None):
    rows, lanes = x.shape
    units = w.shape[0]
    tile = 256
    whole = pl.BlockSpec(memory_space=pltpu.VMEM)
    out_spec = pl.BlockSpec((rows // 2 * 3, tile), lambda j, at: (0, j))
    out_shape = jax.ShapeDtypeStruct((rows // 2 * 3, units), F32)
    rest_shape = jax.ShapeDtypeStruct((rows // 2, lanes // 3 * 2), BF16)
    first = rest is None
    return pl.pallas_call(
        first_kernel if first else hidden_slots,
        grid_spec=pltpu.PrefetchScalarGridSpec(
            num_scalar_prefetch=1,
            grid=(units // tile,),
            in_specs=[whole] * (2 if first else 3),
            out_specs=[out_spec, whole] if first else out_spec,
        ),
        out_shape=[out_shape, rest_shape] if first else out_shape,
        compiler_params=params(),
        cost_estimate=pl.CostEstimate(flops=0, bytes_accessed=0, transcendentals=0),
        name="hidden_other" if first else "hidden_own",
    )(*((at, x, w) if first else (at, x, rest, w)))


def diff_kernel(mine_ref, other_ref, gate_ref, up_ref, out_ref):
    step = pl.program_id(0)
    total, units = mine_ref.shape
    count = total // pl.num_programs(0)
    pairs = count // 24
    rows = pl.ds(pl.multiple_of(step * count, count), count)
    main_rows = pl.ds(pl.multiple_of(step * 16 * pairs, 16 * pairs), 16 * pairs)
    rest_rows = pl.ds(pl.multiple_of(total // 3 * 2 + step * 8 * pairs, 8 * pairs), 8 * pairs)

    def put(value, low):
        lanes = value.shape[1]
        value = value.reshape(pairs, 3, 8, lanes)
        top = iota((pairs, 8, lanes), 1) < REST
        odd = jnp.where(top, pltpu.roll(value[:, 1], REST, 1), pltpu.roll(value[:, 2], REST, 1))
        main = jnp.stack([value[:, 0], odd], axis=1).reshape(16 * pairs, lanes)
        rest = jnp.where(top, value[:, 1], value[:, 2]).reshape(8 * pairs, lanes)
        out_ref[main_rows, low : low + lanes] = main.astype(BF16)
        out_ref[rest_rows, low : low + lanes] = rest.astype(BF16)

    grad = mine_ref[rows, :] + other_ref[rows, :]
    value = gate_ref[rows, :].astype(F32)
    up = up_ref[rows, :].astype(F32)
    sigma = jax.nn.sigmoid(value)
    active = value * sigma
    slope = sigma * (1.0 + value * (1.0 - sigma))
    through = grad * active
    score = jnp.sum(through * up, axis=1, keepdims=True)
    put(grad * up * slope, 0)
    put(through, units)
    put(jnp.broadcast_to(score, (count, 128)), 2 * units)


def diffs(mine, other, gate, up):
    rows, units = mine.shape
    whole = pl.BlockSpec(memory_space=pltpu.VMEM)
    return pl.pallas_call(
        diff_kernel,
        grid=(2,),
        in_specs=[whole] * 4,
        out_specs=whole,
        out_shape=jax.ShapeDtypeStruct((rows, 2 * units + 128), BF16),
        compiler_params=params(),
        cost_estimate=pl.CostEstimate(flops=0, bytes_accessed=0, transcendentals=0),
        name="diffs",
    )(mine, other, gate, up)


def spread_rows(low, high):
    rows, lanes = low.shape
    pairs = rows // 8
    low = low.reshape(pairs, 8, lanes)
    high = high.reshape(pairs, 8, lanes)
    top = iota((pairs, 8, lanes), 1) < REST
    even = jnp.where(top, low, pltpu.roll(high, REST, 1))
    odd = jnp.where(top, pltpu.roll(low, REST, 1), high)
    return jnp.stack([even, odd], axis=1).reshape(2 * rows, lanes)


def own_block(units, steps, shift):
    return pl.BlockSpec((TILE, units), lambda j, at: (at[0] * 2 * steps + shift * steps + j, 0))


def early_kernel(at_ref, mine_ref, g0, g1, u0, u1, out_ref):
    units = g0.shape[1]
    w = jnp.concatenate(
        [
            jnp.concatenate([g0[...], u0[...]], axis=1),
            jnp.concatenate([g1[...], u1[...]], axis=1),
        ],
        axis=0,
    )
    cols = pl.ds(pl.multiple_of(pl.program_id(0) * 2 * TILE, TILE), 2 * TILE)
    out_ref[:, cols] = lax.dot_general(mine_ref[:, : 2 * units], w, NT, preferred_element_type=F32)


def early_inputs(at, mine, w_gate, w_up):
    w_gate, w_up = in_hbm(w_gate, w_up)
    rows = mine.shape[0]
    units = w_gate.shape[1]
    steps = w_gate.shape[0] // 4 // TILE
    whole = pl.BlockSpec(memory_space=pltpu.VMEM)
    blocks = [own_block(units, steps, 0), own_block(units, steps, 1)]
    return pl.pallas_call(
        early_kernel,
        grid_spec=pltpu.PrefetchScalarGridSpec(
            num_scalar_prefetch=1,
            grid=(EARLY,),
            in_specs=[whole] + blocks + blocks,
            out_specs=whole,
        ),
        out_shape=jax.ShapeDtypeStruct((rows, EARLY * 2 * TILE), F32),
        compiler_params=params(),
        cost_estimate=pl.CostEstimate(
            flops=8 * EARLY * rows * TILE * units, bytes_accessed=10**7, transcendentals=0
        ),
        name="early_inputs",
    )(at, mine, w_gate, w_gate, w_up, w_up)


def inputs_kernel(
    at_ref, mine_ref, other_ref, early_ref, g0, g1, u0, u1, og_ref, ou_ref, out_ref
):
    step = pl.program_id(0)
    units = g0.shape[1]
    main = out_ref.shape[0]
    quarter = pl.num_programs(0) * TILE

    def at_cols(start):
        return pl.ds(pl.multiple_of(start + step * TILE, TILE), TILE)

    def far(start):
        rows = at_cols(2 * quarter * at_ref[0] + start)
        return [og_ref[rows, :], ou_ref[rows, :]]

    def product(x, low, high):
        w = jnp.concatenate(
            [jnp.concatenate(low, axis=1), jnp.concatenate(high, axis=1)], axis=0
        )
        return lax.dot_general(x, w, NT, preferred_element_type=F32)

    def finish(result):
        out_ref[:, at_cols(0)] = result[:main, :TILE].astype(BF16)
        out_ref[:, at_cols(quarter)] = result[:main, TILE:].astype(BF16)
        rest = spread_rows(result[main:, :TILE], result[main:, TILE:])
        out_ref[:, at_cols(2 * quarter)] = rest.astype(BF16)

    @pl.when(step < EARLY)
    def _():
        cols = pl.ds(pl.multiple_of(step * 2 * TILE, TILE), 2 * TILE)
        finish(product(other_ref[:, : 2 * units], far(0), far(quarter)) + early_ref[:, cols])

    @pl.when(step >= EARLY)
    def _():
        x = jnp.concatenate([mine_ref[:, : 2 * units], other_ref[:, : 2 * units]], axis=1)
        low = [g0[...], u0[...]] + far(0)
        high = [g1[...], u1[...]] + far(quarter)
        finish(product(x, low, high))

    @pl.when(step == 0)
    def _():
        score = mine_ref[:, 2 * units :].astype(F32) + other_ref[:, 2 * units :].astype(F32)
        rest = spread_rows(score[main:], score[main:])
        lane = iota(rest.shape, 1)
        end = out_ref.shape[1] - 128
        out_ref[:, end:] = jnp.where(lane == 0, score[:main], rest).astype(BF16)


def inputs(at, mine, other, early, w_gate, w_up, gate_other, up_other):
    w_gate, w_up = in_hbm(w_gate, w_up)
    rows, lanes = mine.shape
    units = w_gate.shape[1]
    part = w_gate.shape[0] // 2
    steps = part // 2 // TILE
    main = rows // 3 * 2

    def block(shift):
        return pl.BlockSpec(
            (TILE, units),
            lambda j, at: (at[0] * 2 * steps + shift * steps + jnp.maximum(j, EARLY), 0),
        )

    whole = pl.BlockSpec(memory_space=pltpu.VMEM)
    return pl.pallas_call(
        inputs_kernel,
        grid_spec=pltpu.PrefetchScalarGridSpec(
            num_scalar_prefetch=1,
            grid=(steps,),
            in_specs=[whole] * 3 + [block(0), block(1), block(0), block(1), whole, whole],
            out_specs=whole,
        ),
        out_shape=jax.ShapeDtypeStruct((main, 3 * TILE * steps + 128), BF16),
        compiler_params=params(),
        cost_estimate=pl.CostEstimate(
            flops=8 * rows * part * units, bytes_accessed=24 * 10**6, transcendentals=0
        ),
        name="inputs",
    )(at, mine, other, early, w_gate, w_gate, w_up, w_up, gate_other, up_other)


def tokens_of(w_ref, back_ref, out_ref, first):
    step = pl.program_id(0)
    half, tile = out_ref.shape
    tokens = 2 * half
    low = pl.ds(pl.multiple_of(step * tile, 128), tile)
    rest = pl.ds(pl.multiple_of((4 + step % 2) * tile, 128), tile)
    part = pl.ds(pl.multiple_of((1 + step // 2) * tokens + first, half), half)
    slots = jnp.concatenate([back_ref[:, low], back_ref[:, rest]], axis=0)
    w = jnp.concatenate([w_ref[first : first + half, :], w_ref[part, :]], axis=1)
    out_ref[...] = dot(w, slots).astype(BF16)


def send_kernel(w_ref, back_ref, send_ref):
    tokens_of(w_ref, back_ref, send_ref, send_ref.shape[0])


def combine_send(w, back):
    half = w.shape[0] // 6
    tile = (back.shape[1] - 128) // 6
    whole = pl.BlockSpec(memory_space=pltpu.VMEM)
    return pl.pallas_call(
        send_kernel,
        grid=(4,),
        in_specs=[whole, whole],
        out_specs=pl.BlockSpec((half, tile), lambda j: (0, j)),
        out_shape=jax.ShapeDtypeStruct((half, 4 * tile), BF16),
        compiler_params=params(),
        cost_estimate=pl.CostEstimate(flops=10**9, bytes_accessed=7 * 10**6, transcendentals=0),
        name="combine_send",
    )(w, back)


def keep_kernel(at_ref, ids_ref, pa_ref, pb_ref, w_ref, back_ref, keep_ref, grad_ref):
    topk, half = grad_ref.shape
    rows = back_ref.shape[0]
    experts = rows // MAIN

    @pl.when(pl.program_id(0) == 0)
    def _():
        block = iota((rows, experts), 0) // MAIN == iota((rows, experts), 1)
        score = back_ref[:, back_ref.shape[1] - 128 :].astype(F32)

        def one(column, slots):
            value = jnp.where(block, column, 0.0).astype(BF16)
            return lax.dot_general(value, slots, (((0,), (0,)), ((), ())), preferred_element_type=F32)

        table = one(score[:, 0:1], pa_ref[:, :half]) + one(score[:, 1:2], pb_ref[:, :half])
        names = iota((experts, half), 0)
        row = iota((topk, half), 0)
        ids = ids_ref[:, pl.ds(pl.multiple_of(at_ref[0] * half, half), half)]
        result = jnp.zeros((topk, half), F32)
        for k in range(topk):
            hit = names == ids[k : k + 1, :]
            picked = jnp.sum(jnp.where(hit, table, 0.0), axis=0, keepdims=True)
            result = result + jnp.where(row == k, picked, 0.0)
        grad_ref[...] = result.astype(BF16)

    tokens_of(w_ref, back_ref, keep_ref, 0)


def combine_keep(at, ids_t, pa, pb, w, back):
    topk, tokens = ids_t.shape
    half = tokens // 2
    tile = (back.shape[1] - 128) // 6
    whole = pl.BlockSpec(memory_space=pltpu.VMEM)
    return pl.pallas_call(
        keep_kernel,
        grid_spec=pltpu.PrefetchScalarGridSpec(
            num_scalar_prefetch=1,
            grid=(4,),
            in_specs=[whole] * 5,
            out_specs=[
                pl.BlockSpec((half, tile), lambda j, at: (0, 4 * at[0] + j)),
                pl.BlockSpec((topk, half), lambda j, at: (0, 0)),
            ],
        ),
        out_shape=[
            jax.ShapeDtypeStruct((half, 8 * tile), BF16),
            jax.ShapeDtypeStruct((topk, half), BF16),
        ],
        compiler_params=params(),
        cost_estimate=pl.CostEstimate(flops=10**9, bytes_accessed=7 * 10**6, transcendentals=0),
        name="combine_keep",
    )(at, ids_t, pa, pb, w, back)


def join_kernel(at_ref, base_ref, came_ref, out_ref):
    out_ref[...] = came_ref[...]


def join(at, base, came):
    half, part = came.shape
    return pl.pallas_call(
        join_kernel,
        grid_spec=pltpu.PrefetchScalarGridSpec(
            num_scalar_prefetch=1,
            grid=(2,),
            in_specs=[
                pl.BlockSpec(memory_space=pl.ANY),
                pl.BlockSpec((half, part // 2), lambda j, at: (0, j)),
            ],
            out_specs=pl.BlockSpec((half, part // 2), lambda j, at: (0, 2 * (1 - at[0]) + j)),
        ),
        out_shape=jax.ShapeDtypeStruct(base.shape, BF16),
        input_output_aliases={1: 0},
        compiler_params=params(),
        cost_estimate=pl.CostEstimate(flops=0, bytes_accessed=2 * 10**6, transcendentals=0),
        name="join",
    )(at, base, came)


def exchange(value, groups):
    rows, lanes = value.shape
    value = lax.all_to_all(
        value.reshape(groups, MAIN, lanes), "expert", split_axis=0, concat_axis=0, tiled=True
    )
    return value.reshape(rows, lanes)


def on_device(out_grad, route_ids, route_weights, gate_pre, up_pre, w_gate, w_up, w_down):
    groups = lax.axis_size("expert")
    seq_at = lax.axis_index("seq")
    at = seq_at.astype(jnp.int32).reshape(1)
    part = out_grad.shape[1] // 2
    w_gate, w_up, w_down = w_gate[0], w_up[0], w_down[0]
    other = swap(lax.dynamic_slice_in_dim(out_grad, (1 - seq_at) * part, part, 1))
    ids_t = route_ids.T
    pa, pb, w = routes(at, ids_t, route_weights.T, groups)
    sent = dispatch(at, pa, pb, out_grad, other)
    w_gate, w_up, w_down, sent = lax.optimization_barrier((w_gate, w_up, w_down, sent))
    down_other, gate_other, up_other = swap(w_down), swap(w_gate), swap(w_up)
    received = exchange(sent, groups)
    received, down_other, gate_other, up_other = lax.optimization_barrier(
        (received, down_other, gate_other, up_other)
    )
    grad_other, rest = hidden(at, received, down_other)
    grad_other = swap(grad_other)
    grad_mine = hidden(at, received, w_down, rest)
    mine = diffs(grad_mine, grad_other, gate_pre[0], up_pre[0])
    theirs = swap(mine)
    early = early_inputs(at, mine, w_gate, w_up)
    slots = inputs(at, mine, theirs, early, w_gate, w_up, gate_other, up_other)
    back = exchange(slots, groups)
    came = swap(combine_send(w, back))
    keep, weight_grad = combine_keep(at, ids_t, pa, pb, w, back)
    return join(at, keep, came), weight_grad.T


def solution(mesh):
    in_specs = (
        P(("expert", "seq"), None),
        P("expert", None),
        P("expert", None),
        P("expert", None, "seq"),
        P("expert", None, "seq"),
        P("expert", None, "seq"),
        P("expert", None, "seq"),
        P("expert", "seq", None),
    )
    out_specs = (P(("expert", "seq"), None), P(("expert", "seq"), None))
    return jax.shard_map(
        on_device, mesh=mesh, in_specs=in_specs, out_specs=out_specs, check_vma=False
    )
```

```python
import jax
import jax.numpy as jnp
from jax import lax
from jax.experimental import pallas as pl
from jax.experimental.pallas import tpu as pltpu
from jax.sharding import PartitionSpec as P

F32 = jnp.float32
BF16 = jnp.bfloat16
NT = (((1,), (1,)), ((), ()))
MAIN = 8
REST = 4
MIB = 1024 * 1024
LIMIT = 14 * MIB
TILE = 256
EARLY = 2


def iota(shape, dim):
    return lax.broadcasted_iota(jnp.int32, shape, dim)


def flag(cond):
    return jnp.where(cond, 1.0, 0.0).astype(F32)


def dot(a, b):
    return jnp.dot(a, b, preferred_element_type=F32)


def params(limit=LIMIT):
    return pltpu.CompilerParams(vmem_limit_bytes=limit)


def in_hbm(*values):
    return [pltpu.with_memory_space_constraint(v, pltpu.HBM) for v in values]


def swap(value):
    return lax.ppermute(value, "seq", [(0, 1), (1, 0)])


def actual(index, at, half):
    return (index + half * at) % (2 * half)


def routes_kernel(at_ref, own_ids, other_ids, own_weights, other_weights, pa_ref, pb_ref, w_ref):
    at = at_ref[0]
    ids = jnp.concatenate([own_ids[...], other_ids[...]], axis=1)
    weights = jnp.concatenate([own_weights[...], other_weights[...]], axis=1)
    topk, tokens = ids.shape
    rows = pa_ref.shape[0]
    experts = rows // MAIN
    names = iota((experts, tokens), 0)
    member = jnp.zeros((experts, tokens), F32)
    gate = jnp.zeros((experts, tokens), F32)
    for k in range(topk):
        hit = names == ids[k : k + 1, :]
        member = member + flag(hit)
        gate = gate + jnp.where(hit, weights[k : k + 1, :], 0.0)
    first = actual(iota((tokens, tokens), 0), at, tokens // 2)
    before = flag(first < actual(iota((tokens, tokens), 1), at, tokens // 2)).astype(BF16)
    place = dot(member.astype(BF16), before)
    place = jnp.where(member > 0.5, place, -1.0).astype(BF16)
    spread = flag(iota((rows, experts), 0) // MAIN == iota((rows, experts), 1)).astype(BF16)
    wide = dot(spread, place).astype(jnp.int32)
    row = iota((rows, tokens), 0)
    pa_ref[...] = flag(wide == row % MAIN).astype(BF16)
    rest = flag(wide == MAIN + row % REST)
    upper = (row // REST) % 2
    pb_ref[:, :tokens] = jnp.where(upper == 0, rest, 0.0).astype(BF16)
    pb_ref[:, tokens:] = jnp.where(upper == 1, rest, 0.0).astype(BF16)

    def by_token(value):
        return lax.dot_general(value, spread, (((0,), (1,)), ((), ())), preferred_element_type=F32)

    wide = by_token(place).astype(jnp.int32)
    lane = iota((tokens, rows), 1)
    in_rest = wide == MAIN + lane % REST
    upper = (lane // REST) % 2
    gate = by_token(gate.astype(BF16))
    masks = (wide == lane % MAIN, in_rest & (upper == 0), in_rest & (upper == 1))
    for at_mask, mask in enumerate(masks):
        low = at_mask * tokens
        w_ref[low : low + tokens, :] = jnp.where(mask, gate, 0.0).astype(BF16)


def routes(at, ids_t, weights_t, experts):
    topk, tokens = ids_t.shape
    half = tokens // 2
    rows = experts * MAIN
    own = pl.BlockSpec((topk, half), lambda j, at: (0, at[0]))
    other = pl.BlockSpec((topk, half), lambda j, at: (0, 1 - at[0]))
    shapes = [(rows, tokens), (rows, 2 * tokens), (3 * tokens, rows)]
    return pl.pallas_call(
        routes_kernel,
        grid_spec=pltpu.PrefetchScalarGridSpec(
            num_scalar_prefetch=1,
            grid=(1,),
            in_specs=[own, other, own, other],
            out_specs=[pl.BlockSpec(shape, lambda j, at: (0, 0)) for shape in shapes],
        ),
        out_shape=[jax.ShapeDtypeStruct(shape, BF16) for shape in shapes],
        compiler_params=params(),
        cost_estimate=pl.CostEstimate(flops=10**9, bytes_accessed=10**6, transcendentals=0),
        name="routes",
    )(at, ids_t, ids_t, weights_t, weights_t)


def dispatch_kernel(at_ref, pa_ref, pb_ref, own_ref, other_ref, out_ref):
    step = pl.program_id(0)
    part = other_ref.shape[1]
    tile = part // 2
    cols = pl.ds(pl.multiple_of(step * tile, 128), tile)

    def tokens(index):
        own = pl.ds(pl.multiple_of(at_ref[0] * part + index * tile, 128), tile)
        other = pl.ds(pl.multiple_of(index * tile, 128), tile)
        return [own_ref[:, own], other_ref[:, other]]

    @pl.when(step < 2)
    def _():
        out_ref[:, cols] = dot(pa_ref[...], jnp.concatenate(tokens(step), axis=0)).astype(BF16)

    @pl.when(step == 2)
    def _():
        both = jnp.concatenate(tokens(0) + tokens(1), axis=0)
        out_ref[:, cols] = dot(pb_ref[...], both).astype(BF16)


def dispatch(at, pa, pb, out_grad, other):
    rows = pa.shape[0]
    whole = pl.BlockSpec(memory_space=pltpu.VMEM)
    return pl.pallas_call(
        dispatch_kernel,
        grid_spec=pltpu.PrefetchScalarGridSpec(
            num_scalar_prefetch=1,
            grid=(3,),
            in_specs=[whole] * 4,
            out_specs=whole,
        ),
        out_shape=jax.ShapeDtypeStruct((rows, other.shape[1] // 2 * 3), BF16),
        compiler_params=params(),
        cost_estimate=pl.CostEstimate(flops=2 * 10**9, bytes_accessed=8 * 10**6, transcendentals=0),
        name="dispatch",
    )(at, pa, pb, out_grad, other)


def hidden_slots(at_ref, x_ref, rest_ref, w_ref, out_ref):
    step = pl.program_id(0)
    main = x_ref.shape[0]
    units = out_ref.shape[1]
    part = rest_ref.shape[1]
    rows = pl.ds(pl.multiple_of(step * units, units), units)
    cols = pl.ds(pl.multiple_of(at_ref[0] * part, 128), part)
    w = w_ref[rows, cols]
    pairs = main // 16
    first = lax.dot_general(x_ref[:, :part], w, NT, preferred_element_type=F32)
    first = first.reshape(pairs, 2, 8, units)
    rest = lax.dot_general(rest_ref[...], w, NT, preferred_element_type=F32)
    rest = rest.reshape(pairs, 8, units)
    top = iota((pairs, 8, units), 1) < REST
    turned = pltpu.roll(first[:, 1], REST, 1)
    out_ref[...] = jnp.stack(
        [first[:, 0], jnp.where(top, rest, turned), jnp.where(top, turned, rest)], axis=1
    ).reshape(main // 2 * 3, units)


def first_kernel(at_ref, x_ref, w_ref, out_ref, rest_ref):
    rows, part = rest_ref.shape
    pairs = rows // 8
    quarter = part // 2

    @pl.when(pl.program_id(0) == 0)
    def _():
        value = x_ref[:, part:].astype(F32).reshape(pairs, 2, 8, quarter)
        top = iota((pairs, 8, quarter), 1) < REST
        low = jnp.where(top, value[:, 0], pltpu.roll(value[:, 1], REST, 1))
        high = jnp.where(top, pltpu.roll(value[:, 0], REST, 1), value[:, 1])
        rest_ref[:, :quarter] = low.reshape(rows, quarter).astype(BF16)
        rest_ref[:, quarter:] = high.reshape(rows, quarter).astype(BF16)

    hidden_slots(at_ref, x_ref, rest_ref, w_ref, out_ref)


def hidden(at, x, w, rest=None):
    rows, lanes = x.shape
    units = w.shape[0]
    tile = 256
    whole = pl.BlockSpec(memory_space=pltpu.VMEM)
    out_spec = pl.BlockSpec((rows // 2 * 3, tile), lambda j, at: (0, j))
    out_shape = jax.ShapeDtypeStruct((rows // 2 * 3, units), F32)
    rest_shape = jax.ShapeDtypeStruct((rows // 2, lanes // 3 * 2), BF16)
    first = rest is None
    return pl.pallas_call(
        first_kernel if first else hidden_slots,
        grid_spec=pltpu.PrefetchScalarGridSpec(
            num_scalar_prefetch=1,
            grid=(units // tile,),
            in_specs=[whole] * (2 if first else 3),
            out_specs=[out_spec, whole] if first else out_spec,
        ),
        out_shape=[out_shape, rest_shape] if first else out_shape,
        compiler_params=params(),
        cost_estimate=pl.CostEstimate(flops=0, bytes_accessed=0, transcendentals=0),
        name="hidden_other" if first else "hidden_own",
    )(*((at, x, w) if first else (at, x, rest, w)))


def diff_kernel(mine_ref, other_ref, gate_ref, up_ref, out_ref):
    step = pl.program_id(0)
    total, units = mine_ref.shape
    count = total // pl.num_programs(0)
    pairs = count // 24
    rows = pl.ds(pl.multiple_of(step * count, count), count)
    main_rows = pl.ds(pl.multiple_of(step * 16 * pairs, 16 * pairs), 16 * pairs)
    rest_rows = pl.ds(pl.multiple_of(total // 3 * 2 + step * 8 * pairs, 8 * pairs), 8 * pairs)

    def put(value, low):
        lanes = value.shape[1]
        value = value.reshape(pairs, 3, 8, lanes)
        top = iota((pairs, 8, lanes), 1) < REST
        odd = jnp.where(top, pltpu.roll(value[:, 1], REST, 1), pltpu.roll(value[:, 2], REST, 1))
        main = jnp.stack([value[:, 0], odd], axis=1).reshape(16 * pairs, lanes)
        rest = jnp.where(top, value[:, 1], value[:, 2]).reshape(8 * pairs, lanes)
        out_ref[main_rows, low : low + lanes] = main.astype(BF16)
        out_ref[rest_rows, low : low + lanes] = rest.astype(BF16)

    grad = mine_ref[rows, :] + other_ref[rows, :]
    value = gate_ref[rows, :].astype(F32)
    up = up_ref[rows, :].astype(F32)
    sigma = jax.nn.sigmoid(value)
    active = value * sigma
    slope = sigma * (1.0 + value * (1.0 - sigma))
    through = grad * active
    score = jnp.sum(through * up, axis=1, keepdims=True)
    put(grad * up * slope, 0)
    put(through, units)
    put(jnp.broadcast_to(score, (count, 128)), 2 * units)


def diffs(mine, other, gate, up):
    rows, units = mine.shape
    whole = pl.BlockSpec(memory_space=pltpu.VMEM)
    return pl.pallas_call(
        diff_kernel,
        grid=(2,),
        in_specs=[whole] * 4,
        out_specs=whole,
        out_shape=jax.ShapeDtypeStruct((rows, 2 * units + 128), BF16),
        compiler_params=params(),
        cost_estimate=pl.CostEstimate(flops=0, bytes_accessed=0, transcendentals=0),
        name="diffs",
    )(mine, other, gate, up)


def spread_rows(low, high):
    rows, lanes = low.shape
    pairs = rows // 8
    low = low.reshape(pairs, 8, lanes)
    high = high.reshape(pairs, 8, lanes)
    top = iota((pairs, 8, lanes), 1) < REST
    even = jnp.where(top, low, pltpu.roll(high, REST, 1))
    odd = jnp.where(top, pltpu.roll(low, REST, 1), high)
    return jnp.stack([even, odd], axis=1).reshape(2 * rows, lanes)


def own_block(units, steps, shift):
    return pl.BlockSpec((TILE, units), lambda j, at: (at[0] * 2 * steps + shift * steps + j, 0))


def early_kernel(at_ref, mine_ref, g0, g1, u0, u1, out_ref):
    units = g0.shape[1]
    w = jnp.concatenate(
        [
            jnp.concatenate([g0[...], u0[...]], axis=1),
            jnp.concatenate([g1[...], u1[...]], axis=1),
        ],
        axis=0,
    )
    cols = pl.ds(pl.multiple_of(pl.program_id(0) * 2 * TILE, TILE), 2 * TILE)
    out_ref[:, cols] = lax.dot_general(mine_ref[:, : 2 * units], w, NT, preferred_element_type=F32)


def early_inputs(at, mine, w_gate, w_up):
    w_gate, w_up = in_hbm(w_gate, w_up)
    rows = mine.shape[0]
    units = w_gate.shape[1]
    steps = w_gate.shape[0] // 4 // TILE
    whole = pl.BlockSpec(memory_space=pltpu.VMEM)
    blocks = [own_block(units, steps, 0), own_block(units, steps, 1)]
    return pl.pallas_call(
        early_kernel,
        grid_spec=pltpu.PrefetchScalarGridSpec(
            num_scalar_prefetch=1,
            grid=(EARLY,),
            in_specs=[whole] + blocks + blocks,
            out_specs=whole,
        ),
        out_shape=jax.ShapeDtypeStruct((rows, EARLY * 2 * TILE), F32),
        compiler_params=params(),
        cost_estimate=pl.CostEstimate(
            flops=8 * EARLY * rows * TILE * units, bytes_accessed=10**7, transcendentals=0
        ),
        name="early_inputs",
    )(at, mine, w_gate, w_gate, w_up, w_up)


def inputs_kernel(
    at_ref, mine_ref, other_ref, early_ref, g0, g1, u0, u1, og_ref, ou_ref, out_ref
):
    step = pl.program_id(0)
    units = g0.shape[1]
    main = out_ref.shape[0]
    quarter = pl.num_programs(0) * TILE

    def at_cols(start):
        return pl.ds(pl.multiple_of(start + step * TILE, TILE), TILE)

    def far(start):
        rows = at_cols(2 * quarter * at_ref[0] + start)
        return [og_ref[rows, :], ou_ref[rows, :]]

    def product(x, low, high):
        w = jnp.concatenate(
            [jnp.concatenate(low, axis=1), jnp.concatenate(high, axis=1)], axis=0
        )
        return lax.dot_general(x, w, NT, preferred_element_type=F32)

    def finish(result):
        out_ref[:, at_cols(0)] = result[:main, :TILE].astype(BF16)
        out_ref[:, at_cols(quarter)] = result[:main, TILE:].astype(BF16)
        rest = spread_rows(result[main:, :TILE], result[main:, TILE:])
        out_ref[:, at_cols(2 * quarter)] = rest.astype(BF16)

    @pl.when(step < EARLY)
    def _():
        cols = pl.ds(pl.multiple_of(step * 2 * TILE, TILE), 2 * TILE)
        finish(product(other_ref[:, : 2 * units], far(0), far(quarter)) + early_ref[:, cols])

    @pl.when(step >= EARLY)
    def _():
        x = jnp.concatenate([mine_ref[:, : 2 * units], other_ref[:, : 2 * units]], axis=1)
        low = [g0[...], u0[...]] + far(0)
        high = [g1[...], u1[...]] + far(quarter)
        finish(product(x, low, high))

    @pl.when(step == 0)
    def _():
        score = mine_ref[:, 2 * units :].astype(F32) + other_ref[:, 2 * units :].astype(F32)
        rest = spread_rows(score[main:], score[main:])
        lane = iota(rest.shape, 1)
        end = out_ref.shape[1] - 128
        out_ref[:, end:] = jnp.where(lane == 0, score[:main], rest).astype(BF16)


def inputs(at, mine, other, early, w_gate, w_up, gate_other, up_other):
    w_gate, w_up = in_hbm(w_gate, w_up)
    rows, lanes = mine.shape
    units = w_gate.shape[1]
    part = w_gate.shape[0] // 2
    steps = part // 2 // TILE
    main = rows // 3 * 2

    def block(shift):
        return pl.BlockSpec(
            (TILE, units),
            lambda j, at: (at[0] * 2 * steps + shift * steps + jnp.maximum(j, EARLY), 0),
        )

    whole = pl.BlockSpec(memory_space=pltpu.VMEM)
    return pl.pallas_call(
        inputs_kernel,
        grid_spec=pltpu.PrefetchScalarGridSpec(
            num_scalar_prefetch=1,
            grid=(steps,),
            in_specs=[whole] * 3 + [block(0), block(1), block(0), block(1), whole, whole],
            out_specs=whole,
        ),
        out_shape=jax.ShapeDtypeStruct((main, 3 * TILE * steps + 128), BF16),
        compiler_params=params(),
        cost_estimate=pl.CostEstimate(
            flops=8 * rows * part * units, bytes_accessed=24 * 10**6, transcendentals=0
        ),
        name="inputs",
    )(at, mine, other, early, w_gate, w_gate, w_up, w_up, gate_other, up_other)


def tokens_of(w_ref, back_ref, out_ref, first):
    step = pl.program_id(0)
    half, tile = out_ref.shape
    tokens = 2 * half
    low = pl.ds(pl.multiple_of(step * tile, 128), tile)
    rest = pl.ds(pl.multiple_of((4 + step % 2) * tile, 128), tile)
    part = pl.ds(pl.multiple_of((1 + step // 2) * tokens + first, half), half)
    slots = jnp.concatenate([back_ref[:, low], back_ref[:, rest]], axis=0)
    w = jnp.concatenate([w_ref[first : first + half, :], w_ref[part, :]], axis=1)
    out_ref[...] = dot(w, slots).astype(BF16)


def send_kernel(w_ref, back_ref, send_ref):
    tokens_of(w_ref, back_ref, send_ref, send_ref.shape[0])


def combine_send(w, back):
    half = w.shape[0] // 6
    tile = (back.shape[1] - 128) // 6
    whole = pl.BlockSpec(memory_space=pltpu.VMEM)
    return pl.pallas_call(
        send_kernel,
        grid=(4,),
        in_specs=[whole, whole],
        out_specs=pl.BlockSpec((half, tile), lambda j: (0, j)),
        out_shape=jax.ShapeDtypeStruct((half, 4 * tile), BF16),
        compiler_params=params(),
        cost_estimate=pl.CostEstimate(flops=10**9, bytes_accessed=7 * 10**6, transcendentals=0),
        name="combine_send",
    )(w, back)


def keep_kernel(at_ref, ids_ref, pa_ref, pb_ref, w_ref, back_ref, keep_ref, grad_ref):
    topk, half = ids_ref.shape
    rows = back_ref.shape[0]
    experts = rows // MAIN

    @pl.when(pl.program_id(0) == 0)
    def _():
        block = iota((rows, experts), 0) // MAIN == iota((rows, experts), 1)
        score = back_ref[:, back_ref.shape[1] - 128 :].astype(F32)

        def one(column, slots):
            value = jnp.where(block, column, 0.0).astype(BF16)
            return lax.dot_general(value, slots, (((0,), (0,)), ((), ())), preferred_element_type=F32)

        table = one(score[:, 0:1], pa_ref[...]) + one(score[:, 1:2], pb_ref[...])
        names = iota((experts, half), 0)
        row = iota((topk, half), 0)
        ids = ids_ref[...]
        result = jnp.zeros((topk, half), F32)
        for k in range(topk):
            hit = names == ids[k : k + 1, :]
            picked = jnp.sum(jnp.where(hit, table, 0.0), axis=0, keepdims=True)
            result = result + jnp.where(row == k, picked, 0.0)
        grad_ref[...] = result.astype(BF16)

    tokens_of(w_ref, back_ref, keep_ref, 0)


def combine_keep(at, ids_t, pa, pb, w, back):
    topk, tokens = ids_t.shape
    half = tokens // 2
    rows, lanes = back.shape
    tile = (lanes - 128) // 6
    whole = pl.BlockSpec(memory_space=pltpu.VMEM)
    return pl.pallas_call(
        keep_kernel,
        grid_spec=pltpu.PrefetchScalarGridSpec(
            num_scalar_prefetch=1,
            grid=(4,),
            in_specs=[
                pl.BlockSpec((topk, half), lambda j, at: (0, at[0])),
                pl.BlockSpec((rows, half), lambda j, at: (0, 0)),
                pl.BlockSpec((rows, half), lambda j, at: (0, 0)),
                whole,
                whole,
            ],
            out_specs=[
                pl.BlockSpec((half, tile), lambda j, at: (0, 4 * at[0] + j)),
                pl.BlockSpec((topk, half), lambda j, at: (0, 0)),
            ],
        ),
        out_shape=[
            jax.ShapeDtypeStruct((half, 8 * tile), BF16),
            jax.ShapeDtypeStruct((topk, half), BF16),
        ],
        compiler_params=params(),
        cost_estimate=pl.CostEstimate(flops=10**9, bytes_accessed=7 * 10**6, transcendentals=0),
        name="combine_keep",
    )(at, ids_t, pa, pb, w, back)


def join_kernel(at_ref, base_ref, came_ref, out_ref):
    out_ref[...] = came_ref[...]


def join(at, base, came):
    half, part = came.shape
    return pl.pallas_call(
        join_kernel,
        grid_spec=pltpu.PrefetchScalarGridSpec(
            num_scalar_prefetch=1,
            grid=(2,),
            in_specs=[
                pl.BlockSpec(memory_space=pl.ANY),
                pl.BlockSpec((half, part // 2), lambda j, at: (0, j)),
            ],
            out_specs=pl.BlockSpec((half, part // 2), lambda j, at: (0, 2 * (1 - at[0]) + j)),
        ),
        out_shape=jax.ShapeDtypeStruct(base.shape, BF16),
        input_output_aliases={1: 0},
        compiler_params=params(),
        cost_estimate=pl.CostEstimate(flops=0, bytes_accessed=2 * 10**6, transcendentals=0),
        name="join",
    )(at, base, came)


def exchange(value, groups):
    rows, lanes = value.shape
    value = lax.all_to_all(
        value.reshape(groups, MAIN, lanes), "expert", split_axis=0, concat_axis=0, tiled=True
    )
    return value.reshape(rows, lanes)


def on_device(out_grad, route_ids, route_weights, gate_pre, up_pre, w_gate, w_up, w_down):
    groups = lax.axis_size("expert")
    seq_at = lax.axis_index("seq")
    at = seq_at.astype(jnp.int32).reshape(1)
    part = out_grad.shape[1] // 2
    w_gate, w_up, w_down = w_gate[0], w_up[0], w_down[0]
    other = swap(lax.dynamic_slice_in_dim(out_grad, (1 - seq_at) * part, part, 1))
    ids_t = route_ids.T
    pa, pb, w = routes(at, ids_t, route_weights.T, groups)
    sent = dispatch(at, pa, pb, out_grad, other)
    w_gate, w_up, w_down, sent = lax.optimization_barrier((w_gate, w_up, w_down, sent))
    down_other, gate_other, up_other = swap(w_down), swap(w_gate), swap(w_up)
    received = exchange(sent, groups)
    received, down_other, gate_other, up_other = lax.optimization_barrier(
        (received, down_other, gate_other, up_other)
    )
    grad_other, rest = hidden(at, received, down_other)
    grad_other = swap(grad_other)
    grad_mine = hidden(at, received, w_down, rest)
    mine = diffs(grad_mine, grad_other, gate_pre[0], up_pre[0])
    theirs = swap(mine)
    early = early_inputs(at, mine, w_gate, w_up)
    slots = inputs(at, mine, theirs, early, w_gate, w_up, gate_other, up_other)
    back = exchange(slots, groups)
    came = swap(combine_send(w, back))
    keep, weight_grad = combine_keep(at, ids_t, pa, pb, w, back)
    return join(at, keep, came), weight_grad.T


def solution(mesh):
    in_specs = (
        P(("expert", "seq"), None),
        P("expert", None),
        P("expert", None),
        P("expert", None, "seq"),
        P("expert", None, "seq"),
        P("expert", None, "seq"),
        P("expert", None, "seq"),
        P("expert", "seq", None),
    )
    out_specs = (P(("expert", "seq"), None), P(("expert", "seq"), None))
    return jax.shard_map(
        on_device, mesh=mesh, in_specs=in_specs, out_specs=out_specs, check_vma=False
    )
```
